512 devices in a mesh: dp: 8 (over y, core), shard: 64 (over z, x).
Axes of the slice: x: 4, y: 4, z: 16, core: 2. Of those that a mesh axis runs over, the one named last changes fastest.
Arguments:
- candidates: bfloat16 [114688, 1024], P(('dp', 'shard')), may hold values from -6 to 6
- cotangent: bfloat16 [114688, 1024], P(('dp', 'shard')), may hold values from -6 to 6
- history: bfloat16 [65536, 1024], P(('dp', 'shard')), may hold values from -6 to 6
- request_blocks: int32 [1024, 8], P(('dp', 'shard')), may hold values from 0 to 7, each once within a row
- request_length: int32 [1024], P(('dp', 'shard')), may hold values from 1 to 8
- candidate_request: int32 [114688], P(('dp', 'shard')), may hold values from 0 to 1
- in_weight: bfloat16 [1024, 1024], replicated, may hold values from -0.1875 to 0.1875
- out_weight: bfloat16 [512, 1024], replicated, may hold values from -0.25 to 0.25
Outputs:
- layer_out: bfloat16 [114688, 1024], P(('dp', 'shard'))
- grad_out_weight: float32 [512, 1024], P('shard')
- grad_history: bfloat16 [65536, 1024], P(('dp', 'shard'))
The draws below stay inside these ranges and needn't reach their ends.
Inputs may be any that keep to these rules, and one draw needn't show every extreme that they name: `request_blocks`: each row holds every block number of the window once.
All inputs are finite; a program needn't handle non-finite values.
Results may differ from the reference program's by a relative error of at most 0.0084.
Values may be sent and summed in bfloat16 or wider, within the bound.
No kernel may reach another device: no remote copies, remote signals or barrier semaphores. Data moves between devices by JAX's collectives and lax.ppermute only.
A program may use at most 64 MiB of HBM per device.

```python
import math
import jax
import jax.numpy as jnp
from jax import lax

D = 1024
HEADS = 4
BLK = 128
SPAN = 8
HB = 1
CAND_DEV = 224
REQ_DEV = 2
HD = 512
WBLK = 8
CANDIDATES = 114688
REQUESTS = 1024
HROWS = 65536
N_DP = 8
N_SHARD = 64


def set_ends(values, key, smallest, high):
    extent = values.shape
    spot = [jax.random.randint(jax.random.fold_in(key, axis), (), 0, extent[axis]) for axis in range(len(extent))]
    values = values.at[tuple(spot)].set(smallest)
    longest = extent.index(max(extent))
    spot[longest] = (spot[longest] + 1) % extent[longest]
    return values.at[tuple(spot)].set(high)


def level_of(own_key, shape, cuts, low, largest):
    def one(axis_at, parts):
        draws = jax.random.uniform(jax.random.fold_in(jax.random.fold_in(own_key, 6), axis_at), (parts,), jnp.float32, low / len(cuts), largest / len(cuts))
        return jnp.repeat(jnp.exp(draws), shape[axis_at] // parts).reshape((-1,) + (1,) * (len(shape) - axis_at - 1))

    gain = one(*cuts[0])
    for cut in cuts[1:]:
        gain = gain * one(*cut)
    return gain


def centred(stream_key, dims, spread, reach, pieces=(), kind=jnp.bfloat16):
    values = jax.random.normal(stream_key, dims, jnp.float32) * spread
    if len(pieces) > 0:
        values = level_of(stream_key, dims, pieces, -0.22, 0.18) * values
    return jnp.clip(values, min=-reach, max=reach).astype(kind)


def setup_inputs(seed: int = 0) -> dict:
    key_of = jax.random.split(jax.random.key(seed), 9)
    return {
        "candidates": centred(key_of[0], (CANDIDATES, D), 1.0, 6.0, ((0, 512),)),
        "cotangent": centred(key_of[1], (CANDIDATES, D), 1.0, 6.0, ((0, 512),)),
        "history": centred(key_of[2], (HROWS, 2 * HD), 1.0, 6.0, ((0, 512),)),
        "request_blocks": jax.vmap(lambda own: jax.random.permutation(own, WBLK))(jax.random.split(key_of[3], REQUESTS)).reshape((REQUESTS, WBLK)).astype(jnp.int32),
        "request_length": set_ends(jax.random.randint(key_of[4], (REQUESTS,), 1, WBLK + 1), jax.random.fold_in(key_of[4], 1), 1, WBLK).astype(jnp.int32),
        "candidate_request": set_ends(jax.random.randint(key_of[5], (CANDIDATES,), 0, REQ_DEV), jax.random.fold_in(key_of[5], 1), 0, REQ_DEV - 1).astype(jnp.int32),
        "in_weight": centred(key_of[6], (D, 2 * HD), D ** -0.5, 0.1875),
        "out_weight": centred(key_of[7], (HD, D), HD ** -0.5, 0.25),
    }


def layer_norm(values):
    average = lax.optimization_barrier(jnp.mean(values, axis=-1, keepdims=True))
    centered = values - average
    inv_scale = lax.rsqrt(lax.optimization_barrier(jnp.mean(centered * centered, axis=-1, keepdims=True)) + 1e-05)
    return (centered * inv_scale, inv_scale)

def usage_mask(request_blocks, request_length, candidate_request):
    count_blocks = request_blocks.shape[1]
    positions = jnp.arange(count_blocks, dtype=jnp.int32)
    matches = request_blocks[:, :, None] == positions[None, None, :]
    in_length = positions[None, :] < request_length[:, None]
    used_blocks = lax.optimization_barrier(jnp.sum(jnp.where(matches & in_length[:, :, None], jnp.float32(1.0), jnp.float32(0.0)), axis=1))
    request_ids = jnp.arange(request_blocks.shape[0], dtype=jnp.int32)
    membership = jnp.where(candidate_request[:, None] == request_ids[None, :], jnp.float32(1.0), jnp.float32(0.0))
    return jnp.dot(membership, used_blocks, precision=lax.Precision.HIGHEST)

def score_block(cand_rows, cot_rows, window, usage, in_weight, out_weight):
    cand_count = cand_rows.shape[0]
    inner_width = out_weight.shape[0]
    head_size = inner_width // HEADS
    row_count = window.shape[0]
    grad_scale = 1.0 / math.sqrt(head_size)
    normed_in, _ = layer_norm(cand_rows.astype(jnp.float32))
    projected = jnp.dot(normed_in.astype(jnp.bfloat16), in_weight, preferred_element_type=jnp.float32)
    queries = projected[:, :inner_width].astype(jnp.bfloat16).reshape(cand_count, HEADS, head_size)
    gating = jax.nn.silu(projected[:, inner_width:])
    key_rows = window[:, :inner_width].reshape(row_count, HEADS, head_size)
    value_rows = window[:, inner_width:].reshape(row_count, HEADS, head_size)
    usage_rows = jnp.repeat(usage, BLK, axis=1)
    scores = jnp.einsum('chd,rhd->hcr', queries.astype(jnp.float32), key_rows.astype(jnp.float32)) * grad_scale
    weights = (jax.nn.silu(scores) * usage_rows[None]).astype(jnp.bfloat16)
    attended = jnp.einsum('hcr,rhd->chd', weights.astype(jnp.float32), value_rows.astype(jnp.float32)).reshape(cand_count, inner_width)
    normed, inv_scale = layer_norm(attended)
    gated_out = (normed * gating).astype(jnp.bfloat16)
    result = (cand_rows.astype(jnp.float32) + jnp.dot(gated_out, out_weight, preferred_element_type=jnp.float32)).astype(jnp.bfloat16)
    zed_grad = lax.dot_general(cot_rows, out_weight, (((1,), (1,)), ((), ())), preferred_element_type=jnp.float32)
    pre_grad = zed_grad * gating
    attn_grad = inv_scale * (pre_grad - lax.optimization_barrier(jnp.mean(pre_grad, axis=-1, keepdims=True)) - normed * lax.optimization_barrier(jnp.mean(pre_grad * normed, axis=-1, keepdims=True)))
    attn_grad = attn_grad.astype(jnp.bfloat16).reshape(cand_count, HEADS, head_size)
    value_grad = jnp.einsum('hcr,chd->rhd', weights.astype(jnp.float32), attn_grad.astype(jnp.float32))
    weight_grad = jnp.einsum('chd,rhd->hcr', attn_grad.astype(jnp.float32), value_rows.astype(jnp.float32))
    sigmoid = jax.nn.sigmoid(scores)
    score_grad = (weight_grad * usage_rows[None] * (sigmoid * (1.0 + scores * (1.0 - sigmoid))) * grad_scale).astype(jnp.bfloat16)
    key_grad = jnp.einsum('hcr,chd->rhd', score_grad.astype(jnp.float32), queries.astype(jnp.float32))
    contribution = jnp.concatenate([key_grad.reshape(row_count, inner_width), value_grad.reshape(row_count, inner_width)], axis=1).astype(jnp.bfloat16)
    return (result, gated_out, contribution)

def reference(candidates, cotangent, history, request_blocks, request_length, candidate_request, in_weight, out_weight):
    group_count = N_DP * N_SHARD
    owned_rows = HB * BLK
    wide = 2 * HD
    hist_groups = history.reshape(group_count, owned_rows, wide)
    offsets = jnp.arange(SPAN, dtype=jnp.int32)
    scan_inputs = (candidates.reshape(group_count, CAND_DEV, D), cotangent.reshape(group_count, CAND_DEV, D), request_blocks.reshape(group_count, REQ_DEV, WBLK), request_length.reshape(group_count, REQ_DEV), candidate_request.reshape(group_count, CAND_DEV), jnp.arange(group_count, dtype=jnp.int32))

    def scan_step(running, inputs):
        cand_rows, cot_rows, lists, lengths, owners_of, group_id = inputs
        dp_part = group_id // N_SHARD
        position = group_id % N_SHARD
        owner_ids = (dp_part * N_SHARD + (position + offsets) % N_SHARD).astype(jnp.int32)
        window = jnp.take(hist_groups, owner_ids, axis=0).reshape(SPAN * owned_rows, wide)
        usage = usage_mask(lists, lengths, owners_of)
        result, gated_out, contribution = score_block(cand_rows, cot_rows, window, usage, in_weight, out_weight)
        running = running.at[owner_ids].add(contribution.astype(jnp.float32).reshape(SPAN, owned_rows, wide))
        return (running, (result, gated_out))
    start_grad = jnp.zeros((group_count, owned_rows, wide), jnp.float32)
    grad_sum, (results, gated_all) = lax.scan(scan_step, start_grad, scan_inputs)
    layer_out = results.reshape(CANDIDATES, D)
    gated_flat = gated_all.reshape(CANDIDATES, HD)
    grad_out_weight = lax.dot_general(gated_flat, cotangent, (((0,), (0,)), ((), ())), preferred_element_type=jnp.float32) * (1.0 / math.sqrt(CANDIDATES))
    grad_history = grad_sum.reshape(HROWS, wide).astype(jnp.bfloat16)
    return (layer_out, grad_out_weight, grad_history)
```

```python
import math

import jax
import jax.numpy as jnp
from jax import lax
from jax.sharding import Mesh, PartitionSpec as P

HEADS = 4
BLK = 128
SPAN = 8


SHARD = ("z", "x")


def shifted(block, axis, distance):
    devices = range(lax.axis_size(axis))
    route = [((i - distance) % len(devices), i) for i in devices]
    return lax.ppermute(block, axis, route)


def exchanged(chunks, axis):
    return lax.all_to_all(chunks, axis, 0, 0, tiled=True)


def summed_over(chunks, axis, kind):
    arrived = exchanged(chunks.astype(kind), axis)
    return jnp.sum(arrived.astype(jnp.float32), axis=0)


def spread_over(block, axis):
    size = lax.axis_size(axis)
    return exchanged(jnp.broadcast_to(block[None], (size,) + block.shape), axis)


def summed_rows(full_grad):
    ys, cores, zs, xs = (lax.axis_size(name) for name in ("y", "core", "z", "x"))
    rows, cols = full_grad.shape
    piece = (rows // (zs * xs), cols // (ys * cores))
    chunks = full_grad.reshape(zs, xs, piece[0], cores, ys, piece[1])
    chunks = chunks.transpose(3, 4, 1, 0, 2, 5)
    part = summed_over(chunks, "core", jnp.bfloat16)
    part = summed_over(part, "y", jnp.bfloat16)
    part = summed_over(part, "x", jnp.float32)
    part = summed_over(part, "z", jnp.float32)
    wide = spread_over(spread_over(part, "y"), "core")
    return wide.transpose(2, 0, 1, 3).reshape(piece[0], cols)


def layer_norm(values):
    average = jnp.mean(values, axis=-1, keepdims=True)
    centered = values - average
    inv_scale = lax.rsqrt(jnp.mean(centered * centered, axis=-1, keepdims=True) + 1e-05)
    return (centered * inv_scale, inv_scale)


def usage_mask(request_blocks, request_length, candidate_request):
    count_blocks = request_blocks.shape[1]
    positions = jnp.arange(count_blocks, dtype=jnp.int32)
    matches = request_blocks[:, :, None] == positions[None, None, :]
    in_length = positions[None, :] < request_length[:, None]
    used_blocks = jnp.sum(
        jnp.where(matches & in_length[:, :, None], jnp.float32(1.0), jnp.float32(0.0)), axis=1
    )
    request_ids = jnp.arange(request_blocks.shape[0], dtype=jnp.int32)
    membership = jnp.where(
        candidate_request[:, None] == request_ids[None, :], jnp.float32(1.0), jnp.float32(0.0)
    )
    return jnp.dot(membership, used_blocks, precision=lax.Precision.HIGHEST)


def score_block(cand_rows, cot_rows, window, usage, in_weight, out_weight):
    cand_count = cand_rows.shape[0]
    inner_width = out_weight.shape[0]
    head_size = inner_width // HEADS
    row_count = window.shape[0]
    grad_scale = 1.0 / math.sqrt(head_size)
    normed_in, _ = layer_norm(cand_rows.astype(jnp.float32))
    projected = jnp.dot(
        normed_in.astype(jnp.bfloat16), in_weight, preferred_element_type=jnp.float32
    )
    queries = projected[:, :inner_width].astype(jnp.bfloat16).reshape(cand_count, HEADS, head_size)
    gating = jax.nn.silu(projected[:, inner_width:])
    key_rows = window[:, :inner_width].reshape(row_count, HEADS, head_size)
    value_rows = window[:, inner_width:].reshape(row_count, HEADS, head_size)
    usage_rows = jnp.repeat(usage, BLK, axis=1)
    scores = (
        jnp.einsum("chd,rhd->hcr", queries, key_rows, preferred_element_type=jnp.float32)
        * grad_scale
    )
    weights = (jax.nn.silu(scores) * usage_rows[None]).astype(jnp.bfloat16)
    attended = jnp.einsum(
        "hcr,rhd->chd", weights, value_rows, preferred_element_type=jnp.float32
    ).reshape(cand_count, inner_width)
    normed, inv_scale = layer_norm(attended)
    gated_out = (normed * gating).astype(jnp.bfloat16)
    result = (
        cand_rows.astype(jnp.float32)
        + jnp.dot(gated_out, out_weight, preferred_element_type=jnp.float32)
    ).astype(jnp.bfloat16)
    zed_grad = lax.dot_general(
        cot_rows, out_weight, (((1,), (1,)), ((), ())), preferred_element_type=jnp.float32
    )
    pre_grad = zed_grad * gating
    attn_grad = inv_scale * (
        pre_grad
        - jnp.mean(pre_grad, axis=-1, keepdims=True)
        - normed * jnp.mean(pre_grad * normed, axis=-1, keepdims=True)
    )
    attn_grad = attn_grad.astype(jnp.bfloat16).reshape(cand_count, HEADS, head_size)
    value_grad = jnp.einsum("hcr,chd->rhd", weights, attn_grad, preferred_element_type=jnp.float32)
    weight_grad = jnp.einsum(
        "chd,rhd->hcr", attn_grad, value_rows, preferred_element_type=jnp.float32
    )
    sigmoid = jax.nn.sigmoid(scores)
    score_grad = (
        weight_grad * usage_rows[None] * (sigmoid * (1.0 + scores * (1.0 - sigmoid))) * grad_scale
    ).astype(jnp.bfloat16)
    key_grad = jnp.einsum("hcr,chd->rhd", score_grad, queries, preferred_element_type=jnp.float32)
    contribution = jnp.concatenate(
        [key_grad.reshape(row_count, inner_width), value_grad.reshape(row_count, inner_width)],
        axis=1,
    ).astype(jnp.bfloat16)
    return (result, gated_out, contribution)


def on_device(
    candidates,
    cotangent,
    history,
    request_blocks,
    request_length,
    candidate_request,
    in_weight,
    out_weight,
):
    owned_rows = history.shape[0]
    pieces = [history]
    for offset in range(1, SPAN):
        pieces.append(shifted(history, SHARD, -offset))
    window = jnp.concatenate(pieces, axis=0)
    usage = usage_mask(request_blocks, request_length, candidate_request)
    layer_out, gated_out, contribution = score_block(
        candidates, cotangent, window, usage, in_weight, out_weight
    )
    total_cands = candidates.shape[0] * lax.axis_size(("y", "core", "z", "x"))
    grad_scale = 1.0 / math.sqrt(total_cands)
    full_grad = (
        lax.dot_general(
            gated_out, cotangent, (((0,), (0,)), ((), ())), preferred_element_type=jnp.float32
        )
        * grad_scale
    )
    grad_rows = summed_rows(full_grad)
    accumulated = contribution[:owned_rows].astype(jnp.float32)
    for offset in range(1, SPAN):
        returned = shifted(
            contribution[offset * owned_rows : (offset + 1) * owned_rows], SHARD, offset
        )
        accumulated = accumulated + returned.astype(jnp.float32)
    return (layer_out, grad_rows, accumulated.astype(jnp.bfloat16))


def solution(mesh):
    inner = Mesh(mesh.devices.reshape(4, 2, 16, 4), ("y", "core", "z", "x"))
    rows = P(("y", "core", "z", "x"))
    return jax.shard_map(
        on_device,
        mesh=inner,
        in_specs=(rows, rows, rows, rows, rows, rows, P(), P()),
        out_specs=(rows, P(SHARD), rows),
        check_vma=False,
    )
```

```python
import math

import jax
import jax.numpy as jnp
from jax import lax
from jax.experimental import pallas as pl
from jax.experimental.pallas import tpu as pltpu
from jax.sharding import Mesh, PartitionSpec as P

HEADS = 4
SPAN = 8
BF16 = jnp.bfloat16
F32 = jnp.float32
ALL = ("y", "core", "zh", "zl", "x")
DEPTH = ("zh", "zl")
NT = (((1,), (1,)), ((), ()))
TN = (((0,), (0,)), ((), ()))


def on_core(kernel, outs, *operands):
    return pl.pallas_call(
        kernel,
        out_shape=outs,
        in_specs=[pl.BlockSpec(memory_space=pltpu.VMEM)] * len(operands),
        out_specs=jax.tree.map(lambda _: pl.BlockSpec(memory_space=pltpu.VMEM), outs),
        compiler_params=pltpu.CompilerParams(vmem_limit_bytes=40 * 1024 * 1024),
    )(*operands)


def shaped(shape, kind):
    return jax.ShapeDtypeStruct(shape, kind)


def sigmoid(values):
    return 0.5 + 0.5 * jnp.tanh(0.5 * values)


def served(ring, group):
    return {0: range(group, HEADS), 1: range(0, HEADS), 2: range(0, group)}[ring]


def prepare_kernel(cand_ref, cot_ref, in_ref, out_ref, bundle_ref):
    rows = cand_ref[...].astype(F32)
    centered = rows - jnp.mean(rows, axis=-1, keepdims=True)
    inv_scale = lax.rsqrt(jnp.mean(centered * centered, axis=-1, keepdims=True) + 1e-05)
    normed = (centered * inv_scale).astype(BF16)
    projected = jnp.dot(normed, in_ref[...], preferred_element_type=F32).T
    zed_grad = lax.dot_general(out_ref[...], cot_ref[...], NT, preferred_element_type=F32)
    inner = out_ref.shape[0]
    size = inner // HEADS
    for head in range(HEADS):
        part = slice(head * size, (head + 1) * size)
        gate_in = projected[inner + head * size : inner + (head + 1) * size]
        gating = gate_in * sigmoid(gate_in)
        bundle_ref[head, 0:size] = projected[part].astype(BF16)
        bundle_ref[head, size : 2 * size] = gating.astype(BF16)
        bundle_ref[head, 2 * size : 3 * size] = (zed_grad[part] * gating).astype(BF16)


def attend(ring, blocks_ref, bundle_ref, usage_ref, weight_ref, slope_ref, group):
    size = bundle_ref.shape[1] // 3
    span = served(ring, group)
    if len(span) == 0:
        return None
    first, count, tall = span[0], len(span), blocks_ref.shape[1]
    keys = blocks_ref[first : first + count, :, 0:size].reshape(count * tall, size)
    values = blocks_ref[first : first + count, :, size:].reshape(count * tall, size)
    scale = 1.0 / math.sqrt(size)
    scores = jnp.dot(keys, bundle_ref[group, 0:size], preferred_element_type=F32) * scale
    part = sigmoid(scores)
    weights = scores * part
    slopes = (part + weights * (1.0 - part)) * scale
    usage = usage_ref[group].astype(F32)
    kept = []
    for place, block in enumerate(span):
        position = HEADS * ring + block - group
        mask = usage[position : position + 1]
        lines = slice(place * tall, (place + 1) * tall)
        kept.append((weights[lines] * mask).astype(BF16))
        weight_ref[group, block] = kept[-1]
        slope_ref[group, block] = (slopes[lines] * mask).astype(BF16)
    return lax.dot_general(
        values, jnp.concatenate(kept, axis=0), TN, preferred_element_type=F32
    )


def early_kernel(*refs):
    ring0, ring1, bundle, usage, w0, s0, w1, s1, attended_ref = refs
    for group in range(HEADS):
        attended_ref[group] = attend(0, ring0, bundle, usage, w0, s0, group) + attend(
            1, ring1, bundle, usage, w1, s1, group
        )


def late_kernel(ring2, bundle, usage, before, w2, s2, attended_ref, stats_ref):
    size = bundle.shape[1] // 3
    for group in range(HEADS):
        attended = before[group]
        more = attend(2, ring2, bundle, usage, w2, s2, group)
        if more is not None:
            attended = attended + more
        attended_ref[group] = attended
        dy = bundle[group, 2 * size :].astype(F32)
        mean = jnp.mean(attended, axis=0, keepdims=True)
        centered = attended - mean
        stats_ref[4 * group : 4 * group + 1] = mean
        stats_ref[4 * group + 1 : 4 * group + 2] = jnp.sum(centered * centered, axis=0, keepdims=True)
        stats_ref[4 * group + 2 : 4 * group + 3] = jnp.sum(dy, axis=0, keepdims=True)
        stats_ref[4 * group + 3 : 4 * group + 4] = jnp.sum(dy * centered, axis=0, keepdims=True)


def norm_kernel(total_cands, attended, bundle, stats, cots, gated_ref, grad_ref, out_grad_ref):
    size = bundle.shape[1] // 3
    width = HEADS * size
    total = None
    for group in range(HEADS):
        head_stats = [stats[head, 4 * group : 4 * group + 4] for head in range(HEADS)]
        mean = sum(one[0:1] for one in head_stats) * (1.0 / HEADS)
        apart = [one[0:1] - mean for one in head_stats]
        spread = sum(one[1:2] + size * off * off for one, off in zip(head_stats, apart))
        inv_scale = lax.rsqrt(spread * (1.0 / width) + 1e-05)
        mean_dy = sum(one[2:3] for one in head_stats) * (1.0 / width)
        mixed = sum(one[3:4] + off * one[2:3] for one, off in zip(head_stats, apart))
        mean_mixed = mixed * inv_scale * (1.0 / width)
        normed = (attended[group] - mean) * inv_scale
        gated = (normed * bundle[group, size : 2 * size].astype(F32)).astype(BF16)
        dy = bundle[group, 2 * size :].astype(F32)
        gated_ref[group] = gated
        grad_ref[group] = (inv_scale * (dy - mean_dy - normed * mean_mixed)).astype(BF16)
        part = jnp.dot(gated, cots[group], preferred_element_type=F32)
        total = part if total is None else total + part
    total = (total * (1.0 / math.sqrt(total_cands))).astype(BF16)
    half = total.shape[1] // 2
    out_grad_ref[0] = total[:, :half]
    out_grad_ref[1] = total[:, half:]


def back_kernel(ring, blocks_ref, bundle, grads, weights, slopes, sum_ref):
    size = bundle.shape[1] // 3
    count, tall = sum_ref.shape[0], blocks_ref.shape[1]
    keys = [None] * count
    values = [None] * count
    for group in range(HEADS):
        span = served(ring, group)
        if len(span) == 0:
            continue
        first, many = span[0], len(span)
        grad = grads[group]
        value_rows = blocks_ref[first : first + many, :, size:].reshape(many * tall, size)
        weight_grad = jnp.dot(value_rows, grad, preferred_element_type=F32)
        for place, block in enumerate(span):
            lines = slice(place * tall, (place + 1) * tall)
            score_grad = (weight_grad[lines] * slopes[group, block].astype(F32)).astype(BF16)
            key = lax.dot_general(score_grad, bundle[group, 0:size], NT, preferred_element_type=F32)
            value = lax.dot_general(weights[group, block], grad, NT, preferred_element_type=F32)
            keys[block] = key if keys[block] is None else keys[block] + key
            values[block] = value if values[block] is None else values[block] + value
    for block in range(count):
        sum_ref[block, :, 0:size] = keys[block].astype(sum_ref.dtype)
        sum_ref[block, :, size:] = values[block].astype(sum_ref.dtype)


def out_kernel(cand_ref, gated_ref, out_ref, result_ref):
    heads, size, count = gated_ref.shape
    gated = gated_ref[...].reshape(heads * size, count)
    product = lax.dot_general(gated, out_ref[...], TN, preferred_element_type=F32)
    result_ref[...] = (cand_ref[...].astype(F32) + product).astype(BF16)


def moved(block, distance):
    size = lax.axis_size(DEPTH)
    return lax.ppermute(block, DEPTH, [((i + distance) % size, i) for i in range(size)])


def exchanged(chunks, axis):
    return lax.all_to_all(chunks, axis, 0, 0, tiled=True)


def spread_over(block, axis):
    size = lax.axis_size(axis)
    return exchanged(jnp.broadcast_to(block[None], (size,) + block.shape), axis)


def summed(parts):
    return jnp.sum(parts.astype(F32), axis=0)


def used_blocks(request_blocks, request_length, candidate_request):
    positions = jnp.arange(request_blocks.shape[1], dtype=jnp.int32)
    matches = request_blocks[:, :, None] == positions[None, None, :]
    in_length = positions[None, :] < request_length[:, None]
    used = jnp.sum(jnp.where(matches & in_length[:, :, None], 1.0, 0.0), axis=1)
    ids = jnp.arange(request_blocks.shape[0], dtype=jnp.int32)
    member = jnp.where(candidate_request[None, :] == ids[:, None], 1.0, 0.0)
    return jnp.sum(used[:, :, None] * member[:, None, :], axis=0)


def summed_rows(out_grad):
    rows, half = out_grad.shape[1:]
    zh, zl, xs = (lax.axis_size(name) for name in ("zh", "zl", "x"))
    own = rows // (zl * xs)
    part = summed(exchanged(out_grad, "core")).astype(BF16)
    part = summed(exchanged(part.reshape(zl, xs, own, half), "zl")).astype(BF16)
    part = exchanged(jnp.broadcast_to(part[None], (zh, xs, own, half)).reshape(zh * xs, own, half), ("zh", "x"))
    part = lax.dynamic_index_in_dim(part.reshape(zh, xs, own, half), lax.axis_index("zh"), axis=1, keepdims=False)
    part = summed(spread_over(summed(part), "y"))
    return spread_over(part, "core").transpose(1, 0, 2).reshape(own, 2 * half)


def on_device(
    candidates,
    cotangent,
    history,
    request_blocks,
    request_length,
    candidate_request,
    in_weight,
    out_weight,
):
    tall, wide = history.shape
    inner = wide // 2
    size = inner // HEADS
    count = candidates.shape[0]
    total_cands = count * lax.axis_size(ALL)

    usage = used_blocks(request_blocks, request_length, candidate_request)
    usage = lax.all_gather(usage.astype(BF16), "x")
    cots = lax.all_gather(cotangent, "x")

    by_head = history.reshape(tall, 2, HEADS, size).transpose(2, 0, 1, 3).reshape(HEADS, tall, 2 * size)
    ring0 = exchanged(by_head, "x")
    ring1 = moved(ring0, 1)
    ring2 = moved(ring1[: HEADS - 1], 1)

    bundle = on_core(
        prepare_kernel,
        shaped((HEADS, 3 * size, count), BF16),
        candidates,
        cotangent,
        in_weight,
        out_weight,
    )
    bundle = exchanged(bundle, "x")

    pairs = shaped((HEADS, HEADS, tall, count), BF16)
    late_pairs = shaped((HEADS, HEADS - 1, tall, count), BF16)
    attended_shape = shaped((HEADS, size, count), F32)
    w0, s0, w1, s1, before = on_core(
        early_kernel, (pairs, pairs, pairs, pairs, attended_shape), ring0, ring1, bundle, usage
    )
    w2, s2, attended, stats = on_core(
        late_kernel,
        (late_pairs, late_pairs, attended_shape, shaped((4 * HEADS, count), F32)),
        ring2,
        bundle,
        usage,
        before,
    )
    stats = spread_over(stats, "x")

    head_shape = shaped((HEADS, size, count), BF16)
    gated, grads, out_grad = on_core(
        lambda *refs: norm_kernel(total_cands, *refs),
        (head_shape, head_shape, shaped((2, size, out_weight.shape[1] // 2), BF16)),
        attended,
        bundle,
        stats,
        cots,
    )
    grad_rows = summed_rows(out_grad)

    def back(ring, blocks, weights, slopes, kind):
        return on_core(
            lambda *refs: back_kernel(ring, *refs),
            shaped((blocks.shape[0], tall, 2 * size), kind),
            blocks,
            bundle,
            grads,
            weights,
            slopes,
        )

    back2 = moved(back(2, ring2, w2, s2, BF16), -1)
    back1 = back(1, ring1, w1, s1, F32)
    back0 = back(0, ring0, w0, s0, F32)
    back1 = back1 + jnp.pad(back2, ((0, 1), (0, 0), (0, 0))).astype(F32)
    back1 = moved(back1.astype(BF16), -1)
    own = exchanged((back0 + back1.astype(F32)).astype(BF16), "x")
    grad_history = own.reshape(HEADS, tall, 2, size).transpose(1, 2, 0, 3).reshape(tall, wide)

    gated = exchanged(gated, "x")
    layer_out = on_core(
        out_kernel, shaped(candidates.shape, BF16), candidates, gated, out_weight
    )
    return (layer_out, grad_rows, grad_history)


def solution(mesh):
    inner = Mesh(mesh.devices.reshape(4, 2, 4, 4, 4), ALL)
    rows = P(ALL)
    return jax.shard_map(
        on_device,
        mesh=inner,
        in_specs=(rows, rows, rows, rows, rows, rows, P(), P()),
        out_specs=(rows, P(("zh", "zl", "x")), rows),
        check_vma=False,
    )
```

```python
import math

import jax
import jax.numpy as jnp
from jax import lax
from jax.experimental import pallas as pl
from jax.experimental.pallas import tpu as pltpu
from jax.sharding import Mesh, PartitionSpec as P

HEADS = 4
SPAN = 8
BF16 = jnp.bfloat16
F32 = jnp.float32
ALL = ("y", "core", "zh", "zl", "x")
DEPTH = ("zh", "zl")
NT = (((1,), (1,)), ((), ()))
TN = (((0,), (0,)), ((), ()))


def on_core(kernel, outs, *operands, scalars=()):
    spaces = [pltpu.SMEM] * len(scalars) + [pltpu.VMEM] * len(operands)
    return pl.pallas_call(
        kernel,
        out_shape=outs,
        in_specs=[pl.BlockSpec(memory_space=space) for space in spaces],
        out_specs=jax.tree.map(lambda _: pl.BlockSpec(memory_space=pltpu.VMEM), outs),
        compiler_params=pltpu.CompilerParams(vmem_limit_bytes=12 * 1024 * 1024),
    )(*scalars, *operands)


def shaped(shape, kind):
    return jax.ShapeDtypeStruct(shape, kind)


def sigmoid(values):
    return 0.5 + 0.5 * jnp.tanh(0.5 * values)


def served(ring, group):
    return {0: range(group, HEADS), 1: range(0, HEADS), 2: range(0, group)}[ring]


def split_kernel(history_ref, chunks_ref):
    heads, _, both = chunks_ref.shape
    size = both // 2
    for head in range(heads):
        chunks_ref[head, :, :size] = history_ref[:, head * size : (head + 1) * size]
        chunks_ref[head, :, size:] = history_ref[:, (heads + head) * size : (heads + head + 1) * size]


def prepare_kernel(cand_ref, cot_ref, in_ref, out_ref, usage_ref, bundle_ref):
    rows = cand_ref[...].astype(F32)
    centered = rows - jnp.mean(rows, axis=-1, keepdims=True)
    inv_scale = lax.rsqrt(jnp.mean(centered * centered, axis=-1, keepdims=True) + 1e-05)
    normed = (centered * inv_scale).astype(BF16)
    projected = jnp.dot(normed, in_ref[...], preferred_element_type=F32).T
    zed_grad = lax.dot_general(out_ref[...], cot_ref[...], NT, preferred_element_type=F32)
    inner, count = out_ref.shape[0], cand_ref.shape[0]
    size = inner // HEADS
    bundle_ref[:, : 3 * size, count:] = jnp.zeros(
        (HEADS, 3 * size, bundle_ref.shape[2] - count), BF16
    )
    for head in range(HEADS):
        part = slice(head * size, (head + 1) * size)
        gate_in = projected[inner + head * size : inner + (head + 1) * size]
        gating = gate_in * sigmoid(gate_in)
        bundle_ref[head, 0:size, :count] = projected[part].astype(BF16)
        bundle_ref[head, size : 2 * size, :count] = gating.astype(BF16)
        bundle_ref[head, 2 * size : 3 * size, :count] = (zed_grad[part] * gating).astype(BF16)
        bundle_ref[head, 3 * size :] = usage_ref[...]


def scored(ring, blocks_ref, bundle_ref, group):
    span = served(ring, group)
    tall, size = blocks_ref.shape[1], blocks_ref.shape[2] // 2
    rows = blocks_ref[span[0] : span[-1] + 1].reshape(len(span) * tall, 2 * size)
    scores = jnp.dot(rows[:, :size], bundle_ref[group, 0:size], preferred_element_type=F32)
    scores = scores * (1.0 / math.sqrt(size))
    usage = bundle_ref[group, 3 * size :].astype(F32)
    parts = []
    for place, block in enumerate(span):
        position = HEADS * ring + block - group
        parts.append((scores[place * tall : (place + 1) * tall], usage[position : position + 1]))
    return rows[:, size:], parts


def attend(ring, blocks_ref, bundle_ref, group):
    values, parts = scored(ring, blocks_ref, bundle_ref, group)
    weights = [(scores * sigmoid(scores) * usage).astype(BF16) for scores, usage in parts]
    return lax.dot_general(
        values, jnp.concatenate(weights, axis=0), TN, preferred_element_type=F32
    )


def early_kernel(ring0, ring1, bundle, attended_ref):
    for group in range(HEADS):
        attended_ref[group] = attend(0, ring0, bundle, group) + attend(1, ring1, bundle, group)


def late_kernel(ring2, bundle, before, attended_ref, stats_ref):
    size = before.shape[1]
    for group in range(HEADS):
        attended = before[group]
        if len(served(2, group)) > 0:
            attended = attended + attend(2, ring2, bundle, group)
        attended_ref[group] = attended
        dy = bundle[group, 2 * size : 3 * size].astype(F32)
        mean = jnp.mean(attended, axis=0, keepdims=True)
        centered = attended - mean
        stats_ref[4 * group : 4 * group + 1] = mean
        stats_ref[4 * group + 1 : 4 * group + 2] = jnp.sum(centered * centered, axis=0, keepdims=True)
        stats_ref[4 * group + 2 : 4 * group + 3] = jnp.sum(dy, axis=0, keepdims=True)
        stats_ref[4 * group + 3 : 4 * group + 4] = jnp.sum(dy * centered, axis=0, keepdims=True)


def norm_kernel(total_cands, attended, bundle, stats, cots_ref, gated_ref, grad_ref, out_grad_ref, cots, arrival):
    copy = pltpu.make_async_copy(cots_ref, cots, arrival)
    copy.start()
    size = attended.shape[1]
    count = cots.shape[1]
    width = HEADS * size
    total = None
    for group in range(HEADS):
        head_stats = [stats[head, 4 * group : 4 * group + 4] for head in range(HEADS)]
        mean = sum(one[0:1] for one in head_stats) * (1.0 / HEADS)
        apart = [one[0:1] - mean for one in head_stats]
        spread = sum(one[1:2] + size * off * off for one, off in zip(head_stats, apart))
        inv_scale = lax.rsqrt(spread * (1.0 / width) + 1e-05)
        mean_dy = sum(one[2:3] for one in head_stats) * (1.0 / width)
        mixed = sum(one[3:4] + off * one[2:3] for one, off in zip(head_stats, apart))
        mean_mixed = mixed * inv_scale * (1.0 / width)
        normed = (attended[group] - mean) * inv_scale
        gated = (normed * bundle[group, size : 2 * size].astype(F32)).astype(BF16)
        dy = bundle[group, 2 * size : 3 * size].astype(F32)
        gated_ref[group] = gated
        grad_ref[group] = (inv_scale * (dy - mean_dy - normed * mean_mixed)).astype(BF16)
    copy.wait()
    for group in range(HEADS):
        part = jnp.dot(gated_ref[group, :, :count], cots[group], preferred_element_type=F32)
        total = part if total is None else total + part
    total = (total * (1.0 / math.sqrt(total_cands))).astype(BF16)
    halves, rows_of, lines, columns = out_grad_ref.shape
    for half in range(halves):
        for row in range(rows_of):
            out_grad_ref[half, row] = total[
                row * lines : (row + 1) * lines, half * columns : (half + 1) * columns
            ]


def back(ring, blocks_ref, bundle, grads, sum_ref):
    tall, size = blocks_ref.shape[1], blocks_ref.shape[2] // 2
    scale = 1.0 / math.sqrt(size)
    keys, values = {}, {}
    for group in range(HEADS):
        span = served(ring, group)
        if len(span) == 0:
            continue
        grad = grads[group]
        value_rows, parts = scored(ring, blocks_ref, bundle, group)
        weight_grad = jnp.dot(value_rows, grad, preferred_element_type=F32)
        for place, block in enumerate(span):
            scores, usage = parts[place]
            part = sigmoid(scores)
            weights = scores * part
            slopes = (part + weights * (1.0 - part)) * (usage * scale)
            lines = weight_grad[place * tall : (place + 1) * tall]
            key = lax.dot_general(
                (lines * slopes).astype(BF16), bundle[group, 0:size], NT, preferred_element_type=F32
            )
            value = lax.dot_general(
                (weights * usage).astype(BF16), grad, NT, preferred_element_type=F32
            )
            keys[block] = keys[block] + key if block in keys else key
            values[block] = values[block] + value if block in values else value
    for block in keys:
        sum_ref[block, :, 0:size] = keys[block].astype(sum_ref.dtype)
        sum_ref[block, :, size:] = values[block].astype(sum_ref.dtype)


def far_back_kernel(ring1, ring2, bundle, grads, back1, back2):
    back(2, ring2, bundle, grads, back2)
    back(1, ring1, bundle, grads, back1)


def near_back_kernel(ring0, bundle, grads, back0):
    back(0, ring0, bundle, grads, back0)


def parcel_kernel(place_ref, gated_ref, back0, back1, back2, *parcel_refs):
    size = gated_ref.shape[1]
    for step, parcel in enumerate(parcel_refs):
        target = lax.rem(place_ref[0] + step, HEADS)
        parcel[0:size] = gated_ref[target]
        total = back0[target] + back1[target].astype(F32)
        last = jnp.minimum(target, back2.shape[0] - 1)
        more = back2[last].astype(F32)
        parcel[size:] = (total + jnp.where(last == target, more, 0.0)).astype(BF16)


def join_kernel(place_ref, cand_ref, out_ref, *refs):
    *parcels, result_ref, grad_ref = refs
    inner, count = out_ref.shape[0], cand_ref.shape[0]
    size = inner // HEADS
    product = None
    for step, parcel in enumerate(parcels):
        head = lax.rem(place_ref[0] + HEADS - step, HEADS)
        rows = pl.ds(pl.multiple_of(head * size, size), size)
        part = lax.dot_general(parcel[0:size, :count], out_ref[rows], TN, preferred_element_type=F32)
        product = part if product is None else product + part
        grad_ref[:, rows] = parcel[size:, 0:size]
        grad_ref[:, pl.ds(pl.multiple_of(inner + head * size, size), size)] = parcel[size:, size:]
    result_ref[...] = (cand_ref[...].astype(F32) + product).astype(BF16)


def moved(block, distance):
    size = lax.axis_size(DEPTH)
    return lax.ppermute(block, DEPTH, [((i + distance) % size, i) for i in range(size)])


def exchanged(chunks, axis):
    return lax.all_to_all(chunks, axis, 0, 0, tiled=True)


def spread_over(block, axis):
    size = lax.axis_size(axis)
    return exchanged(jnp.broadcast_to(block[None], (size,) + block.shape), axis)


def summed(parts):
    return jnp.sum(parts.astype(F32), axis=0)


def used_blocks(request_blocks, request_length, candidate_request):
    positions = jnp.arange(request_blocks.shape[1], dtype=jnp.int32)
    matches = request_blocks[:, :, None] == positions[None, None, :]
    in_length = positions[None, :] < request_length[:, None]
    used = jnp.sum(jnp.where(matches & in_length[:, :, None], 1.0, 0.0), axis=1)
    ids = jnp.arange(request_blocks.shape[0], dtype=jnp.int32)
    member = jnp.where(candidate_request[None, :] == ids[:, None], 1.0, 0.0)
    return jnp.sum(used[:, :, None] * member[:, None, :], axis=0)


def on_device(
    candidates,
    cotangent,
    history,
    request_blocks,
    request_length,
    candidate_request,
    in_weight,
    out_weight,
):
    tall, wide = history.shape
    inner = wide // 2
    size = inner // HEADS
    count = candidates.shape[0]
    lanes = 2 * size
    total_cands = count * lax.axis_size(ALL)
    barrier = lax.optimization_barrier
    place = lax.axis_index("x").reshape(1).astype(jnp.int32)

    cots = lax.all_gather(cotangent, "x")
    ring_shape = shaped((HEADS, tall, 2 * size), BF16)
    ring0 = exchanged(on_core(split_kernel, ring_shape, history), "x")

    owners = jnp.pad(candidate_request, (0, lanes - count), constant_values=-1)
    usage = used_blocks(request_blocks, request_length, owners).astype(BF16)
    usage = jnp.pad(usage, ((0, 16 - usage.shape[0]), (0, 0)))
    ring2 = moved(ring0[: HEADS - 1], 2)
    ring1 = moved(ring0, 1)
    bundle = on_core(
        prepare_kernel,
        shaped((HEADS, 3 * size + 16, lanes), BF16),
        candidates,
        cotangent,
        in_weight,
        out_weight,
        usage,
    )
    bundle = exchanged(bundle, "x")

    attended_shape = shaped((HEADS, size, lanes), F32)
    before = on_core(early_kernel, attended_shape, ring0, ring1, bundle)
    ring2, cots = barrier((ring2, cots))
    attended, stats = on_core(
        late_kernel, (attended_shape, shaped((4 * HEADS, lanes), F32)), ring2, bundle, before
    )
    stats = spread_over(stats, "x")
    head_shape = shaped((HEADS, size, lanes), BF16)
    cores, zh, zl, xs = (lax.axis_size(name) for name in ("core", "zh", "zl", "x"))
    own, half = size // (zl * xs), out_weight.shape[1] // cores
    gated, grads, out_grad = pl.pallas_call(
        lambda *refs: norm_kernel(total_cands, *refs),
        out_shape=(head_shape, head_shape, shaped((cores, zl, size // zl, half), BF16)),
        in_specs=[pl.BlockSpec(memory_space=pltpu.VMEM)] * 3 + [pl.BlockSpec(memory_space=pltpu.HBM)],
        out_specs=(pl.BlockSpec(memory_space=pltpu.VMEM),) * 3,
        scratch_shapes=[pltpu.VMEM(cots.shape, BF16), pltpu.SemaphoreType.DMA],
        compiler_params=pltpu.CompilerParams(vmem_limit_bytes=12 * 1024 * 1024),
    )(attended, bundle, stats, cots)

    back1, back2 = on_core(
        far_back_kernel, (shaped(ring1.shape, BF16), shaped(ring2.shape, BF16)), ring1, ring2, bundle, grads
    )
    out_grad, back1, back2 = barrier((out_grad, back1, back2))
    back2 = moved(back2, -2)
    back1 = moved(back1, -1)
    part = exchanged(out_grad.reshape(cores * zl, size // zl, half), ("core", "zl"))
    part = summed(part).astype(BF16)
    part, grads = barrier((part, grads))
    back0 = on_core(near_back_kernel, shaped(ring0.shape, F32), ring0, bundle, grads)
    part = jnp.broadcast_to(part.reshape(1, xs, own, half), (zh, xs, own, half))
    part = exchanged(part.reshape(zh * xs, own, half), ("zh", "x")).reshape(zh, xs, own, half)
    part = lax.dynamic_index_in_dim(part, lax.axis_index("zh"), axis=1, keepdims=False)
    part, back0, back1, back2 = barrier((summed(part), back0, back1, back2))
    part = spread_over(part, ("y", "core")).reshape(-1, cores, own, half)
    grad_rows = summed(part).transpose(1, 0, 2).reshape(own, cores * half)

    parcels = on_core(
        parcel_kernel, [shaped((2 * size, lanes), BF16)] * HEADS, gated, back0, back1, back2, scalars=(place,)
    )
    arrived = [
        lax.ppermute(parcel, "x", [(i, (i + step) % HEADS) for i in range(HEADS)]) if step else parcel
        for step, parcel in enumerate(parcels)
    ]
    layer_out, grad_history = on_core(
        join_kernel,
        (shaped(candidates.shape, BF16), shaped(history.shape, BF16)),
        candidates,
        out_weight,
        *arrived,
        scalars=(place,),
    )
    return (layer_out, grad_rows, grad_history)


def solution(mesh):
    inner = Mesh(mesh.devices.reshape(4, 2, 4, 4, 4), ALL)
    rows = P(ALL)
    return jax.shard_map(
        on_device,
        mesh=inner,
        in_specs=(rows, rows, rows, rows, rows, rows, P(), P()),
        out_specs=(rows, P(("zh", "zl", "x")), rows),
        check_vma=False,
    )
```

```python
import math

import jax
import jax.numpy as jnp
from jax import lax
from jax.experimental import pallas as pl
from jax.experimental.pallas import tpu as pltpu
from jax.sharding import Mesh, PartitionSpec as P

HEADS = 4
SPAN = 8
BF16 = jnp.bfloat16
F32 = jnp.float32
ALL = ("y", "core", "zh", "zl", "x")
DEPTH = ("zh", "zl")
NT = (((1,), (1,)), ((), ()))
TN = (((0,), (0,)), ((), ()))


def on_core(kernel, outs, *operands, scalars=()):
    spaces = [pltpu.SMEM] * len(scalars) + [pltpu.VMEM] * len(operands)
    return pl.pallas_call(
        kernel,
        out_shape=outs,
        in_specs=[pl.BlockSpec(memory_space=space) for space in spaces],
        out_specs=jax.tree.map(lambda _: pl.BlockSpec(memory_space=pltpu.VMEM), outs),
        compiler_params=pltpu.CompilerParams(vmem_limit_bytes=12 * 1024 * 1024),
    )(*scalars, *operands)


def shaped(shape, kind):
    return jax.ShapeDtypeStruct(shape, kind)


def sigmoid(values):
    return 0.5 + 0.5 * jnp.tanh(0.5 * values)


def served(ring, group):
    return {0: range(group, HEADS), 1: range(0, HEADS), 2: range(0, group)}[ring]


def split_kernel(history_ref, chunks_ref):
    heads, _, both = chunks_ref.shape
    size = both // 2
    for head in range(heads):
        chunks_ref[head, :, :size] = history_ref[:, head * size : (head + 1) * size]
        chunks_ref[head, :, size:] = history_ref[:, (heads + head) * size : (heads + head + 1) * size]


def used_blocks(blocks_ref, length_ref, owner_ref):
    requests, width = blocks_ref.shape
    owners = owner_ref[...]
    positions = lax.broadcasted_iota(jnp.int32, (16, owners.shape[1]), 0)
    usage = jnp.zeros(positions.shape, F32)
    for request in range(requests):
        used = jnp.zeros(positions.shape, F32)
        for entry in range(width):
            block = jnp.where(entry < length_ref[request], blocks_ref[request, entry], -1)
            used = used + jnp.where(positions == block, 1.0, 0.0)
        usage = usage + jnp.where(owners == request, used, 0.0)
    return usage


def prepare_kernel(blocks_ref, length_ref, owner_ref, cand_ref, cot_ref, in_ref, out_ref, bundle_ref):
    rows = cand_ref[...].astype(F32)
    centered = rows - jnp.mean(rows, axis=-1, keepdims=True)
    inv_scale = lax.rsqrt(jnp.mean(centered * centered, axis=-1, keepdims=True) + 1e-05)
    normed = (centered * inv_scale).astype(BF16)
    projected = jnp.dot(normed, in_ref[...], preferred_element_type=F32).T
    zed_grad = lax.dot_general(out_ref[...], cot_ref[...], NT, preferred_element_type=F32)
    inner, count = out_ref.shape[0], cand_ref.shape[0]
    size = inner // HEADS
    usage = used_blocks(blocks_ref, length_ref, owner_ref).astype(BF16)
    bundle_ref[:, :, count:] = jnp.zeros(
        (HEADS, bundle_ref.shape[1], bundle_ref.shape[2] - count), BF16
    )
    for head in range(HEADS):
        part = slice(head * size, (head + 1) * size)
        gate_in = projected[inner + head * size : inner + (head + 1) * size]
        gating = gate_in * sigmoid(gate_in)
        bundle_ref[head, 0:size, :count] = projected[part].astype(BF16)
        bundle_ref[head, size : 2 * size, :count] = gating.astype(BF16)
        bundle_ref[head, 2 * size : 3 * size, :count] = (zed_grad[part] * gating).astype(BF16)
        bundle_ref[head, 3 * size :, :count] = usage


def scored(ring, blocks_ref, bundle_ref, group):
    span = served(ring, group)
    tall, size = blocks_ref.shape[1], blocks_ref.shape[2] // 2
    rows = blocks_ref[span[0] : span[-1] + 1].reshape(len(span) * tall, 2 * size)
    scores = jnp.dot(rows[:, :size], bundle_ref[group, 0:size], preferred_element_type=F32)
    scores = scores * (1.0 / math.sqrt(size))
    usage = bundle_ref[group, 3 * size :].astype(F32)
    parts = []
    for place, block in enumerate(span):
        position = HEADS * ring + block - group
        parts.append((scores[place * tall : (place + 1) * tall], usage[position : position + 1]))
    return rows[:, size:], parts


def attend(ring, blocks_ref, bundle_ref, group):
    values, parts = scored(ring, blocks_ref, bundle_ref, group)
    weights = [(scores * sigmoid(scores) * usage).astype(BF16) for scores, usage in parts]
    return lax.dot_general(
        values, jnp.concatenate(weights, axis=0), TN, preferred_element_type=F32
    )


def early_kernel(ring0, ring1, bundle, attended_ref):
    for group in range(HEADS):
        attended_ref[group] = attend(0, ring0, bundle, group) + attend(1, ring1, bundle, group)


def late_kernel(ring2, bundle, before, attended_ref, stats_ref):
    size = before.shape[1]
    for group in range(HEADS):
        attended = before[group]
        if len(served(2, group)) > 0:
            attended = attended + attend(2, ring2, bundle, group)
        attended_ref[group] = attended
        dy = bundle[group, 2 * size : 3 * size].astype(F32)
        mean = jnp.mean(attended, axis=0, keepdims=True)
        centered = attended - mean
        stats_ref[4 * group : 4 * group + 1] = mean
        stats_ref[4 * group + 1 : 4 * group + 2] = jnp.sum(centered * centered, axis=0, keepdims=True)
        stats_ref[4 * group + 2 : 4 * group + 3] = jnp.sum(dy, axis=0, keepdims=True)
        stats_ref[4 * group + 3 : 4 * group + 4] = jnp.sum(dy * centered, axis=0, keepdims=True)


def norm_kernel(attended, bundle, stats, gated_ref, grad_ref):
    size = attended.shape[1]
    width = HEADS * size
    for group in range(HEADS):
        head_stats = [stats[head, 4 * group : 4 * group + 4] for head in range(HEADS)]
        mean = sum(one[0:1] for one in head_stats) * (1.0 / HEADS)
        apart = [one[0:1] - mean for one in head_stats]
        spread = sum(one[1:2] + size * off * off for one, off in zip(head_stats, apart))
        inv_scale = lax.rsqrt(spread * (1.0 / width) + 1e-05)
        mean_dy = sum(one[2:3] for one in head_stats) * (1.0 / width)
        mixed = sum(one[3:4] + off * one[2:3] for one, off in zip(head_stats, apart))
        mean_mixed = mixed * inv_scale * (1.0 / width)
        normed = (attended[group] - mean) * inv_scale
        dy = bundle[group, 2 * size : 3 * size].astype(F32)
        gated_ref[group] = (normed * bundle[group, size : 2 * size].astype(F32)).astype(BF16)
        grad_ref[group] = (inv_scale * (dy - mean_dy - normed * mean_mixed)).astype(BF16)


def out_grad_kernel(total_cands, gated, cots, out_grad_ref):
    count = cots.shape[1]
    total = None
    for group in range(HEADS):
        part = jnp.dot(gated[group, :, :count], cots[group], preferred_element_type=F32)
        total = part if total is None else total + part
    total = (total * (1.0 / math.sqrt(total_cands))).astype(BF16)
    halves, rows_of, lines, columns = out_grad_ref.shape
    for half in range(halves):
        for row in range(rows_of):
            out_grad_ref[half, row] = total[
                row * lines : (row + 1) * lines, half * columns : (half + 1) * columns
            ]


def back(ring, blocks_ref, bundle, grads, sum_ref):
    tall, size = blocks_ref.shape[1], blocks_ref.shape[2] // 2
    scale = 1.0 / math.sqrt(size)
    keys, values = {}, {}
    for group in range(HEADS):
        span = served(ring, group)
        if len(span) == 0:
            continue
        grad = grads[group]
        value_rows, parts = scored(ring, blocks_ref, bundle, group)
        weight_grad = jnp.dot(value_rows, grad, preferred_element_type=F32)
        for place, block in enumerate(span):
            scores, usage = parts[place]
            part = sigmoid(scores)
            weights = scores * part
            slopes = (part + weights * (1.0 - part)) * (usage * scale)
            lines = weight_grad[place * tall : (place + 1) * tall]
            key = lax.dot_general(
                (lines * slopes).astype(BF16), bundle[group, 0:size], NT, preferred_element_type=F32
            )
            value = lax.dot_general(
                (weights * usage).astype(BF16), grad, NT, preferred_element_type=F32
            )
            keys[block] = keys[block] + key if block in keys else key
            values[block] = values[block] + value if block in values else value
    for block in keys:
        sum_ref[block, :, 0:size] = keys[block].astype(sum_ref.dtype)
        sum_ref[block, :, size:] = values[block].astype(sum_ref.dtype)


def far_back_kernel(ring1, ring2, bundle, grads, back1, back2):
    back(2, ring2, bundle, grads, back2)
    back(1, ring1, bundle, grads, back1)


def near_back_kernel(ring0, bundle, grads, back0):
    back(0, ring0, bundle, grads, back0)


def parcel_kernel(place_ref, gated_ref, back0, back1, back2, *parcel_refs):
    size = gated_ref.shape[1]
    for step, parcel in enumerate(parcel_refs):
        target = lax.rem(place_ref[0] + step, HEADS)
        parcel[0:size] = gated_ref[target]
        total = back0[target] + back1[target].astype(F32)
        last = jnp.minimum(target, back2.shape[0] - 1)
        more = back2[last].astype(F32)
        parcel[size:] = (total + jnp.where(last == target, more, 0.0)).astype(BF16)


def join_kernel(place_ref, cand_ref, out_ref, *refs):
    *parcels, result_ref, grad_ref = refs
    inner, count = out_ref.shape[0], cand_ref.shape[0]
    size = inner // HEADS
    product = None
    for step, parcel in enumerate(parcels):
        head = lax.rem(place_ref[0] + HEADS - step, HEADS)
        rows = pl.ds(pl.multiple_of(head * size, size), size)
        part = lax.dot_general(parcel[0:size, :count], out_ref[rows], TN, preferred_element_type=F32)
        product = part if product is None else product + part
        grad_ref[:, rows] = parcel[size:, 0:size]
        grad_ref[:, pl.ds(pl.multiple_of(inner + head * size, size), size)] = parcel[size:, size:]
    result_ref[...] = (cand_ref[...].astype(F32) + product).astype(BF16)


def moved(block, distance):
    size = lax.axis_size(DEPTH)
    return lax.ppermute(block, DEPTH, [((i + distance) % size, i) for i in range(size)])


def exchanged(chunks, axis):
    return lax.all_to_all(chunks, axis, 0, 0, tiled=True)


def spread_over(block, axis):
    size = lax.axis_size(axis)
    return exchanged(jnp.broadcast_to(block[None], (size,) + block.shape), axis)


def summed(parts):
    return jnp.sum(parts.astype(F32), axis=0)


def on_device(
    candidates,
    cotangent,
    history,
    request_blocks,
    request_length,
    candidate_request,
    in_weight,
    out_weight,
):
    tall, wide = history.shape
    inner = wide // 2
    size = inner // HEADS
    count = candidates.shape[0]
    lanes = 2 * size
    total_cands = count * lax.axis_size(ALL)
    barrier = lax.optimization_barrier
    place = lax.axis_index("x").reshape(1).astype(jnp.int32)

    cots = lax.all_gather(cotangent, "x")
    ring_shape = shaped((HEADS, tall, 2 * size), BF16)
    ring0 = exchanged(on_core(split_kernel, ring_shape, history), "x")

    ring2 = moved(ring0[: HEADS - 1], 2)
    ring1 = moved(ring0, 1)
    bundle = on_core(
        prepare_kernel,
        shaped((HEADS, 3 * size + 16, lanes), BF16),
        candidate_request.reshape(1, count),
        candidates,
        cotangent,
        in_weight,
        out_weight,
        scalars=(request_blocks, request_length),
    )
    bundle = exchanged(bundle, "x")

    attended_shape = shaped((HEADS, size, lanes), F32)
    before = on_core(early_kernel, attended_shape, ring0, ring1, bundle)
    attended, stats = on_core(
        late_kernel, (attended_shape, shaped((4 * HEADS, lanes), F32)), ring2, bundle, before
    )
    stats = spread_over(stats, "x")
    head_shape = shaped((HEADS, size, lanes), BF16)
    cores, zh, zl, xs = (lax.axis_size(name) for name in ("core", "zh", "zl", "x"))
    own, half = size // (zl * xs), out_weight.shape[1] // cores
    gated, grads = on_core(norm_kernel, (head_shape, head_shape), attended, bundle, stats)
    back1, back2 = on_core(
        far_back_kernel, (shaped(ring1.shape, BF16), shaped(ring2.shape, BF16)), ring1, ring2, bundle, grads
    )
    back2 = moved(back2, -2)
    back1 = moved(back1, -1)
    out_grad = on_core(
        lambda *refs: out_grad_kernel(total_cands, *refs),
        shaped((cores, zl, size // zl, half), BF16),
        gated,
        cots,
    )
    out_grad, late_grads = barrier((out_grad, grads))
    part = exchanged(out_grad.reshape(cores * zl, size // zl, half), ("core", "zl"))
    back0 = on_core(near_back_kernel, shaped(ring0.shape, F32), ring0, bundle, late_grads)
    part, back0, back1, back2 = barrier((summed(part).astype(BF16), back0, back1, back2))
    part = jnp.broadcast_to(part.reshape(1, xs, own, half), (zh, xs, own, half))
    part = exchanged(part.reshape(zh * xs, own, half), ("zh", "x")).reshape(zh, xs, own, half)
    part = lax.dynamic_index_in_dim(part, lax.axis_index("zh"), axis=1, keepdims=False)

    parcels = on_core(
        parcel_kernel, [shaped((2 * size, lanes), BF16)] * HEADS, gated, back0, back1, back2, scalars=(place,)
    )
    arrived = [
        lax.ppermute(parcel, "x", [(i, (i + step) % HEADS) for i in range(HEADS)]) if step else parcel
        for step, parcel in enumerate(parcels)
    ]
    part, arrived = barrier((summed(part), arrived))
    part = spread_over(part, ("y", "core")).reshape(-1, cores, own, half)
    grad_rows = summed(part).transpose(1, 0, 2).reshape(own, cores * half)

    layer_out, grad_history = on_core(
        join_kernel,
        (shaped(candidates.shape, BF16), shaped(history.shape, BF16)),
        candidates,
        out_weight,
        *arrived,
        scalars=(place,),
    )
    return (layer_out, grad_rows, grad_history)


def solution(mesh):
    inner = Mesh(mesh.devices.reshape(4, 2, 4, 4, 4), ALL)
    rows = P(ALL)
    return jax.shard_map(
        on_device,
        mesh=inner,
        in_specs=(rows, rows, rows, rows, rows, rows, P(), P()),
        out_specs=(rows, P(("zh", "zl", "x")), rows),
        check_vma=False,
    )
```

```python
import math

import jax
import jax.numpy as jnp
from jax import lax
from jax.experimental import pallas as pl
from jax.experimental.pallas import tpu as pltpu
from jax.sharding import Mesh, PartitionSpec as P

HEADS = 4
SPAN = 8
BF16 = jnp.bfloat16
F32 = jnp.float32
ALL = ("y", "core", "zh", "zl", "x")
DEPTH = ("zh", "zl")
NT = (((1,), (1,)), ((), ()))
TN = (((0,), (0,)), ((), ()))


def on_core(kernel, outs, *operands, scalars=()):
    spaces = [pltpu.SMEM] * len(scalars) + [pltpu.VMEM] * len(operands)
    return pl.pallas_call(
        kernel,
        out_shape=outs,
        in_specs=[pl.BlockSpec(memory_space=space) for space in spaces],
        out_specs=jax.tree.map(lambda _: pl.BlockSpec(memory_space=pltpu.VMEM), outs),
        compiler_params=pltpu.CompilerParams(vmem_limit_bytes=12 * 1024 * 1024),
    )(*scalars, *operands)


def on_fetched(kernel, outs, *operands, scalars=()):
    many = len(scalars) + len(operands)
    first = len(jax.tree.leaves(outs)) + many

    def body(*refs):
        places, arrivals = refs[first : first + many], refs[first + many]
        copies = [
            pltpu.make_async_copy(source, place, arrivals.at[i])
            for i, (source, place) in enumerate(zip(refs[:many], places))
        ]
        for copy in copies:
            copy.start()
        kernel(*zip(places, [copy.wait for copy in copies]), *refs[many:first])

    return pl.pallas_call(
        body,
        out_shape=outs,
        in_specs=[pl.BlockSpec(memory_space=pl.ANY)] * many,
        out_specs=jax.tree.map(lambda _: pl.BlockSpec(memory_space=pltpu.VMEM), outs),
        scratch_shapes=[pltpu.SMEM(one.shape, one.dtype) for one in scalars]
        + [pltpu.VMEM(one.shape, one.dtype) for one in operands]
        + [pltpu.SemaphoreType.DMA((many,))],
        compiler_params=pltpu.CompilerParams(vmem_limit_bytes=56 * 1024 * 1024),
    )(*scalars, *operands)


def shaped(shape, kind):
    return jax.ShapeDtypeStruct(shape, kind)


def sigmoid(values):
    return 0.5 + 0.5 * jnp.tanh(0.5 * values)


def served(ring, group):
    return {0: range(group, HEADS), 1: range(0, HEADS), 2: range(0, group)}[ring]


def split_kernel(history_ref, chunks_ref):
    heads, _, both = chunks_ref.shape
    size = both // 2
    for head in range(heads):
        chunks_ref[head, :, :size] = history_ref[:, head * size : (head + 1) * size]
        chunks_ref[head, :, size:] = history_ref[:, (heads + head) * size : (heads + head + 1) * size]


def used_blocks(blocks_ref, length_ref, owner_ref):
    requests, width = blocks_ref.shape
    owners = owner_ref[...]
    positions = lax.broadcasted_iota(jnp.int32, (16, owners.shape[1]), 0)
    usage = jnp.zeros(positions.shape, F32)
    for request in range(requests):
        used = jnp.zeros(positions.shape, F32)
        for entry in range(width):
            block = jnp.where(entry < length_ref[request], blocks_ref[request, entry], -1)
            used = used + jnp.where(positions == block, 1.0, 0.0)
        usage = usage + jnp.where(owners == request, used, 0.0)
    return usage


def prepare_kernel(blocks, lengths, owners, cands, cots, in_weight, out_weight, bundle_ref):
    (cand_ref, cand_here), (cot_ref, cot_here) = cands, cots
    (in_ref, in_here), (out_ref, out_here) = in_weight, out_weight
    inner, count = out_ref.shape[0], cand_ref.shape[0]
    size = inner // HEADS
    bundle_ref[:, :, count:] = jnp.zeros(
        (HEADS, bundle_ref.shape[1], bundle_ref.shape[2] - count), BF16
    )
    for _, here in (blocks, lengths, owners):
        here()
    usage = used_blocks(blocks[0], lengths[0], owners[0]).astype(BF16)
    cand_here()
    rows = cand_ref[...].astype(F32)
    centered = rows - jnp.mean(rows, axis=-1, keepdims=True)
    inv_scale = lax.rsqrt(jnp.mean(centered * centered, axis=-1, keepdims=True) + 1e-05)
    normed = (centered * inv_scale).astype(BF16)
    cot_here()
    out_here()
    zed_grad = lax.dot_general(out_ref[...], cot_ref[...], NT, preferred_element_type=F32)
    in_here()
    projected = jnp.dot(normed, in_ref[...], preferred_element_type=F32).T
    for head in range(HEADS):
        part = slice(head * size, (head + 1) * size)
        gate_in = projected[inner + head * size : inner + (head + 1) * size]
        gating = gate_in * sigmoid(gate_in)
        bundle_ref[head, 0:size, :count] = projected[part].astype(BF16)
        bundle_ref[head, size : 2 * size, :count] = gating.astype(BF16)
        bundle_ref[head, 2 * size : 3 * size, :count] = (zed_grad[part] * gating).astype(BF16)
        bundle_ref[head, 3 * size :, :count] = usage


def scored(ring, blocks_ref, bundle_ref, group):
    span = served(ring, group)
    tall, size = blocks_ref.shape[1], blocks_ref.shape[2] // 2
    rows = blocks_ref[span[0] : span[-1] + 1].reshape(len(span) * tall, 2 * size)
    scores = jnp.dot(rows[:, :size], bundle_ref[group, 0:size], preferred_element_type=F32)
    scores = scores * (1.0 / math.sqrt(size))
    usage = bundle_ref[group, 3 * size :].astype(F32)
    parts = []
    for place, block in enumerate(span):
        position = HEADS * ring + block - group
        parts.append((scores[place * tall : (place + 1) * tall], usage[position : position + 1]))
    return rows[:, size:], parts


def attend(ring, blocks_ref, bundle_ref, group):
    values, parts = scored(ring, blocks_ref, bundle_ref, group)
    weights = [(scores * sigmoid(scores) * usage).astype(BF16) for scores, usage in parts]
    return lax.dot_general(
        values, jnp.concatenate(weights, axis=0), TN, preferred_element_type=F32
    )


def early_kernel(ring0, ring1, bundle, attended_ref):
    for group in range(HEADS):
        attended_ref[group] = attend(0, ring0, bundle, group) + attend(1, ring1, bundle, group)


def late_kernel(ring2, bundle, before, attended_ref, stats_ref):
    size = before.shape[1]
    for group in range(HEADS):
        attended = before[group]
        if len(served(2, group)) > 0:
            attended = attended + attend(2, ring2, bundle, group)
        attended_ref[group] = attended
        dy = bundle[group, 2 * size : 3 * size].astype(F32)
        mean = jnp.mean(attended, axis=0, keepdims=True)
        centered = attended - mean
        stats_ref[4 * group : 4 * group + 1] = mean
        stats_ref[4 * group + 1 : 4 * group + 2] = jnp.sum(centered * centered, axis=0, keepdims=True)
        stats_ref[4 * group + 2 : 4 * group + 3] = jnp.sum(dy, axis=0, keepdims=True)
        stats_ref[4 * group + 3 : 4 * group + 4] = jnp.sum(dy * centered, axis=0, keepdims=True)


def norm_kernel(attended, bundle, stats, gated_ref, grad_ref):
    size = attended.shape[1]
    width = HEADS * size
    for group in range(HEADS):
        head_stats = [stats[head, 4 * group : 4 * group + 4] for head in range(HEADS)]
        mean = sum(one[0:1] for one in head_stats) * (1.0 / HEADS)
        apart = [one[0:1] - mean for one in head_stats]
        spread = sum(one[1:2] + size * off * off for one, off in zip(head_stats, apart))
        inv_scale = lax.rsqrt(spread * (1.0 / width) + 1e-05)
        mean_dy = sum(one[2:3] for one in head_stats) * (1.0 / width)
        mixed = sum(one[3:4] + off * one[2:3] for one, off in zip(head_stats, apart))
        mean_mixed = mixed * inv_scale * (1.0 / width)
        normed = (attended[group] - mean) * inv_scale
        dy = bundle[group, 2 * size : 3 * size].astype(F32)
        gated_ref[group] = (normed * bundle[group, size : 2 * size].astype(F32)).astype(BF16)
        grad_ref[group] = (inv_scale * (dy - mean_dy - normed * mean_mixed)).astype(BF16)


def out_grad_kernel(total_cands, gates, cot_rows, out_grad_ref):
    (gated, gated_here), (cots, cots_here) = gates, cot_rows
    count = cots.shape[1]
    total = None
    gated_here()
    cots_here()
    for group in range(HEADS):
        part = jnp.dot(gated[group, :, :count], cots[group], preferred_element_type=F32)
        total = part if total is None else total + part
    total = (total * (1.0 / math.sqrt(total_cands))).astype(BF16)
    halves, rows_of, lines, columns = out_grad_ref.shape
    for half in range(halves):
        for row in range(rows_of):
            out_grad_ref[half, row] = total[
                row * lines : (row + 1) * lines, half * columns : (half + 1) * columns
            ]


def back(ring, blocks_ref, bundle, grads, sum_ref):
    tall, size = blocks_ref.shape[1], blocks_ref.shape[2] // 2
    scale = 1.0 / math.sqrt(size)
    keys, values = {}, {}
    for group in range(HEADS):
        span = served(ring, group)
        if len(span) == 0:
            continue
        grad = grads[group]
        value_rows, parts = scored(ring, blocks_ref, bundle, group)
        weight_grad = jnp.dot(value_rows, grad, preferred_element_type=F32)
        for place, block in enumerate(span):
            scores, usage = parts[place]
            part = sigmoid(scores)
            weights = scores * part
            slopes = (part + weights * (1.0 - part)) * (usage * scale)
            lines = weight_grad[place * tall : (place + 1) * tall]
            key = lax.dot_general(
                (lines * slopes).astype(BF16), bundle[group, 0:size], NT, preferred_element_type=F32
            )
            value = lax.dot_general(
                (weights * usage).astype(BF16), grad, NT, preferred_element_type=F32
            )
            keys[block] = keys[block] + key if block in keys else key
            values[block] = values[block] + value if block in values else value
    for block in keys:
        sum_ref[block, :, 0:size] = keys[block].astype(sum_ref.dtype)
        sum_ref[block, :, size:] = values[block].astype(sum_ref.dtype)


def back2_kernel(ring2, bundle, grads, sum_ref):
    back(2, ring2, bundle, grads, sum_ref)


def back1_kernel(ring1, bundle, grads, arrived, sum_ref, total):
    back(1, ring1, bundle, grads, total)
    count = arrived.shape[0]
    sum_ref[:count] = (total[:count] + arrived[...].astype(F32)).astype(BF16)
    sum_ref[count:] = total[count:].astype(BF16)


def back0_kernel(ring0, bundle, grads, sum_ref):
    back(0, ring0, bundle, grads, sum_ref)


def fold_kernel(parts, folded_ref):
    total = jnp.sum(parts[...].astype(F32), axis=0).astype(BF16)
    lines = folded_ref.shape[2]
    for row in range(folded_ref.shape[1]):
        for copy in range(folded_ref.shape[0]):
            folded_ref[copy, row] = total[row * lines : (row + 1) * lines]


def pick_kernel(place_ref, parts, spread_ref):
    total = jnp.zeros(spread_ref.shape[1:], F32)
    for source in range(parts.shape[0]):
        total = total + parts[source, place_ref[0]].astype(F32)
    for peer in range(spread_ref.shape[0]):
        spread_ref[peer] = total


def last_kernel(parts, rows_ref):
    cores = parts.shape[1]
    half = rows_ref.shape[1] // cores
    for core in range(cores):
        rows_ref[:, core * half : (core + 1) * half] = jnp.sum(parts[:, core], axis=0)


def parcel_kernel(place_ref, gated_ref, back0, back1, *parcel_refs):
    size = gated_ref.shape[1]
    for step, parcel in enumerate(parcel_refs):
        target = lax.rem(place_ref[0] + step, HEADS)
        parcel[0:size] = gated_ref[target]
        parcel[size:] = (back0[target] + back1[target].astype(F32)).astype(BF16)


def join_kernel(place_ref, cand_ref, out_ref, *refs):
    *parcels, result_ref, grad_ref = refs
    inner, count = out_ref.shape[0], cand_ref.shape[0]
    size = inner // HEADS
    product = None
    for step, parcel in enumerate(parcels):
        head = lax.rem(place_ref[0] + HEADS - step, HEADS)
        rows = pl.ds(pl.multiple_of(head * size, size), size)
        part = lax.dot_general(parcel[0:size, :count], out_ref[rows], TN, preferred_element_type=F32)
        product = part if product is None else product + part
        grad_ref[:, rows] = parcel[size:, 0:size]
        grad_ref[:, pl.ds(pl.multiple_of(inner + head * size, size), size)] = parcel[size:, size:]
    result_ref[...] = (cand_ref[...].astype(F32) + product).astype(BF16)


def moved(block, distance):
    size = lax.axis_size(DEPTH)
    return lax.ppermute(block, DEPTH, [((i + distance) % size, i) for i in range(size)])


def exchanged(chunks, axis):
    return lax.all_to_all(chunks, axis, 0, 0, tiled=True)


def spread_over(block, axis):
    size = lax.axis_size(axis)
    return exchanged(jnp.broadcast_to(block[None], (size,) + block.shape), axis)


def summed(parts):
    return jnp.sum(parts.astype(F32), axis=0)


def on_device(
    candidates,
    cotangent,
    history,
    request_blocks,
    request_length,
    candidate_request,
    in_weight,
    out_weight,
):
    tall, wide = history.shape
    inner = wide // 2
    size = inner // HEADS
    count = candidates.shape[0]
    lanes = 2 * size
    total_cands = count * lax.axis_size(ALL)
    barrier = lax.optimization_barrier
    place = lax.axis_index("x").reshape(1).astype(jnp.int32)

    cots = lax.all_gather(cotangent, "x")
    ring_shape = shaped((HEADS, tall, 2 * size), BF16)
    ring0 = exchanged(on_core(split_kernel, ring_shape, history), "x")

    ring2 = moved(ring0[: HEADS - 1], 2)
    ring1 = moved(ring0, 1)
    bundle = on_fetched(
        prepare_kernel,
        shaped((HEADS, 3 * size + 16, lanes), BF16),
        candidate_request.reshape(1, count),
        candidates,
        cotangent,
        in_weight,
        out_weight,
        scalars=(request_blocks, request_length),
    )
    bundle = exchanged(bundle, "x")

    attended_shape = shaped((HEADS, size, lanes), F32)
    before = on_core(early_kernel, attended_shape, ring0, ring1, bundle)
    attended, stats = on_core(
        late_kernel, (attended_shape, shaped((4 * HEADS, lanes), F32)), ring2, bundle, before
    )
    stats = spread_over(stats, "x")
    head_shape = shaped((HEADS, size, lanes), BF16)
    cores, zh, zl, xs = (lax.axis_size(name) for name in ("core", "zh", "zl", "x"))
    own, half = size // (zl * xs), out_weight.shape[1] // cores
    gated, grads = on_core(norm_kernel, (head_shape, head_shape), attended, bundle, stats)
    back2 = moved(on_core(back2_kernel, shaped(ring2.shape, BF16), ring2, bundle, grads), -1)
    out_grad = on_fetched(
        lambda *refs: out_grad_kernel(total_cands, *refs),
        shaped((cores, zl, size // zl, half), BF16),
        gated,
        cots,
    )
    out_grad, late_grads = barrier((out_grad, grads))
    part = exchanged(out_grad.reshape(cores * zl, size // zl, half), ("core", "zl"))
    back1 = pl.pallas_call(
        back1_kernel,
        out_shape=shaped(ring1.shape, BF16),
        in_specs=[pl.BlockSpec(memory_space=pltpu.VMEM)] * 4,
        out_specs=pl.BlockSpec(memory_space=pltpu.VMEM),
        scratch_shapes=[pltpu.VMEM(ring1.shape, F32)],
        compiler_params=pltpu.CompilerParams(vmem_limit_bytes=12 * 1024 * 1024),
    )(ring1, bundle, late_grads, back2)
    part, back1 = barrier((part, back1))
    back1 = moved(back1, -1)
    part = on_core(fold_kernel, shaped((zh, xs, own, half), BF16), part)
    back0 = on_core(back0_kernel, shaped(ring0.shape, F32), ring0, bundle, late_grads)
    part = exchanged(part.reshape(zh * xs, own, half), ("zh", "x")).reshape(zh, xs, own, half)
    depth = lax.axis_index("zh").reshape(1).astype(jnp.int32)
    peers = lax.axis_size("y") * cores
    part = on_core(pick_kernel, shaped((peers, own, half), F32), part, scalars=(depth,))

    parcels = on_core(
        parcel_kernel, [shaped((2 * size, lanes), BF16)] * HEADS, gated, back0, back1, scalars=(place,)
    )
    arrived = [
        lax.ppermute(parcel, "x", [(i, (i + step) % HEADS) for i in range(HEADS)]) if step else parcel
        for step, parcel in enumerate(parcels)
    ]
    part = exchanged(part, ("y", "core")).reshape(-1, cores, own, half)
    grad_rows = on_core(last_kernel, shaped((own, cores * half), F32), part)

    layer_out, grad_history = on_core(
        join_kernel,
        (shaped(candidates.shape, BF16), shaped(history.shape, BF16)),
        candidates,
        out_weight,
        *arrived,
        scalars=(place,),
    )
    return (layer_out, grad_rows, grad_history)


def solution(mesh):
    inner = Mesh(mesh.devices.reshape(4, 2, 4, 4, 4), ALL)
    rows = P(ALL)
    return jax.shard_map(
        on_device,
        mesh=inner,
        in_specs=(rows, rows, rows, rows, rows, rows, P(), P()),
        out_specs=(rows, P(("zh", "zl", "x")), rows),
        check_vma=False,
    )
```

```python
import math

import jax
import jax.numpy as jnp
from jax import lax
from jax.experimental import pallas as pl
from jax.experimental.pallas import tpu as pltpu
from jax.sharding import Mesh, PartitionSpec as P

HEADS = 4
SPAN = 8
BF16 = jnp.bfloat16
F32 = jnp.float32
ALL = ("y", "core", "zh", "zl", "x")
DEPTH = ("zh", "zl")
NT = (((1,), (1,)), ((), ()))
TN = (((0,), (0,)), ((), ()))


def on_core(kernel, outs, *operands, scalars=()):
    spaces = [pltpu.SMEM] * len(scalars) + [pltpu.VMEM] * len(operands)
    return pl.pallas_call(
        kernel,
        out_shape=outs,
        in_specs=[pl.BlockSpec(memory_space=space) for space in spaces],
        out_specs=jax.tree.map(lambda _: pl.BlockSpec(memory_space=pltpu.VMEM), outs),
        compiler_params=pltpu.CompilerParams(vmem_limit_bytes=12 * 1024 * 1024),
    )(*scalars, *operands)


def on_fetched(kernel, outs, *operands, scalars=(), local=()):
    fetched = list(scalars) + list(operands)
    many = len(fetched)
    first = many + len(local) + len(jax.tree.leaves(outs))
    pieces = [4 if one.size >= 1 << 19 else 1 for one in fetched]

    def body(*refs):
        places, arrivals = refs[first : first + many], refs[first + many]
        waits = []
        for i, (source, place) in enumerate(zip(refs[:many], places)):
            step = place.shape[0] // pieces[i]
            copies = []
            for part in range(pieces[i]):
                rows = (slice(None),) if pieces[i] == 1 else (pl.ds(part * step, step),)
                copy = pltpu.make_async_copy(source.at[rows], place.at[rows], arrivals.at[i, part])
                copy.start()
                copies.append(copy)
            waits.append(lambda copies=copies: [copy.wait() for copy in copies])
        kernel(*zip(places, waits), *refs[many:first])

    return pl.pallas_call(
        body,
        out_shape=outs,
        in_specs=[pl.BlockSpec(memory_space=pl.ANY)] * many
        + [pl.BlockSpec(memory_space=pltpu.VMEM)] * len(local),
        out_specs=jax.tree.map(lambda _: pl.BlockSpec(memory_space=pltpu.VMEM), outs),
        scratch_shapes=[pltpu.SMEM(one.shape, one.dtype) for one in scalars]
        + [pltpu.VMEM(one.shape, one.dtype) for one in operands]
        + [pltpu.SemaphoreType.DMA((many, 4))],
        compiler_params=pltpu.CompilerParams(vmem_limit_bytes=56 * 1024 * 1024),
    )(*fetched, *local)


def shaped(shape, kind):
    return jax.ShapeDtypeStruct(shape, kind)


def sigmoid(values):
    return 0.5 + 0.5 * jnp.tanh(0.5 * values)


def served(ring, group):
    return {0: range(group, HEADS), 1: range(0, HEADS), 2: range(0, group)}[ring]


def split_kernel(history_ref, chunks_ref, arrivals):
    heads, _, both = chunks_ref.shape
    size = both // 2
    copies = []
    for head in range(heads):
        for kind in range(2):
            columns = pl.ds((kind * heads + head) * size, size)
            copies.append(
                pltpu.make_async_copy(
                    history_ref.at[:, columns],
                    chunks_ref.at[head, :, pl.ds(kind * size, size)],
                    arrivals.at[head, kind],
                )
            )
    for copy in copies:
        copy.start()
    for copy in copies:
        copy.wait()


def used_blocks(blocks_ref, length_ref, owner_ref):
    requests, width = blocks_ref.shape
    owners = owner_ref[...]
    positions = lax.broadcasted_iota(jnp.int32, (16, owners.shape[1]), 0)
    usage = jnp.zeros(positions.shape, F32)
    for request in range(requests):
        used = jnp.zeros(positions.shape, F32)
        for entry in range(width):
            block = jnp.where(entry < length_ref[request], blocks_ref[request, entry], -1)
            used = used + jnp.where(positions == block, 1.0, 0.0)
        usage = usage + jnp.where(owners == request, used, 0.0)
    return usage


def prepare_kernel(blocks, lengths, owners, cands, cots, in_weight, out_weight, bundle_ref):
    (cand_ref, cand_here), (cot_ref, cot_here) = cands, cots
    (in_ref, in_here), (out_ref, out_here) = in_weight, out_weight
    inner, count = out_ref.shape[0], cand_ref.shape[0]
    size = inner // HEADS
    bundle_ref[:, :, count:] = jnp.zeros(
        (HEADS, bundle_ref.shape[1], bundle_ref.shape[2] - count), BF16
    )
    for _, here in (blocks, lengths, owners):
        here()
    usage = used_blocks(blocks[0], lengths[0], owners[0]).astype(BF16)
    cand_here()
    rows = cand_ref[...].astype(F32)
    centered = rows - jnp.mean(rows, axis=-1, keepdims=True)
    inv_scale = lax.rsqrt(jnp.mean(centered * centered, axis=-1, keepdims=True) + 1e-05)
    normed = (centered * inv_scale).astype(BF16)
    cot_here()
    out_here()
    zed_grad = lax.dot_general(out_ref[...], cot_ref[...], NT, preferred_element_type=F32)
    in_here()
    projected = jnp.dot(normed, in_ref[...], preferred_element_type=F32).T
    for head in range(HEADS):
        part = slice(head * size, (head + 1) * size)
        gate_in = projected[inner + head * size : inner + (head + 1) * size]
        gating = gate_in * sigmoid(gate_in)
        bundle_ref[head, 0:size, :count] = projected[part].astype(BF16)
        bundle_ref[head, size : 2 * size, :count] = gating.astype(BF16)
        bundle_ref[head, 2 * size : 3 * size, :count] = (zed_grad[part] * gating).astype(BF16)
        bundle_ref[head, 3 * size :, :count] = usage


def scored(ring, blocks_ref, bundle_ref, group):
    span = served(ring, group)
    tall, size = blocks_ref.shape[1], blocks_ref.shape[2] // 2
    rows = blocks_ref[span[0] : span[-1] + 1].reshape(len(span) * tall, 2 * size)
    scores = jnp.dot(rows[:, :size], bundle_ref[group, 0:size], preferred_element_type=F32)
    scores = scores * (1.0 / math.sqrt(size))
    usage = bundle_ref[group, 3 * size :].astype(F32)
    parts = []
    for place, block in enumerate(span):
        position = HEADS * ring + block - group
        parts.append((scores[place * tall : (place + 1) * tall], usage[position : position + 1]))
    return rows[:, size:], parts


def attend(ring, blocks_ref, bundle_ref, group):
    values, parts = scored(ring, blocks_ref, bundle_ref, group)
    weights = [(scores * sigmoid(scores) * usage).astype(BF16) for scores, usage in parts]
    return lax.dot_general(
        values, jnp.concatenate(weights, axis=0), TN, preferred_element_type=F32
    )


def early_kernel(ring0, ring1, bundle, attended_ref):
    for group in range(HEADS):
        attended_ref[group] = attend(0, ring0, bundle, group) + attend(1, ring1, bundle, group)


def late_kernel(ring2, bundle, before, attended_ref, stats_ref):
    size = before.shape[1]
    for group in range(HEADS):
        attended = before[group]
        if len(served(2, group)) > 0:
            attended = attended + attend(2, ring2, bundle, group)
        attended_ref[group] = attended
        dy = bundle[group, 2 * size : 3 * size].astype(F32)
        mean = jnp.mean(attended, axis=0, keepdims=True)
        centered = attended - mean
        stats_ref[4 * group : 4 * group + 1] = mean
        stats_ref[4 * group + 1 : 4 * group + 2] = jnp.sum(centered * centered, axis=0, keepdims=True)
        stats_ref[4 * group + 2 : 4 * group + 3] = jnp.sum(dy, axis=0, keepdims=True)
        stats_ref[4 * group + 3 : 4 * group + 4] = jnp.sum(dy * centered, axis=0, keepdims=True)


def norm_kernel(attended, bundle, stats, gated_ref, grad_ref):
    size = attended.shape[1]
    width = HEADS * size
    for group in range(HEADS):
        head_stats = [stats[head, 4 * group : 4 * group + 4] for head in range(HEADS)]
        mean = sum(one[0:1] for one in head_stats) * (1.0 / HEADS)
        apart = [one[0:1] - mean for one in head_stats]
        spread = sum(one[1:2] + size * off * off for one, off in zip(head_stats, apart))
        inv_scale = lax.rsqrt(spread * (1.0 / width) + 1e-05)
        mean_dy = sum(one[2:3] for one in head_stats) * (1.0 / width)
        mixed = sum(one[3:4] + off * one[2:3] for one, off in zip(head_stats, apart))
        mean_mixed = mixed * inv_scale * (1.0 / width)
        normed = (attended[group] - mean) * inv_scale
        dy = bundle[group, 2 * size : 3 * size].astype(F32)
        gated_ref[group] = (normed * bundle[group, size : 2 * size].astype(F32)).astype(BF16)
        grad_ref[group] = (inv_scale * (dy - mean_dy - normed * mean_mixed)).astype(BF16)


def out_grad_kernel(total_cands, cot_rows, gated, out_grad_ref):
    cots, cots_here = cot_rows
    count = cots.shape[1]
    total = None
    cots_here()
    for group in range(HEADS):
        part = jnp.dot(gated[group, :, :count], cots[group], preferred_element_type=F32)
        total = part if total is None else total + part
    total = (total * (1.0 / math.sqrt(total_cands))).astype(BF16)
    halves, rows_of, lines, columns = out_grad_ref.shape
    for half in range(halves):
        for row in range(rows_of):
            out_grad_ref[half, row] = total[
                row * lines : (row + 1) * lines, half * columns : (half + 1) * columns
            ]


def back(ring, blocks_ref, bundle, grads, sum_ref):
    tall, size = blocks_ref.shape[1], blocks_ref.shape[2] // 2
    scale = 1.0 / math.sqrt(size)
    keys, values = {}, {}
    for group in range(HEADS):
        span = served(ring, group)
        if len(span) == 0:
            continue
        grad = grads[group]
        value_rows, parts = scored(ring, blocks_ref, bundle, group)
        weight_grad = jnp.dot(value_rows, grad, preferred_element_type=F32)
        for place, block in enumerate(span):
            scores, usage = parts[place]
            part = sigmoid(scores)
            weights = scores * part
            slopes = (part + weights * (1.0 - part)) * (usage * scale)
            lines = weight_grad[place * tall : (place + 1) * tall]
            key = lax.dot_general(
                (lines * slopes).astype(BF16), bundle[group, 0:size], NT, preferred_element_type=F32
            )
            value = lax.dot_general(
                (weights * usage).astype(BF16), grad, NT, preferred_element_type=F32
            )
            keys[block] = keys[block] + key if block in keys else key
            values[block] = values[block] + value if block in values else value
    for block in keys:
        sum_ref[block, :, 0:size] = keys[block].astype(sum_ref.dtype)
        sum_ref[block, :, size:] = values[block].astype(sum_ref.dtype)


def back2_kernel(ring2, bundle, grads, sum_ref):
    back(2, ring2, bundle, grads, sum_ref)


def back1_kernel(ring1, bundle, grads, arrived, sum_ref, total):
    back(1, ring1, bundle, grads, total)
    count = arrived.shape[0]
    sum_ref[:count] = (total[:count] + arrived[...].astype(F32)).astype(BF16)
    sum_ref[count:] = total[count:].astype(BF16)


def back0_kernel(ring0, bundle, grads, sum_ref):
    back(0, ring0, bundle, grads, sum_ref)


def fold_kernel(parts, folded_ref):
    total = jnp.sum(parts[...].astype(F32), axis=0).astype(BF16)
    lines = folded_ref.shape[2]
    for row in range(folded_ref.shape[1]):
        for copy in range(folded_ref.shape[0]):
            folded_ref[copy, row] = total[row * lines : (row + 1) * lines]


def pick_kernel(place_ref, parts, spread_ref):
    total = jnp.zeros(spread_ref.shape[1:], F32)
    for source in range(parts.shape[0]):
        total = total + parts[source, place_ref[0]].astype(F32)
    for peer in range(spread_ref.shape[0]):
        spread_ref[peer] = total


def last_kernel(parts, rows_ref):
    cores = parts.shape[1]
    half = rows_ref.shape[1] // cores
    for core in range(cores):
        rows_ref[:, core * half : (core + 1) * half] = jnp.sum(parts[:, core], axis=0)


def parcel_kernel(place_ref, gated_ref, back0, back1, *parcel_refs):
    size = gated_ref.shape[1]
    for step, parcel in enumerate(parcel_refs):
        target = lax.rem(place_ref[0] + step, HEADS)
        parcel[0:size] = gated_ref[target]
        parcel[size:] = (back0[target] + back1[target].astype(F32)).astype(BF16)


def join_kernel(place_ref, cand_ref, out_ref, *refs):
    *parcels, result_ref, grad_ref = refs
    inner, count = out_ref.shape[0], cand_ref.shape[0]
    size = inner // HEADS
    product = None
    for step, parcel in enumerate(parcels):
        head = lax.rem(place_ref[0] + HEADS - step, HEADS)
        rows = pl.ds(pl.multiple_of(head * size, size), size)
        part = lax.dot_general(parcel[0:size, :count], out_ref[rows], TN, preferred_element_type=F32)
        product = part if product is None else product + part
        grad_ref[:, rows] = parcel[size:, 0:size]
        grad_ref[:, pl.ds(pl.multiple_of(inner + head * size, size), size)] = parcel[size:, size:]
    result_ref[...] = (cand_ref[...].astype(F32) + product).astype(BF16)


def moved(block, distance):
    size = lax.axis_size(DEPTH)
    return lax.ppermute(block, DEPTH, [((i + distance) % size, i) for i in range(size)])


def exchanged(chunks, axis):
    return lax.all_to_all(chunks, axis, 0, 0, tiled=True)


def spread_over(block, axis):
    size = lax.axis_size(axis)
    return exchanged(jnp.broadcast_to(block[None], (size,) + block.shape), axis)


def summed(parts):
    return jnp.sum(parts.astype(F32), axis=0)


def on_device(
    candidates,
    cotangent,
    history,
    request_blocks,
    request_length,
    candidate_request,
    in_weight,
    out_weight,
):
    tall, wide = history.shape
    inner = wide // 2
    size = inner // HEADS
    count = candidates.shape[0]
    lanes = 2 * size
    total_cands = count * lax.axis_size(ALL)
    barrier = lax.optimization_barrier
    place = lax.axis_index("x").reshape(1).astype(jnp.int32)

    cots = lax.all_gather(cotangent, "x")
    ring_shape = shaped((HEADS, tall, 2 * size), BF16)
    by_head = pl.pallas_call(
        split_kernel,
        out_shape=ring_shape,
        in_specs=[pl.BlockSpec(memory_space=pl.ANY)],
        out_specs=pl.BlockSpec(memory_space=pltpu.VMEM),
        scratch_shapes=[pltpu.SemaphoreType.DMA((HEADS, 2))],
        compiler_params=pltpu.CompilerParams(vmem_limit_bytes=56 * 1024 * 1024),
    )(history)
    ring0 = exchanged(by_head, "x")

    ring2 = moved(ring0[: HEADS - 1], 2)
    ring1 = moved(ring0, 1)
    bundle = on_fetched(
        prepare_kernel,
        shaped((HEADS, 3 * size + 16, lanes), BF16),
        candidate_request.reshape(1, count),
        candidates,
        cotangent,
        in_weight,
        out_weight,
        scalars=(request_blocks, request_length),
    )
    bundle = exchanged(bundle, "x")

    attended_shape = shaped((HEADS, size, lanes), F32)
    before = on_core(early_kernel, attended_shape, ring0, ring1, bundle)
    attended, stats = on_core(
        late_kernel, (attended_shape, shaped((4 * HEADS, lanes), F32)), ring2, bundle, before
    )
    stats = spread_over(stats, "x")
    head_shape = shaped((HEADS, size, lanes), BF16)
    cores, zh, zl, xs = (lax.axis_size(name) for name in ("core", "zh", "zl", "x"))
    own, half = size // (zl * xs), out_weight.shape[1] // cores
    gated, grads = on_core(norm_kernel, (head_shape, head_shape), attended, bundle, stats)
    back2 = on_core(back2_kernel, shaped(ring2.shape, BF16), ring2, bundle, grads)
    gated, back2 = barrier((gated, back2))
    back2 = moved(back2, -1)
    out_grad = on_fetched(
        lambda *refs: out_grad_kernel(total_cands, *refs),
        shaped((cores, zl, size // zl, half), BF16),
        cots,
        local=(gated,),
    )
    out_grad, late_grads = barrier((out_grad, grads))
    part = exchanged(out_grad.reshape(cores * zl, size // zl, half), ("core", "zl"))
    back1 = pl.pallas_call(
        back1_kernel,
        out_shape=shaped(ring1.shape, BF16),
        in_specs=[pl.BlockSpec(memory_space=pltpu.VMEM)] * 4,
        out_specs=pl.BlockSpec(memory_space=pltpu.VMEM),
        scratch_shapes=[pltpu.VMEM(ring1.shape, F32)],
        compiler_params=pltpu.CompilerParams(vmem_limit_bytes=12 * 1024 * 1024),
    )(ring1, bundle, late_grads, back2)
    part, back1 = barrier((part, moved(back1, -1)))
    part, back1 = barrier((on_core(fold_kernel, shaped((zh, xs, own, half), BF16), part), back1))
    back0 = on_core(back0_kernel, shaped(ring0.shape, F32), ring0, bundle, late_grads)
    part = exchanged(part.reshape(zh * xs, own, half), ("zh", "x")).reshape(zh, xs, own, half)
    depth = lax.axis_index("zh").reshape(1).astype(jnp.int32)
    peers = lax.axis_size("y") * cores
    part = on_core(pick_kernel, shaped((peers, own, half), F32), part, scalars=(depth,))

    parcels = on_core(
        parcel_kernel, [shaped((2 * size, lanes), BF16)] * HEADS, gated, back0, back1, scalars=(place,)
    )
    arrived = [
        lax.ppermute(parcel, "x", [(i, (i + step) % HEADS) for i in range(HEADS)]) if step else parcel
        for step, parcel in enumerate(parcels)
    ]
    part = exchanged(part, ("y", "core")).reshape(-1, cores, own, half)
    grad_rows = on_core(last_kernel, shaped((own, cores * half), F32), part)

    layer_out, grad_history = on_core(
        join_kernel,
        (shaped(candidates.shape, BF16), shaped(history.shape, BF16)),
        candidates,
        out_weight,
        *arrived,
        scalars=(place,),
    )
    return (layer_out, grad_rows, grad_history)


def solution(mesh):
    inner = Mesh(mesh.devices.reshape(4, 2, 4, 4, 4), ALL)
    rows = P(ALL)
    return jax.shard_map(
        on_device,
        mesh=inner,
        in_specs=(rows, rows, rows, rows, rows, rows, P(), P()),
        out_specs=(rows, P(("zh", "zl", "x")), rows),
        check_vma=False,
    )
```

```python
import math

import jax
import jax.numpy as jnp
from jax import lax
from jax.experimental import pallas as pl
from jax.experimental.pallas import tpu as pltpu
from jax.sharding import Mesh, PartitionSpec as P

HEADS = 4
SPAN = 8
BF16 = jnp.bfloat16
F32 = jnp.float32
ALL = ("y", "core", "zh", "zl", "x")
DEPTH = ("zh", "zl")
NT = (((1,), (1,)), ((), ()))
TN = (((0,), (0,)), ((), ()))


def on_core(kernel, outs, *operands, scalars=()):
    spaces = [pltpu.SMEM] * len(scalars) + [pltpu.VMEM] * len(operands)
    return pl.pallas_call(
        kernel,
        out_shape=outs,
        in_specs=[pl.BlockSpec(memory_space=space) for space in spaces],
        out_specs=jax.tree.map(lambda _: pl.BlockSpec(memory_space=pltpu.VMEM), outs),
        compiler_params=pltpu.CompilerParams(vmem_limit_bytes=12 * 1024 * 1024),
    )(*scalars, *operands)


def on_fetched(kernel, outs, *operands, scalars=(), local=()):
    fetched = list(scalars) + list(operands)
    many = len(fetched)
    first = many + len(local) + len(jax.tree.leaves(outs))
    pieces = [4 if one.size >= 1 << 19 else 1 for one in fetched]

    def body(*refs):
        places, arrivals = refs[first : first + many], refs[first + many]
        waits = []
        for i, (source, place) in enumerate(zip(refs[:many], places)):
            step = place.shape[0] // pieces[i]
            copies = []
            for part in range(pieces[i]):
                rows = (slice(None),) if pieces[i] == 1 else (pl.ds(part * step, step),)
                copy = pltpu.make_async_copy(source.at[rows], place.at[rows], arrivals.at[i, part])
                copy.start()
                copies.append(copy)
            waits.append(lambda copies=copies: [copy.wait() for copy in copies])
        kernel(*zip(places, waits), *refs[many:first])

    return pl.pallas_call(
        body,
        out_shape=outs,
        in_specs=[pl.BlockSpec(memory_space=pl.ANY)] * many
        + [pl.BlockSpec(memory_space=pltpu.VMEM)] * len(local),
        out_specs=jax.tree.map(lambda _: pl.BlockSpec(memory_space=pltpu.VMEM), outs),
        scratch_shapes=[pltpu.SMEM(one.shape, one.dtype) for one in scalars]
        + [pltpu.VMEM(one.shape, one.dtype) for one in operands]
        + [pltpu.SemaphoreType.DMA((many, 4))],
        compiler_params=pltpu.CompilerParams(vmem_limit_bytes=56 * 1024 * 1024),
    )(*fetched, *local)


def shaped(shape, kind):
    return jax.ShapeDtypeStruct(shape, kind)


def sigmoid(values):
    return 0.5 + 0.5 * jnp.tanh(0.5 * values)


def served(ring, group):
    return {0: range(group, HEADS), 1: range(0, HEADS), 2: range(0, group)}[ring]


def split_kernel(history_ref, chunks_ref, arrivals):
    heads, _, both = chunks_ref.shape
    size = both // 2
    copies = []
    for head in range(heads):
        for kind in range(2):
            columns = pl.ds((kind * heads + head) * size, size)
            copies.append(
                pltpu.make_async_copy(
                    history_ref.at[:, columns],
                    chunks_ref.at[head, :, pl.ds(kind * size, size)],
                    arrivals.at[head, kind],
                )
            )
    for copy in copies:
        copy.start()
    for copy in copies:
        copy.wait()


def used_blocks(blocks_ref, length_ref, owner_ref):
    requests, width = blocks_ref.shape
    owners = owner_ref[...]
    positions = lax.broadcasted_iota(jnp.int32, (16, owners.shape[1]), 0)
    usage = jnp.zeros(positions.shape, F32)
    for request in range(requests):
        used = jnp.zeros(positions.shape, F32)
        for entry in range(width):
            block = jnp.where(entry < length_ref[request], blocks_ref[request, entry], -1)
            used = used + jnp.where(positions == block, 1.0, 0.0)
        usage = usage + jnp.where(owners == request, used, 0.0)
    return usage


def prepare_kernel(blocks, lengths, owners, cands, cots, in_weight, out_weight, bundle_ref):
    (cand_ref, cand_here), (cot_ref, cot_here) = cands, cots
    (in_ref, in_here), (out_ref, out_here) = in_weight, out_weight
    inner, count = out_ref.shape[0], cand_ref.shape[0]
    size = inner // HEADS
    bundle_ref[:, :, count:] = jnp.zeros(
        (HEADS, bundle_ref.shape[1], bundle_ref.shape[2] - count), BF16
    )
    for _, here in (blocks, lengths, owners):
        here()
    usage = used_blocks(blocks[0], lengths[0], owners[0]).astype(BF16)
    cand_here()
    rows = cand_ref[...].astype(F32)
    centered = rows - jnp.mean(rows, axis=-1, keepdims=True)
    inv_scale = lax.rsqrt(jnp.mean(centered * centered, axis=-1, keepdims=True) + 1e-05)
    normed = (centered * inv_scale).astype(BF16)
    cot_here()
    out_here()
    zed_grad = lax.dot_general(out_ref[...], cot_ref[...], NT, preferred_element_type=F32)
    in_here()
    projected = jnp.dot(normed, in_ref[...], preferred_element_type=F32).T
    for head in range(HEADS):
        part = slice(head * size, (head + 1) * size)
        gate_in = projected[inner + head * size : inner + (head + 1) * size]
        gating = gate_in * sigmoid(gate_in)
        bundle_ref[head, 0:size, :count] = projected[part].astype(BF16)
        bundle_ref[head, size : 2 * size, :count] = gating.astype(BF16)
        bundle_ref[head, 2 * size : 3 * size, :count] = (zed_grad[part] * gating).astype(BF16)
        bundle_ref[head, 3 * size :, :count] = usage


def scored(ring, blocks_ref, bundle_ref, group):
    span = served(ring, group)
    tall, size = blocks_ref.shape[1], blocks_ref.shape[2] // 2
    rows = blocks_ref[span[0] : span[-1] + 1].reshape(len(span) * tall, 2 * size)
    scores = jnp.dot(rows[:, :size], bundle_ref[group, 0:size], preferred_element_type=F32)
    scores = scores * (1.0 / math.sqrt(size))
    usage = bundle_ref[group, 3 * size :].astype(F32)
    parts = []
    for place, block in enumerate(span):
        position = HEADS * ring + block - group
        parts.append((scores[place * tall : (place + 1) * tall], usage[position : position + 1]))
    return rows[:, size:], parts


def attend(ring, blocks_ref, bundle_ref, group):
    values, parts = scored(ring, blocks_ref, bundle_ref, group)
    weights = [(scores * sigmoid(scores) * usage).astype(BF16) for scores, usage in parts]
    return lax.dot_general(
        values, jnp.concatenate(weights, axis=0), TN, preferred_element_type=F32
    )


def early_kernel(ring0, ring1, bundle, attended_ref):
    for group in range(HEADS):
        attended_ref[group] = attend(0, ring0, bundle, group) + attend(1, ring1, bundle, group)


def late_kernel(ring2, bundle, before, attended_ref, stats_ref):
    size = before.shape[1]
    for group in range(HEADS):
        attended = before[group]
        if len(served(2, group)) > 0:
            attended = attended + attend(2, ring2, bundle, group)
        attended_ref[group] = attended
        dy = bundle[group, 2 * size : 3 * size].astype(F32)
        mean = jnp.mean(attended, axis=0, keepdims=True)
        centered = attended - mean
        stats_ref[4 * group : 4 * group + 1] = mean
        stats_ref[4 * group + 1 : 4 * group + 2] = jnp.sum(centered * centered, axis=0, keepdims=True)
        stats_ref[4 * group + 2 : 4 * group + 3] = jnp.sum(dy, axis=0, keepdims=True)
        stats_ref[4 * group + 3 : 4 * group + 4] = jnp.sum(dy * centered, axis=0, keepdims=True)


def norm_kernel(attended, bundle, stats, gated_ref, grad_ref):
    size = attended.shape[1]
    width = HEADS * size
    for group in range(HEADS):
        head_stats = [stats[head, 4 * group : 4 * group + 4] for head in range(HEADS)]
        mean = sum(one[0:1] for one in head_stats) * (1.0 / HEADS)
        apart = [one[0:1] - mean for one in head_stats]
        spread = sum(one[1:2] + size * off * off for one, off in zip(head_stats, apart))
        inv_scale = lax.rsqrt(spread * (1.0 / width) + 1e-05)
        mean_dy = sum(one[2:3] for one in head_stats) * (1.0 / width)
        mixed = sum(one[3:4] + off * one[2:3] for one, off in zip(head_stats, apart))
        mean_mixed = mixed * inv_scale * (1.0 / width)
        normed = (attended[group] - mean) * inv_scale
        dy = bundle[group, 2 * size : 3 * size].astype(F32)
        gated_ref[group] = (normed * bundle[group, size : 2 * size].astype(F32)).astype(BF16)
        grad_ref[group] = (inv_scale * (dy - mean_dy - normed * mean_mixed)).astype(BF16)


def out_grad_kernel(total_cands, cot_rows, gated, out_grad_ref):
    cots, cots_here = cot_rows
    count = cots.shape[1]
    total = None
    cots_here()
    for group in range(HEADS):
        part = jnp.dot(gated[group, :, :count], cots[group], preferred_element_type=F32)
        total = part if total is None else total + part
    total = (total * (1.0 / math.sqrt(total_cands))).astype(BF16)
    halves, rows_of, lines, columns = out_grad_ref.shape
    for half in range(halves):
        for row in range(rows_of):
            out_grad_ref[half, row] = total[
                row * lines : (row + 1) * lines, half * columns : (half + 1) * columns
            ]


def back(ring, blocks_ref, bundle, grads, sum_ref):
    tall, size = blocks_ref.shape[1], blocks_ref.shape[2] // 2
    scale = 1.0 / math.sqrt(size)
    keys, values = {}, {}
    for group in range(HEADS):
        span = served(ring, group)
        if len(span) == 0:
            continue
        grad = grads[group]
        value_rows, parts = scored(ring, blocks_ref, bundle, group)
        weight_grad = jnp.dot(value_rows, grad, preferred_element_type=F32)
        for place, block in enumerate(span):
            scores, usage = parts[place]
            part = sigmoid(scores)
            weights = scores * part
            slopes = (part + weights * (1.0 - part)) * (usage * scale)
            lines = weight_grad[place * tall : (place + 1) * tall]
            key = lax.dot_general(
                (lines * slopes).astype(BF16), bundle[group, 0:size], NT, preferred_element_type=F32
            )
            value = lax.dot_general(
                (weights * usage).astype(BF16), grad, NT, preferred_element_type=F32
            )
            keys[block] = keys[block] + key if block in keys else key
            values[block] = values[block] + value if block in values else value
    for block in keys:
        sum_ref[block, :, 0:size] = keys[block].astype(sum_ref.dtype)
        sum_ref[block, :, size:] = values[block].astype(sum_ref.dtype)


def back2_kernel(ring2, bundle, grads, sum_ref):
    back(2, ring2, bundle, grads, sum_ref)


def back1_kernel(ring1, bundle, grads, arrived, sum_ref, total):
    back(1, ring1, bundle, grads, total)
    count = arrived.shape[0]
    sum_ref[:count] = (total[:count] + arrived[...].astype(F32)).astype(BF16)
    sum_ref[count:] = total[count:].astype(BF16)


def back0_kernel(ring0, bundle, grads, sum_ref):
    back(0, ring0, bundle, grads, sum_ref)


def fold_kernel(parts, folded_ref):
    total = jnp.sum(parts[...].astype(F32), axis=0).astype(BF16)
    lines = folded_ref.shape[2]
    for row in range(folded_ref.shape[1]):
        for copy in range(folded_ref.shape[0]):
            folded_ref[copy, row] = total[row * lines : (row + 1) * lines]


def pick_kernel(place_ref, parts, spread_ref):
    total = jnp.zeros(spread_ref.shape[1:], F32)
    for source in range(parts.shape[0]):
        total = total + parts[source, place_ref[0]].astype(F32)
    for peer in range(spread_ref.shape[0]):
        spread_ref[peer] = total


def last_kernel(parts, rows_ref):
    cores = parts.shape[1]
    half = rows_ref.shape[1] // cores
    for core in range(cores):
        rows_ref[:, core * half : (core + 1) * half] = jnp.sum(parts[:, core], axis=0)


def parcel_kernel(place_ref, gated_ref, back0, back1, *parcel_refs):
    size = gated_ref.shape[1]
    for step, parcel in enumerate(parcel_refs):
        target = lax.rem(place_ref[0] + step, HEADS)
        parcel[0:size] = gated_ref[target]
        parcel[size:] = (back0[target] + back1[target].astype(F32)).astype(BF16)


def join_kernel(place_ref, cand_ref, out_ref, *refs):
    *parcels, result_ref, grad_ref = refs
    inner, count = out_ref.shape[0], cand_ref.shape[0]
    size = inner // HEADS
    product = None
    for step, parcel in enumerate(parcels):
        head = lax.rem(place_ref[0] + HEADS - step, HEADS)
        rows = pl.ds(pl.multiple_of(head * size, size), size)
        part = lax.dot_general(parcel[0:size, :count], out_ref[rows], TN, preferred_element_type=F32)
        product = part if product is None else product + part
        grad_ref[:, rows] = parcel[size:, 0:size]
        grad_ref[:, pl.ds(pl.multiple_of(inner + head * size, size), size)] = parcel[size:, size:]
    result_ref[...] = (cand_ref[...].astype(F32) + product).astype(BF16)


def moved(block, distance):
    size = lax.axis_size(DEPTH)
    return lax.ppermute(block, DEPTH, [((i + distance) % size, i) for i in range(size)])


def exchanged(chunks, axis):
    return lax.all_to_all(chunks, axis, 0, 0, tiled=True)


def spread_over(block, axis):
    size = lax.axis_size(axis)
    return exchanged(jnp.broadcast_to(block[None], (size,) + block.shape), axis)


def summed(parts):
    return jnp.sum(parts.astype(F32), axis=0)


def on_device(
    candidates,
    cotangent,
    history,
    request_blocks,
    request_length,
    candidate_request,
    in_weight,
    out_weight,
):
    tall, wide = history.shape
    inner = wide // 2
    size = inner // HEADS
    count = candidates.shape[0]
    lanes = 2 * size
    total_cands = count * lax.axis_size(ALL)
    barrier = lax.optimization_barrier
    place = lax.axis_index("x").reshape(1).astype(jnp.int32)

    cots = lax.all_gather(cotangent, "x")
    ring_shape = shaped((HEADS, tall, 2 * size), BF16)
    by_head = pl.pallas_call(
        split_kernel,
        out_shape=ring_shape,
        in_specs=[pl.BlockSpec(memory_space=pl.ANY)],
        out_specs=pl.BlockSpec(memory_space=pltpu.VMEM),
        scratch_shapes=[pltpu.SemaphoreType.DMA((HEADS, 2))],
        compiler_params=pltpu.CompilerParams(vmem_limit_bytes=56 * 1024 * 1024),
    )(history)
    ring0 = exchanged(by_head, "x")

    ring2 = moved(ring0[: HEADS - 1], 2)
    ring1 = moved(ring0, 1)
    bundle = on_fetched(
        prepare_kernel,
        shaped((HEADS, 3 * size + 16, lanes), BF16),
        candidate_request.reshape(1, count),
        candidates,
        cotangent,
        in_weight,
        out_weight,
        scalars=(request_blocks, request_length),
    )
    bundle = exchanged(bundle, "x")

    attended_shape = shaped((HEADS, size, lanes), F32)
    before = on_core(early_kernel, attended_shape, ring0, ring1, bundle)
    attended, stats = on_core(
        late_kernel, (attended_shape, shaped((4 * HEADS, lanes), F32)), ring2, bundle, before
    )
    stats = spread_over(stats, "x")
    head_shape = shaped((HEADS, size, lanes), BF16)
    cores, zh, zl, xs = (lax.axis_size(name) for name in ("core", "zh", "zl", "x"))
    own, half = size // (zl * xs), out_weight.shape[1] // cores
    gated, grads = on_core(norm_kernel, (head_shape, head_shape), attended, bundle, stats)
    back2 = on_core(back2_kernel, shaped(ring2.shape, BF16), ring2, bundle, grads)
    gated, back2 = barrier((gated, back2))
    back2 = moved(back2, -1)
    out_grad = on_fetched(
        lambda *refs: out_grad_kernel(total_cands, *refs),
        shaped((cores, zl, size // zl, half), BF16),
        cots,
        local=(gated,),
    )
    out_grad, back2, late_grads = barrier((out_grad, back2, grads))
    part = exchanged(out_grad.reshape(cores * zl, size // zl, half), ("core", "zl"))
    back1 = pl.pallas_call(
        back1_kernel,
        out_shape=shaped(ring1.shape, BF16),
        in_specs=[pl.BlockSpec(memory_space=pltpu.VMEM)] * 4,
        out_specs=pl.BlockSpec(memory_space=pltpu.VMEM),
        scratch_shapes=[pltpu.VMEM(ring1.shape, F32)],
        compiler_params=pltpu.CompilerParams(vmem_limit_bytes=12 * 1024 * 1024),
    )(ring1, bundle, late_grads, back2)
    back0 = on_core(back0_kernel, shaped(ring0.shape, F32), ring0, bundle, late_grads)
    part, back0, back1 = barrier((part, back0, moved(back1, -1)))
    part = on_core(fold_kernel, shaped((zh, xs, own, half), BF16), part)
    part, back0, back1 = barrier((part, back0, back1))
    part = exchanged(part.reshape(zh * xs, own, half), ("zh", "x")).reshape(zh, xs, own, half)
    depth = lax.axis_index("zh").reshape(1).astype(jnp.int32)
    peers = lax.axis_size("y") * cores
    part = on_core(pick_kernel, shaped((peers, own, half), F32), part, scalars=(depth,))

    parcels = on_core(
        parcel_kernel, [shaped((2 * size, lanes), BF16)] * HEADS, gated, back0, back1, scalars=(place,)
    )
    arrived = [
        lax.ppermute(parcel, "x", [(i, (i + step) % HEADS) for i in range(HEADS)]) if step else parcel
        for step, parcel in enumerate(parcels)
    ]
    part = exchanged(part, ("y", "core")).reshape(-1, cores, own, half)
    grad_rows = on_core(last_kernel, shaped((own, cores * half), F32), part)

    layer_out, grad_history = on_core(
        join_kernel,
        (shaped(candidates.shape, BF16), shaped(history.shape, BF16)),
        candidates,
        out_weight,
        *arrived,
        scalars=(place,),
    )
    return (layer_out, grad_rows, grad_history)


def solution(mesh):
    inner = Mesh(mesh.devices.reshape(4, 2, 4, 4, 4), ALL)
    rows = P(ALL)
    return jax.shard_map(
        on_device,
        mesh=inner,
        in_specs=(rows, rows, rows, rows, rows, rows, P(), P()),
        out_specs=(rows, P(("zh", "zl", "x")), rows),
        check_vma=False,
    )
```

```python
import math

import jax
import jax.numpy as jnp
from jax import lax
from jax.experimental import pallas as pl
from jax.experimental.pallas import tpu as pltpu
from jax.sharding import Mesh, PartitionSpec as P

HEADS = 4
SPAN = 8
BF16 = jnp.bfloat16
F32 = jnp.float32
ALL = ("y", "core", "zh", "zl", "x")
DEPTH = ("zh", "zl")
NT = (((1,), (1,)), ((), ()))
TN = (((0,), (0,)), ((), ()))


def on_core(kernel, outs, *operands, scalars=()):
    spaces = [pltpu.SMEM] * len(scalars) + [pltpu.VMEM] * len(operands)
    return pl.pallas_call(
        kernel,
        out_shape=outs,
        in_specs=[pl.BlockSpec(memory_space=space) for space in spaces],
        out_specs=jax.tree.map(lambda _: pl.BlockSpec(memory_space=pltpu.VMEM), outs),
        compiler_params=pltpu.CompilerParams(vmem_limit_bytes=12 * 1024 * 1024),
    )(*scalars, *operands)


def on_fetched(kernel, outs, *operands, scalars=()):
    fetched = list(scalars) + list(operands)
    many = len(fetched)
    first = many + len(jax.tree.leaves(outs))
    pieces = [4 if one.size >= 1 << 19 else 1 for one in fetched]

    def body(*refs):
        places, arrivals = refs[first : first + many], refs[first + many]
        waits = []
        for i, (source, place) in enumerate(zip(refs[:many], places)):
            step = place.shape[0] // pieces[i]
            copies = []
            for part in range(pieces[i]):
                rows = (slice(None),) if pieces[i] == 1 else (pl.ds(part * step, step),)
                copy = pltpu.make_async_copy(source.at[rows], place.at[rows], arrivals.at[i, part])
                copy.start()
                copies.append(copy)
            waits.append(lambda copies=copies: [copy.wait() for copy in copies])
        kernel(*zip(places, waits), *refs[many:first])

    return pl.pallas_call(
        body,
        out_shape=outs,
        in_specs=[pl.BlockSpec(memory_space=pl.ANY)] * many,
        out_specs=jax.tree.map(lambda _: pl.BlockSpec(memory_space=pltpu.VMEM), outs),
        scratch_shapes=[pltpu.SMEM(one.shape, one.dtype) for one in scalars]
        + [pltpu.VMEM(one.shape, one.dtype) for one in operands]
        + [pltpu.SemaphoreType.DMA((many, 4))],
        compiler_params=pltpu.CompilerParams(vmem_limit_bytes=56 * 1024 * 1024),
    )(*fetched)


def shaped(shape, kind):
    return jax.ShapeDtypeStruct(shape, kind)


def sigmoid(values):
    return 0.5 + 0.5 * jnp.tanh(0.5 * values)


def served(ring, group):
    return {0: range(group, HEADS), 1: range(0, HEADS), 2: range(0, group)}[ring]


def split_kernel(history_ref, chunks_ref, arrivals):
    heads, _, both = chunks_ref.shape
    size = both // 2
    copies = []
    for head in range(heads):
        for kind in range(2):
            columns = pl.ds((kind * heads + head) * size, size)
            copies.append(
                pltpu.make_async_copy(
                    history_ref.at[:, columns],
                    chunks_ref.at[head, :, pl.ds(kind * size, size)],
                    arrivals.at[head, kind],
                )
            )
    for copy in copies:
        copy.start()
    for copy in copies:
        copy.wait()


def used_blocks(blocks_ref, length_ref, owner_ref):
    requests, width = blocks_ref.shape
    owners = owner_ref[...]
    positions = lax.broadcasted_iota(jnp.int32, (16, owners.shape[1]), 0)
    usage = jnp.zeros(positions.shape, F32)
    for request in range(requests):
        used = jnp.zeros(positions.shape, F32)
        for entry in range(width):
            block = jnp.where(entry < length_ref[request], blocks_ref[request, entry], -1)
            used = used + jnp.where(positions == block, 1.0, 0.0)
        usage = usage + jnp.where(owners == request, used, 0.0)
    return usage


def prepare_kernel(blocks, lengths, owners, cands, cots, in_weight, out_weight, bundle_ref):
    (cand_ref, cand_here), (cot_ref, cot_here) = cands, cots
    (in_ref, in_here), (out_ref, out_here) = in_weight, out_weight
    inner, count = out_ref.shape[0], cand_ref.shape[0]
    size = inner // HEADS
    bundle_ref[:, :, count:] = jnp.zeros(
        (HEADS, bundle_ref.shape[1], bundle_ref.shape[2] - count), BF16
    )
    for _, here in (blocks, lengths, owners):
        here()
    usage = used_blocks(blocks[0], lengths[0], owners[0]).astype(BF16)
    cand_here()
    rows = cand_ref[...].astype(F32)
    centered = rows - jnp.mean(rows, axis=-1, keepdims=True)
    inv_scale = lax.rsqrt(jnp.mean(centered * centered, axis=-1, keepdims=True) + 1e-05)
    normed = (centered * inv_scale).astype(BF16)
    cot_here()
    out_here()
    zed_grad = lax.dot_general(out_ref[...], cot_ref[...], NT, preferred_element_type=F32)
    in_here()
    projected = jnp.dot(normed, in_ref[...], preferred_element_type=F32).T
    for head in range(HEADS):
        part = slice(head * size, (head + 1) * size)
        gate_in = projected[inner + head * size : inner + (head + 1) * size]
        gating = gate_in * sigmoid(gate_in)
        bundle_ref[head, 0:size, :count] = projected[part].astype(BF16)
        bundle_ref[head, size : 2 * size, :count] = gating.astype(BF16)
        bundle_ref[head, 2 * size : 3 * size, :count] = (zed_grad[part] * gating).astype(BF16)
        bundle_ref[head, 3 * size :, :count] = usage


def scored(ring, blocks_ref, bundle_ref, group):
    span = served(ring, group)
    tall, size = blocks_ref.shape[1], blocks_ref.shape[2] // 2
    rows = blocks_ref[span[0] : span[-1] + 1].reshape(len(span) * tall, 2 * size)
    scores = jnp.dot(rows[:, :size], bundle_ref[group, 0:size], preferred_element_type=F32)
    scores = scores * (1.0 / math.sqrt(size))
    usage = bundle_ref[group, 3 * size :].astype(F32)
    parts = []
    for place, block in enumerate(span):
        position = HEADS * ring + block - group
        parts.append((scores[place * tall : (place + 1) * tall], usage[position : position + 1]))
    return rows[:, size:], parts


def attend(ring, blocks_ref, bundle_ref, group):
    values, parts = scored(ring, blocks_ref, bundle_ref, group)
    weights = [(scores * sigmoid(scores) * usage).astype(BF16) for scores, usage in parts]
    return lax.dot_general(
        values, jnp.concatenate(weights, axis=0), TN, preferred_element_type=F32
    )


def early_kernel(ring0, ring1, bundle, attended_ref):
    for group in range(HEADS):
        attended_ref[group] = attend(0, ring0, bundle, group) + attend(1, ring1, bundle, group)


def late_kernel(ring2, bundle, before, attended_ref, stats_ref):
    size = before.shape[1]
    for group in range(HEADS):
        attended = before[group]
        if len(served(2, group)) > 0:
            attended = attended + attend(2, ring2, bundle, group)
        attended_ref[group] = attended
        dy = bundle[group, 2 * size : 3 * size].astype(F32)
        mean = jnp.mean(attended, axis=0, keepdims=True)
        centered = attended - mean
        stats_ref[4 * group : 4 * group + 1] = mean
        stats_ref[4 * group + 1 : 4 * group + 2] = jnp.sum(centered * centered, axis=0, keepdims=True)
        stats_ref[4 * group + 2 : 4 * group + 3] = jnp.sum(dy, axis=0, keepdims=True)
        stats_ref[4 * group + 3 : 4 * group + 4] = jnp.sum(dy * centered, axis=0, keepdims=True)


def norm_kernel(attended, bundle, stats, gated_ref, grad_ref):
    size = attended.shape[1]
    width = HEADS * size
    for group in range(HEADS):
        head_stats = [stats[head, 4 * group : 4 * group + 4] for head in range(HEADS)]
        mean = sum(one[0:1] for one in head_stats) * (1.0 / HEADS)
        apart = [one[0:1] - mean for one in head_stats]
        spread = sum(one[1:2] + size * off * off for one, off in zip(head_stats, apart))
        inv_scale = lax.rsqrt(spread * (1.0 / width) + 1e-05)
        mean_dy = sum(one[2:3] for one in head_stats) * (1.0 / width)
        mixed = sum(one[3:4] + off * one[2:3] for one, off in zip(head_stats, apart))
        mean_mixed = mixed * inv_scale * (1.0 / width)
        normed = (attended[group] - mean) * inv_scale
        dy = bundle[group, 2 * size : 3 * size].astype(F32)
        gated_ref[group] = (normed * bundle[group, size : 2 * size].astype(F32)).astype(BF16)
        grad_ref[group] = (inv_scale * (dy - mean_dy - normed * mean_mixed)).astype(BF16)


def out_grad_kernel(total_cands, cots, gated, out_grad_ref):
    count = cots.shape[1]
    total = None
    for group in range(HEADS):
        part = jnp.dot(gated[group, :, :count], cots[group], preferred_element_type=F32)
        total = part if total is None else total + part
    total = (total * (1.0 / math.sqrt(total_cands))).astype(BF16)
    halves, rows_of, lines, columns = out_grad_ref.shape
    for half in range(halves):
        for row in range(rows_of):
            out_grad_ref[half, row] = total[
                row * lines : (row + 1) * lines, half * columns : (half + 1) * columns
            ]


def back(ring, blocks_ref, bundle, grads, sum_ref):
    tall, size = blocks_ref.shape[1], blocks_ref.shape[2] // 2
    scale = 1.0 / math.sqrt(size)
    keys, values = {}, {}
    for group in range(HEADS):
        span = served(ring, group)
        if len(span) == 0:
            continue
        grad = grads[group]
        value_rows, parts = scored(ring, blocks_ref, bundle, group)
        weight_grad = jnp.dot(value_rows, grad, preferred_element_type=F32)
        for place, block in enumerate(span):
            scores, usage = parts[place]
            part = sigmoid(scores)
            weights = scores * part
            slopes = (part + weights * (1.0 - part)) * (usage * scale)
            lines = weight_grad[place * tall : (place + 1) * tall]
            key = lax.dot_general(
                (lines * slopes).astype(BF16), bundle[group, 0:size], NT, preferred_element_type=F32
            )
            value = lax.dot_general(
                (weights * usage).astype(BF16), grad, NT, preferred_element_type=F32
            )
            keys[block] = keys[block] + key if block in keys else key
            values[block] = values[block] + value if block in values else value
    for block in keys:
        sum_ref[block, :, 0:size] = keys[block].astype(sum_ref.dtype)
        sum_ref[block, :, size:] = values[block].astype(sum_ref.dtype)


def back2_kernel(ring2, bundle, grads, sum_ref):
    back(2, ring2, bundle, grads, sum_ref)


def back1_kernel(ring1, bundle, grads, sum_ref):
    back(1, ring1, bundle, grads, sum_ref)


def add_kernel(own, arrived, sum_ref):
    count = arrived.shape[0]
    sum_ref[:count] = (own[:count] + arrived[...].astype(F32)).astype(BF16)
    sum_ref[count:] = own[count:].astype(BF16)


def back0_kernel(ring0, bundle, grads, sum_ref):
    back(0, ring0, bundle, grads, sum_ref)


def fold_kernel(parts, folded_ref):
    total = jnp.sum(parts[...].astype(F32), axis=0).astype(BF16)
    lines = folded_ref.shape[2]
    for row in range(folded_ref.shape[1]):
        for copy in range(folded_ref.shape[0]):
            folded_ref[copy, row] = total[row * lines : (row + 1) * lines]


def pick_kernel(place_ref, parts, spread_ref):
    total = jnp.zeros(spread_ref.shape[1:], F32)
    for source in range(parts.shape[0]):
        total = total + parts[source, place_ref[0]].astype(F32)
    for peer in range(spread_ref.shape[0]):
        spread_ref[peer] = total


def last_kernel(parts, rows_ref):
    cores = parts.shape[1]
    half = rows_ref.shape[1] // cores
    for core in range(cores):
        rows_ref[:, core * half : (core + 1) * half] = jnp.sum(parts[:, core], axis=0)


def parcel_kernel(place_ref, gated_ref, back0, back1, *parcel_refs):
    size = gated_ref.shape[1]
    for step, parcel in enumerate(parcel_refs):
        target = lax.rem(place_ref[0] + step, HEADS)
        parcel[0:size] = gated_ref[target]
        parcel[size:] = (back0[target] + back1[target].astype(F32)).astype(BF16)


def join_kernel(place_ref, cand_ref, out_ref, *refs):
    *parcels, result_ref, grad_ref = refs
    inner, count = out_ref.shape[0], cand_ref.shape[0]
    size = inner // HEADS
    product = None
    for step, parcel in enumerate(parcels):
        head = lax.rem(place_ref[0] + HEADS - step, HEADS)
        rows = pl.ds(pl.multiple_of(head * size, size), size)
        part = lax.dot_general(parcel[0:size, :count], out_ref[rows], TN, preferred_element_type=F32)
        product = part if product is None else product + part
        grad_ref[:, rows] = parcel[size:, 0:size]
        grad_ref[:, pl.ds(pl.multiple_of(inner + head * size, size), size)] = parcel[size:, size:]
    result_ref[...] = (cand_ref[...].astype(F32) + product).astype(BF16)


def moved(block, distance):
    size = lax.axis_size(DEPTH)
    return lax.ppermute(block, DEPTH, [((i + distance) % size, i) for i in range(size)])


def exchanged(chunks, axis):
    return lax.all_to_all(chunks, axis, 0, 0, tiled=True)


def spread_over(block, axis):
    size = lax.axis_size(axis)
    return exchanged(jnp.broadcast_to(block[None], (size,) + block.shape), axis)


def summed(parts):
    return jnp.sum(parts.astype(F32), axis=0)


def on_device(
    candidates,
    cotangent,
    history,
    request_blocks,
    request_length,
    candidate_request,
    in_weight,
    out_weight,
):
    tall, wide = history.shape
    inner = wide // 2
    size = inner // HEADS
    count = candidates.shape[0]
    lanes = 2 * size
    total_cands = count * lax.axis_size(ALL)
    barrier = lax.optimization_barrier
    place = lax.axis_index("x").reshape(1).astype(jnp.int32)

    cots = lax.all_gather(cotangent, "x")
    ring_shape = shaped((HEADS, tall, 2 * size), BF16)
    by_head = pl.pallas_call(
        split_kernel,
        out_shape=ring_shape,
        in_specs=[pl.BlockSpec(memory_space=pl.ANY)],
        out_specs=pl.BlockSpec(memory_space=pltpu.VMEM),
        scratch_shapes=[pltpu.SemaphoreType.DMA((HEADS, 2))],
        compiler_params=pltpu.CompilerParams(vmem_limit_bytes=56 * 1024 * 1024),
    )(history)
    ring0 = exchanged(by_head, "x")

    ring2 = moved(ring0[: HEADS - 1], 2)
    ring1 = moved(ring0, 1)
    bundle = on_fetched(
        prepare_kernel,
        shaped((HEADS, 3 * size + 16, lanes), BF16),
        candidate_request.reshape(1, count),
        candidates,
        cotangent,
        in_weight,
        out_weight,
        scalars=(request_blocks, request_length),
    )
    bundle = exchanged(bundle, "x")

    attended_shape = shaped((HEADS, size, lanes), F32)
    before = on_core(early_kernel, attended_shape, ring0, ring1, bundle)
    attended, stats = on_core(
        late_kernel, (attended_shape, shaped((4 * HEADS, lanes), F32)), ring2, bundle, before
    )
    stats = spread_over(stats, "x")
    head_shape = shaped((HEADS, size, lanes), BF16)
    cores, zh, zl, xs = (lax.axis_size(name) for name in ("core", "zh", "zl", "x"))
    own, half = size // (zl * xs), out_weight.shape[1] // cores
    gated, grads = on_core(norm_kernel, (head_shape, head_shape), attended, bundle, stats)
    back2 = on_core(back2_kernel, shaped(ring2.shape, BF16), ring2, bundle, grads)
    gated, back2 = barrier((gated, back2))
    back2 = moved(back2, -1)
    out_grad = on_core(
        lambda *refs: out_grad_kernel(total_cands, *refs),
        shaped((cores, zl, size // zl, half), BF16),
        cots,
        gated,
    )
    back1 = on_core(back1_kernel, shaped(ring1.shape, F32), ring1, bundle, grads)
    back1 = on_core(add_kernel, shaped(ring1.shape, BF16), back1, back2)
    out_grad, back1, late_grads = barrier((out_grad, back1, grads))
    part = exchanged(out_grad.reshape(cores * zl, size // zl, half), ("core", "zl"))
    back0 = on_core(back0_kernel, shaped(ring0.shape, F32), ring0, bundle, late_grads)
    part, back0, back1 = barrier((part, back0, moved(back1, -1)))
    part = on_core(fold_kernel, shaped((zh, xs, own, half), BF16), part)
    part, back0, back1 = barrier((part, back0, back1))
    part = exchanged(part.reshape(zh * xs, own, half), ("zh", "x")).reshape(zh, xs, own, half)
    depth = lax.axis_index("zh").reshape(1).astype(jnp.int32)
    peers = lax.axis_size("y") * cores
    part = on_core(pick_kernel, shaped((peers, own, half), F32), part, scalars=(depth,))

    parcels = on_core(
        parcel_kernel, [shaped((2 * size, lanes), BF16)] * HEADS, gated, back0, back1, scalars=(place,)
    )
    arrived = [
        lax.ppermute(parcel, "x", [(i, (i + step) % HEADS) for i in range(HEADS)]) if step else parcel
        for step, parcel in enumerate(parcels)
    ]
    part = exchanged(part, ("y", "core")).reshape(-1, cores, own, half)
    grad_rows = on_core(last_kernel, shaped((own, cores * half), F32), part)

    layer_out, grad_history = on_core(
        join_kernel,
        (shaped(candidates.shape, BF16), shaped(history.shape, BF16)),
        candidates,
        out_weight,
        *arrived,
        scalars=(place,),
    )
    return (layer_out, grad_rows, grad_history)


def solution(mesh):
    inner = Mesh(mesh.devices.reshape(4, 2, 4, 4, 4), ALL)
    rows = P(ALL)
    return jax.shard_map(
        on_device,
        mesh=inner,
        in_specs=(rows, rows, rows, rows, rows, rows, P(), P()),
        out_specs=(rows, P(("zh", "zl", "x")), rows),
        check_vma=False,
    )
```

```python
import math

import jax
import jax.numpy as jnp
from jax import lax
from jax.experimental import pallas as pl
from jax.experimental.pallas import tpu as pltpu
from jax.sharding import Mesh, PartitionSpec as P

HEADS = 4
SPAN = 8
BF16 = jnp.bfloat16
F32 = jnp.float32
ALL = ("y", "core", "zh", "zl", "x")
DEPTH = ("zh", "zl")
NT = (((1,), (1,)), ((), ()))
TN = (((0,), (0,)), ((), ()))


def on_core(kernel, outs, *operands, scalars=()):
    spaces = [pltpu.SMEM] * len(scalars) + [pltpu.VMEM] * len(operands)
    return pl.pallas_call(
        kernel,
        out_shape=outs,
        in_specs=[pl.BlockSpec(memory_space=space) for space in spaces],
        out_specs=jax.tree.map(lambda _: pl.BlockSpec(memory_space=pltpu.VMEM), outs),
        compiler_params=pltpu.CompilerParams(vmem_limit_bytes=12 * 1024 * 1024),
    )(*scalars, *operands)


def on_fetched(kernel, outs, *operands, scalars=()):
    fetched = list(scalars) + list(operands)
    many = len(fetched)
    first = many + len(jax.tree.leaves(outs))
    pieces = [4 if one.size >= 1 << 19 else 1 for one in fetched]

    def body(*refs):
        places, arrivals = refs[first : first + many], refs[first + many]
        waits = []
        for i, (source, place) in enumerate(zip(refs[:many], places)):
            step = place.shape[0] // pieces[i]
            copies = []
            for part in range(pieces[i]):
                rows = (slice(None),) if pieces[i] == 1 else (pl.ds(part * step, step),)
                copy = pltpu.make_async_copy(source.at[rows], place.at[rows], arrivals.at[i, part])
                copy.start()
                copies.append(copy)
            waits.append(lambda copies=copies: [copy.wait() for copy in copies])
        kernel(*zip(places, waits), *refs[many:first])

    return pl.pallas_call(
        body,
        out_shape=outs,
        in_specs=[pl.BlockSpec(memory_space=pl.ANY)] * many,
        out_specs=jax.tree.map(lambda _: pl.BlockSpec(memory_space=pltpu.VMEM), outs),
        scratch_shapes=[pltpu.SMEM(one.shape, one.dtype) for one in scalars]
        + [pltpu.VMEM(one.shape, one.dtype) for one in operands]
        + [pltpu.SemaphoreType.DMA((many, 4))],
        compiler_params=pltpu.CompilerParams(vmem_limit_bytes=56 * 1024 * 1024),
    )(*fetched)


def shaped(shape, kind):
    return jax.ShapeDtypeStruct(shape, kind)


def sigmoid(values):
    return 0.5 + 0.5 * jnp.tanh(0.5 * values)


def served(ring, group):
    return {0: range(group, HEADS), 1: range(0, HEADS), 2: range(0, group)}[ring]


def split_kernel(history_ref, chunks_ref, arrivals):
    heads, _, both = chunks_ref.shape
    size = both // 2
    copies = []
    for head in range(heads):
        for kind in range(2):
            columns = pl.ds((kind * heads + head) * size, size)
            copies.append(
                pltpu.make_async_copy(
                    history_ref.at[:, columns],
                    chunks_ref.at[head, :, pl.ds(kind * size, size)],
                    arrivals.at[head, kind],
                )
            )
    for copy in copies:
        copy.start()
    for copy in copies:
        copy.wait()


def used_blocks(blocks_ref, length_ref, owner_ref):
    requests, width = blocks_ref.shape
    owners = owner_ref[...]
    positions = lax.broadcasted_iota(jnp.int32, (16, owners.shape[1]), 0)
    usage = jnp.zeros(positions.shape, F32)
    for request in range(requests):
        used = jnp.zeros(positions.shape, F32)
        for entry in range(width):
            block = jnp.where(entry < length_ref[request], blocks_ref[request, entry], -1)
            used = used + jnp.where(positions == block, 1.0, 0.0)
        usage = usage + jnp.where(owners == request, used, 0.0)
    return usage


def prepare_kernel(blocks, lengths, owners, cands, cots, in_weight, out_weight, bundle_ref):
    (cand_ref, cand_here), (cot_ref, cot_here) = cands, cots
    (in_ref, in_here), (out_ref, out_here) = in_weight, out_weight
    inner, count = out_ref.shape[0], cand_ref.shape[0]
    size = inner // HEADS
    bundle_ref[:, :, count:] = jnp.zeros(
        (HEADS, bundle_ref.shape[1], bundle_ref.shape[2] - count), BF16
    )
    for _, here in (blocks, lengths, owners):
        here()
    usage = used_blocks(blocks[0], lengths[0], owners[0]).astype(BF16)
    cand_here()
    rows = cand_ref[...].astype(F32)
    centered = rows - jnp.mean(rows, axis=-1, keepdims=True)
    inv_scale = lax.rsqrt(jnp.mean(centered * centered, axis=-1, keepdims=True) + 1e-05)
    normed = (centered * inv_scale).astype(BF16)
    cot_here()
    out_here()
    zed_grad = lax.dot_general(out_ref[...], cot_ref[...], NT, preferred_element_type=F32)
    in_here()
    projected = jnp.dot(normed, in_ref[...], preferred_element_type=F32).T
    for head in range(HEADS):
        part = slice(head * size, (head + 1) * size)
        gate_in = projected[inner + head * size : inner + (head + 1) * size]
        gating = gate_in * sigmoid(gate_in)
        bundle_ref[head, 0:size, :count] = projected[part].astype(BF16)
        bundle_ref[head, size : 2 * size, :count] = gating.astype(BF16)
        bundle_ref[head, 2 * size : 3 * size, :count] = (zed_grad[part] * gating).astype(BF16)
        bundle_ref[head, 3 * size :, :count] = usage


def scored(ring, blocks_ref, bundle_ref, group):
    span = served(ring, group)
    tall, size = blocks_ref.shape[1], blocks_ref.shape[2] // 2
    rows = blocks_ref[span[0] : span[-1] + 1].reshape(len(span) * tall, 2 * size)
    scores = jnp.dot(rows[:, :size], bundle_ref[group, 0:size], preferred_element_type=F32)
    scores = scores * (1.0 / math.sqrt(size))
    usage = bundle_ref[group, 3 * size :].astype(F32)
    parts = []
    for place, block in enumerate(span):
        position = HEADS * ring + block - group
        parts.append((scores[place * tall : (place + 1) * tall], usage[position : position + 1]))
    return rows[:, size:], parts


def attend(ring, blocks_ref, bundle_ref, group):
    values, parts = scored(ring, blocks_ref, bundle_ref, group)
    weights = [(scores * sigmoid(scores) * usage).astype(BF16) for scores, usage in parts]
    return lax.dot_general(
        values, jnp.concatenate(weights, axis=0), TN, preferred_element_type=F32
    )


def early_kernel(ring0, ring1, bundle, attended_ref):
    for group in range(HEADS):
        attended_ref[group] = attend(0, ring0, bundle, group) + attend(1, ring1, bundle, group)


def late_kernel(ring2, bundle, before, attended_ref, stats_ref):
    size = before.shape[1]
    for group in range(HEADS):
        attended = before[group]
        if len(served(2, group)) > 0:
            attended = attended + attend(2, ring2, bundle, group)
        attended_ref[group] = attended
        dy = bundle[group, 2 * size : 3 * size].astype(F32)
        mean = jnp.mean(attended, axis=0, keepdims=True)
        centered = attended - mean
        stats_ref[4 * group : 4 * group + 1] = mean
        stats_ref[4 * group + 1 : 4 * group + 2] = jnp.sum(centered * centered, axis=0, keepdims=True)
        stats_ref[4 * group + 2 : 4 * group + 3] = jnp.sum(dy, axis=0, keepdims=True)
        stats_ref[4 * group + 3 : 4 * group + 4] = jnp.sum(dy * centered, axis=0, keepdims=True)


def norm_kernel(attended, bundle, stats, gated_ref, grad_ref):
    size = attended.shape[1]
    width = HEADS * size
    for group in range(HEADS):
        head_stats = [stats[head, 4 * group : 4 * group + 4] for head in range(HEADS)]
        mean = sum(one[0:1] for one in head_stats) * (1.0 / HEADS)
        apart = [one[0:1] - mean for one in head_stats]
        spread = sum(one[1:2] + size * off * off for one, off in zip(head_stats, apart))
        inv_scale = lax.rsqrt(spread * (1.0 / width) + 1e-05)
        mean_dy = sum(one[2:3] for one in head_stats) * (1.0 / width)
        mixed = sum(one[3:4] + off * one[2:3] for one, off in zip(head_stats, apart))
        mean_mixed = mixed * inv_scale * (1.0 / width)
        normed = (attended[group] - mean) * inv_scale
        dy = bundle[group, 2 * size : 3 * size].astype(F32)
        gated_ref[group] = (normed * bundle[group, size : 2 * size].astype(F32)).astype(BF16)
        grad_ref[group] = (inv_scale * (dy - mean_dy - normed * mean_mixed)).astype(BF16)


def out_grad_kernel(total_cands, cots, gated, out_grad_ref):
    count = cots.shape[1]
    total = None
    for group in range(HEADS):
        part = jnp.dot(gated[group, :, :count], cots[group], preferred_element_type=F32)
        total = part if total is None else total + part
    total = (total * (1.0 / math.sqrt(total_cands))).astype(BF16)
    halves, rows_of, lines, columns = out_grad_ref.shape
    for half in range(halves):
        for row in range(rows_of):
            out_grad_ref[half, row] = total[
                row * lines : (row + 1) * lines, half * columns : (half + 1) * columns
            ]


def back(ring, blocks_ref, bundle, grads, sum_ref):
    tall, size = blocks_ref.shape[1], blocks_ref.shape[2] // 2
    scale = 1.0 / math.sqrt(size)
    keys, values = {}, {}
    for group in range(HEADS):
        span = served(ring, group)
        if len(span) == 0:
            continue
        grad = grads[group]
        value_rows, parts = scored(ring, blocks_ref, bundle, group)
        weight_grad = jnp.dot(value_rows, grad, preferred_element_type=F32)
        for place, block in enumerate(span):
            scores, usage = parts[place]
            part = sigmoid(scores)
            weights = scores * part
            slopes = (part + weights * (1.0 - part)) * (usage * scale)
            lines = weight_grad[place * tall : (place + 1) * tall]
            key = lax.dot_general(
                (lines * slopes).astype(BF16), bundle[group, 0:size], NT, preferred_element_type=F32
            )
            value = lax.dot_general(
                (weights * usage).astype(BF16), grad, NT, preferred_element_type=F32
            )
            keys[block] = keys[block] + key if block in keys else key
            values[block] = values[block] + value if block in values else value
    for block in keys:
        sum_ref[block, :, 0:size] = keys[block].astype(sum_ref.dtype)
        sum_ref[block, :, size:] = values[block].astype(sum_ref.dtype)


def back2_kernel(ring2, bundle, grads, sum_ref):
    back(2, ring2, bundle, grads, sum_ref)


def back1_kernel(ring1, bundle, grads, sum_ref):
    back(1, ring1, bundle, grads, sum_ref)


def add_kernel(own, arrived, sum_ref):
    count = arrived.shape[0]
    sum_ref[:count] = (own[:count] + arrived[...].astype(F32)).astype(BF16)
    sum_ref[count:] = own[count:].astype(BF16)


def back0_kernel(ring0, bundle, grads, sum_ref):
    back(0, ring0, bundle, grads, sum_ref)


def fold_kernel(parts, folded_ref):
    total = jnp.sum(parts[...].astype(F32), axis=0).astype(BF16)
    lines = folded_ref.shape[2]
    for row in range(folded_ref.shape[1]):
        for copy in range(folded_ref.shape[0]):
            folded_ref[copy, row] = total[row * lines : (row + 1) * lines]


def pick_kernel(place_ref, parts, spread_ref):
    total = jnp.zeros(spread_ref.shape[1:], F32)
    for source in range(parts.shape[0]):
        total = total + parts[source, place_ref[0]].astype(F32)
    for peer in range(spread_ref.shape[0]):
        spread_ref[peer] = total


def last_kernel(parts, rows_ref):
    cores = parts.shape[1]
    half = rows_ref.shape[1] // cores
    for core in range(cores):
        rows_ref[:, core * half : (core + 1) * half] = jnp.sum(parts[:, core], axis=0)


def parcel_kernel(place_ref, gated_ref, back0, back1, *parcel_refs):
    size = gated_ref.shape[1]
    for step, parcel in enumerate(parcel_refs):
        target = lax.rem(place_ref[0] + step, HEADS)
        parcel[0:size] = gated_ref[target]
        parcel[size:] = (back0[target] + back1[target].astype(F32)).astype(BF16)


def join_kernel(place_ref, cand_ref, out_ref, *refs):
    *parcels, result_ref, grad_ref = refs
    inner, count = out_ref.shape[0], cand_ref.shape[0]
    size = inner // HEADS
    product = None
    for step, parcel in enumerate(parcels):
        head = lax.rem(place_ref[0] + HEADS - step, HEADS)
        rows = pl.ds(pl.multiple_of(head * size, size), size)
        part = lax.dot_general(parcel[0:size, :count], out_ref[rows], TN, preferred_element_type=F32)
        product = part if product is None else product + part
        grad_ref[:, rows] = parcel[size:, 0:size]
        grad_ref[:, pl.ds(pl.multiple_of(inner + head * size, size), size)] = parcel[size:, size:]
    result_ref[...] = (cand_ref[...].astype(F32) + product).astype(BF16)


def moved(block, distance):
    size = lax.axis_size(DEPTH)
    return lax.ppermute(block, DEPTH, [((i + distance) % size, i) for i in range(size)])


def exchanged(chunks, axis):
    return lax.all_to_all(chunks, axis, 0, 0, tiled=True)


def spread_over(block, axis):
    size = lax.axis_size(axis)
    return exchanged(jnp.broadcast_to(block[None], (size,) + block.shape), axis)


def summed(parts):
    return jnp.sum(parts.astype(F32), axis=0)


def on_device(
    candidates,
    cotangent,
    history,
    request_blocks,
    request_length,
    candidate_request,
    in_weight,
    out_weight,
):
    tall, wide = history.shape
    inner = wide // 2
    size = inner // HEADS
    count = candidates.shape[0]
    lanes = 2 * size
    total_cands = count * lax.axis_size(ALL)
    barrier = lax.optimization_barrier
    place = lax.axis_index("x").reshape(1).astype(jnp.int32)

    cots = lax.all_gather(cotangent, "x")
    ring_shape = shaped((HEADS, tall, 2 * size), BF16)
    by_head = pl.pallas_call(
        split_kernel,
        out_shape=ring_shape,
        in_specs=[pl.BlockSpec(memory_space=pl.ANY)],
        out_specs=pl.BlockSpec(memory_space=pltpu.VMEM),
        scratch_shapes=[pltpu.SemaphoreType.DMA((HEADS, 2))],
        compiler_params=pltpu.CompilerParams(vmem_limit_bytes=56 * 1024 * 1024),
    )(history)
    ring0 = exchanged(by_head, "x")

    ring2 = moved(ring0[: HEADS - 1], 2)
    ring1 = moved(ring0, 1)
    bundle = on_fetched(
        prepare_kernel,
        shaped((HEADS, 3 * size + 16, lanes), BF16),
        candidate_request.reshape(1, count),
        candidates,
        cotangent,
        in_weight,
        out_weight,
        scalars=(request_blocks, request_length),
    )
    bundle = exchanged(bundle, "x")

    attended_shape = shaped((HEADS, size, lanes), F32)
    before = on_core(early_kernel, attended_shape, ring0, ring1, bundle)
    attended, stats = on_core(
        late_kernel, (attended_shape, shaped((4 * HEADS, lanes), F32)), ring2, bundle, before
    )
    stats = spread_over(stats, "x")
    head_shape = shaped((HEADS, size, lanes), BF16)
    cores, zh, zl, xs = (lax.axis_size(name) for name in ("core", "zh", "zl", "x"))
    own, half = size // (zl * xs), out_weight.shape[1] // cores
    gated, grads = on_core(norm_kernel, (head_shape, head_shape), attended, bundle, stats)
    back2 = on_core(back2_kernel, shaped(ring2.shape, BF16), ring2, bundle, grads)
    gated, back2 = barrier((gated, back2))
    back2 = moved(back2, -1)
    out_grad = on_core(
        lambda *refs: out_grad_kernel(total_cands, *refs),
        shaped((cores, zl, size // zl, half), BF16),
        cots,
        gated,
    )
    out_grad, late_grads = barrier((out_grad, grads))
    back1 = on_core(back1_kernel, shaped(ring1.shape, F32), ring1, bundle, late_grads)
    out_grad, back2, back1, late_grads = barrier((out_grad, back2, back1, late_grads))
    part = exchanged(out_grad.reshape(cores * zl, size // zl, half), ("core", "zl"))
    back1 = on_core(add_kernel, shaped(ring1.shape, BF16), back1, back2)
    back0 = on_core(back0_kernel, shaped(ring0.shape, F32), ring0, bundle, late_grads)
    parcels = on_core(
        parcel_kernel, [shaped((2 * size, lanes), BF16)] * HEADS, gated, back0, moved(back1, -1), scalars=(place,)
    )
    part, *parcels = barrier((part, *parcels))
    part, *parcels = barrier((on_core(fold_kernel, shaped((zh, xs, own, half), BF16), part), *parcels))
    part = exchanged(part.reshape(zh * xs, own, half), ("zh", "x")).reshape(zh, xs, own, half)
    depth = lax.axis_index("zh").reshape(1).astype(jnp.int32)
    peers = lax.axis_size("y") * cores
    part = on_core(pick_kernel, shaped((peers, own, half), F32), part, scalars=(depth,))

    arrived = [
        lax.ppermute(parcel, "x", [(i, (i + step) % HEADS) for i in range(HEADS)]) if step else parcel
        for step, parcel in enumerate(parcels)
    ]
    part = exchanged(part, ("y", "core")).reshape(-1, cores, own, half)
    grad_rows = on_core(last_kernel, shaped((own, cores * half), F32), part)

    layer_out, grad_history = on_core(
        join_kernel,
        (shaped(candidates.shape, BF16), shaped(history.shape, BF16)),
        candidates,
        out_weight,
        *arrived,
        scalars=(place,),
    )
    return (layer_out, grad_rows, grad_history)


def solution(mesh):
    inner = Mesh(mesh.devices.reshape(4, 2, 4, 4, 4), ALL)
    rows = P(ALL)
    return jax.shard_map(
        on_device,
        mesh=inner,
        in_specs=(rows, rows, rows, rows, rows, rows, P(), P()),
        out_specs=(rows, P(("zh", "zl", "x")), rows),
        check_vma=False,
    )
```

```python
import math

import jax
import jax.numpy as jnp
from jax import lax
from jax.experimental import pallas as pl
from jax.experimental.pallas import tpu as pltpu
from jax.sharding import Mesh, PartitionSpec as P

HEADS = 4
SPAN = 8
BF16 = jnp.bfloat16
F32 = jnp.float32
ALL = ("y", "core", "zh", "zl", "x")
DEPTH = ("zh", "zl")
NT = (((1,), (1,)), ((), ()))
TN = (((0,), (0,)), ((), ()))


def on_core(kernel, outs, *operands, scalars=()):
    spaces = [pltpu.SMEM] * len(scalars) + [pltpu.VMEM] * len(operands)
    return pl.pallas_call(
        kernel,
        out_shape=outs,
        in_specs=[pl.BlockSpec(memory_space=space) for space in spaces],
        out_specs=jax.tree.map(lambda _: pl.BlockSpec(memory_space=pltpu.VMEM), outs),
        compiler_params=pltpu.CompilerParams(vmem_limit_bytes=12 * 1024 * 1024),
    )(*scalars, *operands)


def on_fetched(kernel, outs, *operands, scalars=()):
    fetched = list(scalars) + list(operands)
    many = len(fetched)
    first = many + len(jax.tree.leaves(outs))
    pieces = [4 if one.size >= 1 << 19 else 1 for one in fetched]

    def body(*refs):
        places, arrivals = refs[first : first + many], refs[first + many]
        waits = []
        for i, (source, place) in enumerate(zip(refs[:many], places)):
            step = place.shape[0] // pieces[i]
            copies = []
            for part in range(pieces[i]):
                rows = (slice(None),) if pieces[i] == 1 else (pl.ds(part * step, step),)
                copy = pltpu.make_async_copy(source.at[rows], place.at[rows], arrivals.at[i, part])
                copy.start()
                copies.append(copy)
            waits.append(lambda copies=copies: [copy.wait() for copy in copies])
        kernel(*zip(places, waits), *refs[many:first])

    return pl.pallas_call(
        body,
        out_shape=outs,
        in_specs=[pl.BlockSpec(memory_space=pl.ANY)] * many,
        out_specs=jax.tree.map(lambda _: pl.BlockSpec(memory_space=pltpu.VMEM), outs),
        scratch_shapes=[pltpu.SMEM(one.shape, one.dtype) for one in scalars]
        + [pltpu.VMEM(one.shape, one.dtype) for one in operands]
        + [pltpu.SemaphoreType.DMA((many, 4))],
        compiler_params=pltpu.CompilerParams(vmem_limit_bytes=56 * 1024 * 1024),
    )(*fetched)


def shaped(shape, kind):
    return jax.ShapeDtypeStruct(shape, kind)


def sigmoid(values):
    return 0.5 + 0.5 * jnp.tanh(0.5 * values)


def served(ring, group):
    return {0: range(group, HEADS), 1: range(0, HEADS), 2: range(0, group)}[ring]


def split_kernel(history_ref, chunks_ref, arrivals):
    heads, _, both = chunks_ref.shape
    size = both // 2
    copies = []
    for head in range(heads):
        for kind in range(2):
            columns = pl.ds((kind * heads + head) * size, size)
            copies.append(
                pltpu.make_async_copy(
                    history_ref.at[:, columns],
                    chunks_ref.at[head, :, pl.ds(kind * size, size)],
                    arrivals.at[head, kind],
                )
            )
    for copy in copies:
        copy.start()
    for copy in copies:
        copy.wait()


def used_blocks(blocks_ref, length_ref, owner_ref):
    requests, width = blocks_ref.shape
    owners = owner_ref[...]
    positions = lax.broadcasted_iota(jnp.int32, (16, owners.shape[1]), 0)
    usage = jnp.zeros(positions.shape, F32)
    for request in range(requests):
        used = jnp.zeros(positions.shape, F32)
        for entry in range(width):
            block = jnp.where(entry < length_ref[request], blocks_ref[request, entry], -1)
            used = used + jnp.where(positions == block, 1.0, 0.0)
        usage = usage + jnp.where(owners == request, used, 0.0)
    return usage


def prepare_kernel(blocks, lengths, owners, cands, cots, in_weight, out_weight, bundle_ref):
    (cand_ref, cand_here), (cot_ref, cot_here) = cands, cots
    (in_ref, in_here), (out_ref, out_here) = in_weight, out_weight
    inner, count = out_ref.shape[0], cand_ref.shape[0]
    size = inner // HEADS
    bundle_ref[:, :, count:] = jnp.zeros(
        (HEADS, bundle_ref.shape[1], bundle_ref.shape[2] - count), BF16
    )
    for _, here in (blocks, lengths, owners):
        here()
    usage = used_blocks(blocks[0], lengths[0], owners[0]).astype(BF16)
    cand_here()
    rows = cand_ref[...].astype(F32)
    centered = rows - jnp.mean(rows, axis=-1, keepdims=True)
    inv_scale = lax.rsqrt(jnp.mean(centered * centered, axis=-1, keepdims=True) + 1e-05)
    normed = (centered * inv_scale).astype(BF16)
    cot_here()
    out_here()
    zed_grad = lax.dot_general(out_ref[...], cot_ref[...], NT, preferred_element_type=F32)
    in_here()
    projected = jnp.dot(normed, in_ref[...], preferred_element_type=F32).T
    for head in range(HEADS):
        part = slice(head * size, (head + 1) * size)
        gate_in = projected[inner + head * size : inner + (head + 1) * size]
        gating = gate_in * sigmoid(gate_in)
        bundle_ref[head, 0:size, :count] = projected[part].astype(BF16)
        bundle_ref[head, size : 2 * size, :count] = gating.astype(BF16)
        bundle_ref[head, 2 * size : 3 * size, :count] = (zed_grad[part] * gating).astype(BF16)
        bundle_ref[head, 3 * size :, :count] = usage


def scored(ring, blocks_ref, bundle_ref, group):
    span = served(ring, group)
    tall, size = blocks_ref.shape[1], blocks_ref.shape[2] // 2
    rows = blocks_ref[span[0] : span[-1] + 1].reshape(len(span) * tall, 2 * size)
    scores = jnp.dot(rows[:, :size], bundle_ref[group, 0:size], preferred_element_type=F32)
    scores = scores * (1.0 / math.sqrt(size))
    usage = bundle_ref[group, 3 * size :].astype(F32)
    parts = []
    for place, block in enumerate(span):
        position = HEADS * ring + block - group
        parts.append((scores[place * tall : (place + 1) * tall], usage[position : position + 1]))
    return rows[:, size:], parts


def attend(ring, blocks_ref, bundle_ref, group):
    values, parts = scored(ring, blocks_ref, bundle_ref, group)
    weights = [(scores * sigmoid(scores) * usage).astype(BF16) for scores, usage in parts]
    return lax.dot_general(
        values, jnp.concatenate(weights, axis=0), TN, preferred_element_type=F32
    )


def early_kernel(ring0, ring1, bundle, attended_ref):
    for group in range(HEADS):
        attended_ref[group] = attend(0, ring0, bundle, group) + attend(1, ring1, bundle, group)


def late_kernel(ring2, bundle, before, attended_ref, stats_ref):
    size = before.shape[1]
    for group in range(HEADS):
        attended = before[group]
        if len(served(2, group)) > 0:
            attended = attended + attend(2, ring2, bundle, group)
        attended_ref[group] = attended
        dy = bundle[group, 2 * size : 3 * size].astype(F32)
        mean = jnp.mean(attended, axis=0, keepdims=True)
        centered = attended - mean
        stats_ref[4 * group : 4 * group + 1] = mean
        stats_ref[4 * group + 1 : 4 * group + 2] = jnp.sum(centered * centered, axis=0, keepdims=True)
        stats_ref[4 * group + 2 : 4 * group + 3] = jnp.sum(dy, axis=0, keepdims=True)
        stats_ref[4 * group + 3 : 4 * group + 4] = jnp.sum(dy * centered, axis=0, keepdims=True)


def norm_kernel(attended, bundle, stats, gated_ref, grad_ref):
    size = attended.shape[1]
    width = HEADS * size
    for group in range(HEADS):
        head_stats = [stats[head, 4 * group : 4 * group + 4] for head in range(HEADS)]
        mean = sum(one[0:1] for one in head_stats) * (1.0 / HEADS)
        apart = [one[0:1] - mean for one in head_stats]
        spread = sum(one[1:2] + size * off * off for one, off in zip(head_stats, apart))
        inv_scale = lax.rsqrt(spread * (1.0 / width) + 1e-05)
        mean_dy = sum(one[2:3] for one in head_stats) * (1.0 / width)
        mixed = sum(one[3:4] + off * one[2:3] for one, off in zip(head_stats, apart))
        mean_mixed = mixed * inv_scale * (1.0 / width)
        normed = (attended[group] - mean) * inv_scale
        dy = bundle[group, 2 * size : 3 * size].astype(F32)
        gated_ref[group] = (normed * bundle[group, size : 2 * size].astype(F32)).astype(BF16)
        grad_ref[group] = (inv_scale * (dy - mean_dy - normed * mean_mixed)).astype(BF16)


def out_grad_kernel(total_cands, cots, gated, out_grad_ref):
    count = cots.shape[1]
    total = None
    for group in range(HEADS):
        part = jnp.dot(gated[group, :, :count], cots[group], preferred_element_type=F32)
        total = part if total is None else total + part
    total = (total * (1.0 / math.sqrt(total_cands))).astype(BF16)
    halves, rows_of, lines, columns = out_grad_ref.shape
    for half in range(halves):
        for row in range(rows_of):
            out_grad_ref[half, row] = total[
                row * lines : (row + 1) * lines, half * columns : (half + 1) * columns
            ]


def back(ring, blocks_ref, bundle, grads, sum_ref):
    tall, size = blocks_ref.shape[1], blocks_ref.shape[2] // 2
    scale = 1.0 / math.sqrt(size)
    keys, values = {}, {}
    for group in range(HEADS):
        span = served(ring, group)
        if len(span) == 0:
            continue
        grad = grads[group]
        value_rows, parts = scored(ring, blocks_ref, bundle, group)
        weight_grad = jnp.dot(value_rows, grad, preferred_element_type=F32)
        for place, block in enumerate(span):
            scores, usage = parts[place]
            part = sigmoid(scores)
            weights = scores * part
            slopes = (part + weights * (1.0 - part)) * (usage * scale)
            lines = weight_grad[place * tall : (place + 1) * tall]
            key = lax.dot_general(
                (lines * slopes).astype(BF16), bundle[group, 0:size], NT, preferred_element_type=F32
            )
            value = lax.dot_general(
                (weights * usage).astype(BF16), grad, NT, preferred_element_type=F32
            )
            keys[block] = keys[block] + key if block in keys else key
            values[block] = values[block] + value if block in values else value
    for block in keys:
        sum_ref[block, :, 0:size] = keys[block].astype(sum_ref.dtype)
        sum_ref[block, :, size:] = values[block].astype(sum_ref.dtype)


def back2_kernel(ring2, bundle, grads, sum_ref):
    back(2, ring2, bundle, grads, sum_ref)


def back1_kernel(ring1, bundle, grads, sum_ref):
    back(1, ring1, bundle, grads, sum_ref)


def add_kernel(own, arrived, sum_ref):
    count = arrived.shape[0]
    sum_ref[:count] = (own[:count] + arrived[...].astype(F32)).astype(BF16)
    sum_ref[count:] = own[count:].astype(BF16)


def back0_kernel(ring0, bundle, grads, sum_ref):
    back(0, ring0, bundle, grads, sum_ref)


def fold_kernel(parts, folded_ref):
    total = jnp.sum(parts[...].astype(F32), axis=0).astype(BF16)
    lines = folded_ref.shape[2]
    for row in range(folded_ref.shape[1]):
        for copy in range(folded_ref.shape[0]):
            folded_ref[copy, row] = total[row * lines : (row + 1) * lines]


def pick_kernel(place_ref, parts, spread_ref):
    total = jnp.zeros(spread_ref.shape[1:], F32)
    for source in range(parts.shape[0]):
        total = total + parts[source, place_ref[0]].astype(F32)
    for peer in range(spread_ref.shape[0]):
        spread_ref[peer] = total


def last_kernel(parts, rows_ref):
    cores = parts.shape[1]
    half = rows_ref.shape[1] // cores
    for core in range(cores):
        rows_ref[:, core * half : (core + 1) * half] = jnp.sum(parts[:, core], axis=0)


def parcel_kernel(place_ref, gated_ref, back0, back1, *parcel_refs):
    size = gated_ref.shape[1]
    for step, parcel in enumerate(parcel_refs):
        target = lax.rem(place_ref[0] + step, HEADS)
        parcel[0:size] = gated_ref[target]
        parcel[size:] = (back0[target] + back1[target].astype(F32)).astype(BF16)


def join_kernel(place_ref, cand_ref, out_ref, *refs):
    *parcels, result_ref, grad_ref = refs
    inner, count = out_ref.shape[0], cand_ref.shape[0]
    size = inner // HEADS
    product = None
    for step, parcel in enumerate(parcels):
        head = lax.rem(place_ref[0] + HEADS - step, HEADS)
        rows = pl.ds(pl.multiple_of(head * size, size), size)
        part = lax.dot_general(parcel[0:size, :count], out_ref[rows], TN, preferred_element_type=F32)
        product = part if product is None else product + part
        grad_ref[:, rows] = parcel[size:, 0:size]
        grad_ref[:, pl.ds(pl.multiple_of(inner + head * size, size), size)] = parcel[size:, size:]
    result_ref[...] = (cand_ref[...].astype(F32) + product).astype(BF16)


def moved(block, distance):
    size = lax.axis_size(DEPTH)
    return lax.ppermute(block, DEPTH, [((i + distance) % size, i) for i in range(size)])


def exchanged(chunks, axis):
    return lax.all_to_all(chunks, axis, 0, 0, tiled=True)


def spread_over(block, axis):
    size = lax.axis_size(axis)
    return exchanged(jnp.broadcast_to(block[None], (size,) + block.shape), axis)


def summed(parts):
    return jnp.sum(parts.astype(F32), axis=0)


def on_device(
    candidates,
    cotangent,
    history,
    request_blocks,
    request_length,
    candidate_request,
    in_weight,
    out_weight,
):
    tall, wide = history.shape
    inner = wide // 2
    size = inner // HEADS
    count = candidates.shape[0]
    lanes = 2 * size
    total_cands = count * lax.axis_size(ALL)
    barrier = lax.optimization_barrier
    place = lax.axis_index("x").reshape(1).astype(jnp.int32)

    ring_shape = shaped((HEADS, tall, 2 * size), BF16)
    by_head = pl.pallas_call(
        split_kernel,
        out_shape=ring_shape,
        in_specs=[pl.BlockSpec(memory_space=pl.ANY)],
        out_specs=pl.BlockSpec(memory_space=pltpu.VMEM),
        scratch_shapes=[pltpu.SemaphoreType.DMA((HEADS, 2))],
        compiler_params=pltpu.CompilerParams(vmem_limit_bytes=56 * 1024 * 1024),
    )(history)
    ring0 = exchanged(by_head, "x")

    ring2 = moved(ring0[: HEADS - 1], 2)
    ring1 = moved(ring0, 1)
    bundle = on_fetched(
        prepare_kernel,
        shaped((HEADS, 3 * size + 16, lanes), BF16),
        candidate_request.reshape(1, count),
        candidates,
        cotangent,
        in_weight,
        out_weight,
        scalars=(request_blocks, request_length),
    )
    bundle, cots = barrier((bundle, cotangent))
    cots = lax.all_gather(cots, "x")
    bundle = exchanged(bundle, "x")

    attended_shape = shaped((HEADS, size, lanes), F32)
    before = on_core(early_kernel, attended_shape, ring0, ring1, bundle)
    attended, stats = on_core(
        late_kernel, (attended_shape, shaped((4 * HEADS, lanes), F32)), ring2, bundle, before
    )
    stats = spread_over(stats, "x")
    head_shape = shaped((HEADS, size, lanes), BF16)
    cores, zh, zl, xs = (lax.axis_size(name) for name in ("core", "zh", "zl", "x"))
    own, half = size // (zl * xs), out_weight.shape[1] // cores
    gated, grads = on_core(norm_kernel, (head_shape, head_shape), attended, bundle, stats)
    back2 = on_core(back2_kernel, shaped(ring2.shape, BF16), ring2, bundle, grads)
    gated, back2 = barrier((gated, back2))
    back2 = moved(back2, -1)
    out_grad = on_core(
        lambda *refs: out_grad_kernel(total_cands, *refs),
        shaped((cores, zl, size // zl, half), BF16),
        cots,
        gated,
    )
    out_grad, late_grads = barrier((out_grad, grads))
    back1 = on_core(back1_kernel, shaped(ring1.shape, F32), ring1, bundle, late_grads)
    out_grad, back2, back1, late_grads = barrier((out_grad, back2, back1, late_grads))
    part = exchanged(out_grad.reshape(cores * zl, size // zl, half), ("core", "zl"))
    back1 = on_core(add_kernel, shaped(ring1.shape, BF16), back1, back2)
    back0 = on_core(back0_kernel, shaped(ring0.shape, F32), ring0, bundle, late_grads)
    parcels = on_core(
        parcel_kernel, [shaped((2 * size, lanes), BF16)] * HEADS, gated, back0, moved(back1, -1), scalars=(place,)
    )
    part, *parcels = barrier((part, *parcels))
    part, *parcels = barrier((on_core(fold_kernel, shaped((zh, xs, own, half), BF16), part), *parcels))
    part = exchanged(part.reshape(zh * xs, own, half), ("zh", "x")).reshape(zh, xs, own, half)
    depth = lax.axis_index("zh").reshape(1).astype(jnp.int32)
    peers = lax.axis_size("y") * cores
    part = on_core(pick_kernel, shaped((peers, own, half), F32), part, scalars=(depth,))

    arrived = [
        lax.ppermute(parcel, "x", [(i, (i + step) % HEADS) for i in range(HEADS)]) if step else parcel
        for step, parcel in enumerate(parcels)
    ]
    part = exchanged(part, ("y", "core")).reshape(-1, cores, own, half)
    grad_rows = on_core(last_kernel, shaped((own, cores * half), F32), part)

    layer_out, grad_history = on_core(
        join_kernel,
        (shaped(candidates.shape, BF16), shaped(history.shape, BF16)),
        candidates,
        out_weight,
        *arrived,
        scalars=(place,),
    )
    return (layer_out, grad_rows, grad_history)


def solution(mesh):
    inner = Mesh(mesh.devices.reshape(4, 2, 4, 4, 4), ALL)
    rows = P(ALL)
    return jax.shard_map(
        on_device,
        mesh=inner,
        in_specs=(rows, rows, rows, rows, rows, rows, P(), P()),
        out_specs=(rows, P(("zh", "zl", "x")), rows),
        check_vma=False,
    )
```

```python
import math

import jax
import jax.numpy as jnp
from jax import lax
from jax.experimental import pallas as pl
from jax.experimental.pallas import tpu as pltpu
from jax.sharding import Mesh, PartitionSpec as P

HEADS = 4
SPAN = 8
BF16 = jnp.bfloat16
F32 = jnp.float32
ALL = ("y", "core", "zh", "zl", "x")
DEPTH = ("zh", "zl")
NT = (((1,), (1,)), ((), ()))
TN = (((0,), (0,)), ((), ()))


def on_core(kernel, outs, *operands, scalars=()):
    spaces = [pltpu.SMEM] * len(scalars) + [pltpu.VMEM] * len(operands)
    return pl.pallas_call(
        kernel,
        out_shape=outs,
        in_specs=[pl.BlockSpec(memory_space=space) for space in spaces],
        out_specs=jax.tree.map(lambda _: pl.BlockSpec(memory_space=pltpu.VMEM), outs),
        compiler_params=pltpu.CompilerParams(vmem_limit_bytes=12 * 1024 * 1024),
    )(*scalars, *operands)


def on_fetched(kernel, outs, *operands, scalars=()):
    fetched = list(scalars) + list(operands)
    many = len(fetched)
    first = many + len(jax.tree.leaves(outs))
    pieces = [4 if one.size >= 1 << 19 else 1 for one in fetched]

    def body(*refs):
        places, arrivals = refs[first : first + many], refs[first + many]
        waits = []
        for i, (source, place) in enumerate(zip(refs[:many], places)):
            step = place.shape[0] // pieces[i]
            copies = []
            for part in range(pieces[i]):
                rows = (slice(None),) if pieces[i] == 1 else (pl.ds(part * step, step),)
                copy = pltpu.make_async_copy(source.at[rows], place.at[rows], arrivals.at[i, part])
                copy.start()
                copies.append(copy)
            waits.append(lambda copies=copies: [copy.wait() for copy in copies])
        kernel(*zip(places, waits), *refs[many:first])

    return pl.pallas_call(
        body,
        out_shape=outs,
        in_specs=[pl.BlockSpec(memory_space=pl.ANY)] * many,
        out_specs=jax.tree.map(lambda _: pl.BlockSpec(memory_space=pltpu.VMEM), outs),
        scratch_shapes=[pltpu.SMEM(one.shape, one.dtype) for one in scalars]
        + [pltpu.VMEM(one.shape, one.dtype) for one in operands]
        + [pltpu.SemaphoreType.DMA((many, 4))],
        compiler_params=pltpu.CompilerParams(vmem_limit_bytes=56 * 1024 * 1024),
    )(*fetched)


def shaped(shape, kind):
    return jax.ShapeDtypeStruct(shape, kind)


def sigmoid(values):
    return 0.5 + 0.5 * jnp.tanh(0.5 * values)


def served(ring, group):
    return {0: range(group, HEADS), 1: range(0, HEADS), 2: range(0, group)}[ring]


def split_kernel(history_ref, chunks_ref, arrivals):
    heads, _, both = chunks_ref.shape
    size = both // 2
    copies = []
    for head in range(heads):
        for kind in range(2):
            columns = pl.ds((kind * heads + head) * size, size)
            copies.append(
                pltpu.make_async_copy(
                    history_ref.at[:, columns],
                    chunks_ref.at[head, :, pl.ds(kind * size, size)],
                    arrivals.at[head, kind],
                )
            )
    for copy in copies:
        copy.start()
    for copy in copies:
        copy.wait()


def used_blocks(blocks_ref, length_ref, owner_ref):
    requests, width = blocks_ref.shape
    owners = owner_ref[...]
    positions = lax.broadcasted_iota(jnp.int32, (16, owners.shape[1]), 0)
    usage = jnp.zeros(positions.shape, F32)
    for request in range(requests):
        used = jnp.zeros(positions.shape, F32)
        for entry in range(width):
            block = jnp.where(entry < length_ref[request], blocks_ref[request, entry], -1)
            used = used + jnp.where(positions == block, 1.0, 0.0)
        usage = usage + jnp.where(owners == request, used, 0.0)
    return usage


def prepare_kernel(blocks, lengths, owners, cands, cots, in_weight, out_weight, bundle_ref):
    (cand_ref, cand_here), (cot_ref, cot_here) = cands, cots
    (in_ref, in_here), (out_ref, out_here) = in_weight, out_weight
    inner, count = out_ref.shape[0], cand_ref.shape[0]
    size = inner // HEADS
    bundle_ref[:, :, count:] = jnp.zeros(
        (HEADS, bundle_ref.shape[1], bundle_ref.shape[2] - count), BF16
    )
    for _, here in (blocks, lengths, owners):
        here()
    usage = used_blocks(blocks[0], lengths[0], owners[0]).astype(BF16)
    cand_here()
    rows = cand_ref[...].astype(F32)
    centered = rows - jnp.mean(rows, axis=-1, keepdims=True)
    inv_scale = lax.rsqrt(jnp.mean(centered * centered, axis=-1, keepdims=True) + 1e-05)
    normed = (centered * inv_scale).astype(BF16)
    cot_here()
    out_here()
    zed_grad = lax.dot_general(out_ref[...], cot_ref[...], NT, preferred_element_type=F32)
    in_here()
    projected = jnp.dot(normed, in_ref[...], preferred_element_type=F32).T
    for head in range(HEADS):
        part = slice(head * size, (head + 1) * size)
        gate_in = projected[inner + head * size : inner + (head + 1) * size]
        gating = gate_in * sigmoid(gate_in)
        bundle_ref[head, 0:size, :count] = projected[part].astype(BF16)
        bundle_ref[head, size : 2 * size, :count] = gating.astype(BF16)
        bundle_ref[head, 2 * size : 3 * size, :count] = (zed_grad[part] * gating).astype(BF16)
        bundle_ref[head, 3 * size :, :count] = usage


def scored(ring, blocks_ref, bundle_ref, group):
    span = served(ring, group)
    tall, size = blocks_ref.shape[1], blocks_ref.shape[2] // 2
    rows = blocks_ref[span[0] : span[-1] + 1].reshape(len(span) * tall, 2 * size)
    scores = jnp.dot(rows[:, :size], bundle_ref[group, 0:size], preferred_element_type=F32)
    scores = scores * (1.0 / math.sqrt(size))
    usage = bundle_ref[group, 3 * size :].astype(F32)
    parts = []
    for place, block in enumerate(span):
        position = HEADS * ring + block - group
        parts.append((scores[place * tall : (place + 1) * tall], usage[position : position + 1]))
    return rows[:, size:], parts


def attend(ring, blocks_ref, bundle_ref, group):
    values, parts = scored(ring, blocks_ref, bundle_ref, group)
    weights = [(scores * sigmoid(scores) * usage).astype(BF16) for scores, usage in parts]
    return lax.dot_general(
        values, jnp.concatenate(weights, axis=0), TN, preferred_element_type=F32
    )


def early_kernel(ring0, ring1, bundle, attended_ref):
    for group in range(HEADS):
        attended_ref[group] = attend(0, ring0, bundle, group) + attend(1, ring1, bundle, group)


def late_kernel(ring2, bundle, before, attended_ref, stats_ref):
    size = before.shape[1]
    for group in range(HEADS):
        attended = before[group]
        if len(served(2, group)) > 0:
            attended = attended + attend(2, ring2, bundle, group)
        attended_ref[group] = attended
        dy = bundle[group, 2 * size : 3 * size].astype(F32)
        mean = jnp.mean(attended, axis=0, keepdims=True)
        centered = attended - mean
        stats_ref[4 * group : 4 * group + 1] = mean
        stats_ref[4 * group + 1 : 4 * group + 2] = jnp.sum(centered * centered, axis=0, keepdims=True)
        stats_ref[4 * group + 2 : 4 * group + 3] = jnp.sum(dy, axis=0, keepdims=True)
        stats_ref[4 * group + 3 : 4 * group + 4] = jnp.sum(dy * centered, axis=0, keepdims=True)


def norm_kernel(attended, bundle, stats, gated_ref, grad_ref):
    size = attended.shape[1]
    width = HEADS * size
    for group in range(HEADS):
        head_stats = [stats[head, 4 * group : 4 * group + 4] for head in range(HEADS)]
        mean = sum(one[0:1] for one in head_stats) * (1.0 / HEADS)
        apart = [one[0:1] - mean for one in head_stats]
        spread = sum(one[1:2] + size * off * off for one, off in zip(head_stats, apart))
        inv_scale = lax.rsqrt(spread * (1.0 / width) + 1e-05)
        mean_dy = sum(one[2:3] for one in head_stats) * (1.0 / width)
        mixed = sum(one[3:4] + off * one[2:3] for one, off in zip(head_stats, apart))
        mean_mixed = mixed * inv_scale * (1.0 / width)
        normed = (attended[group] - mean) * inv_scale
        dy = bundle[group, 2 * size : 3 * size].astype(F32)
        gated_ref[group] = (normed * bundle[group, size : 2 * size].astype(F32)).astype(BF16)
        grad_ref[group] = (inv_scale * (dy - mean_dy - normed * mean_mixed)).astype(BF16)


def out_grad_kernel(total_cands, cots, gated, out_grad_ref):
    count = cots.shape[1]
    total = None
    for group in range(HEADS):
        part = jnp.dot(gated[group, :, :count], cots[group], preferred_element_type=F32)
        total = part if total is None else total + part
    total = (total * (1.0 / math.sqrt(total_cands))).astype(BF16)
    halves, rows_of, lines, columns = out_grad_ref.shape
    for half in range(halves):
        for row in range(rows_of):
            out_grad_ref[half, row] = total[
                row * lines : (row + 1) * lines, half * columns : (half + 1) * columns
            ]


def back(ring, blocks_ref, bundle, grads, sum_ref):
    tall, size = blocks_ref.shape[1], blocks_ref.shape[2] // 2
    scale = 1.0 / math.sqrt(size)
    keys, values = {}, {}
    for group in range(HEADS):
        span = served(ring, group)
        if len(span) == 0:
            continue
        grad = grads[group]
        value_rows, parts = scored(ring, blocks_ref, bundle, group)
        weight_grad = jnp.dot(value_rows, grad, preferred_element_type=F32)
        for place, block in enumerate(span):
            scores, usage = parts[place]
            part = sigmoid(scores)
            weights = scores * part
            slopes = (part + weights * (1.0 - part)) * (usage * scale)
            lines = weight_grad[place * tall : (place + 1) * tall]
            key = lax.dot_general(
                (lines * slopes).astype(BF16), bundle[group, 0:size], NT, preferred_element_type=F32
            )
            value = lax.dot_general(
                (weights * usage).astype(BF16), grad, NT, preferred_element_type=F32
            )
            keys[block] = keys[block] + key if block in keys else key
            values[block] = values[block] + value if block in values else value
    for block in keys:
        sum_ref[block, :, 0:size] = keys[block].astype(sum_ref.dtype)
        sum_ref[block, :, size:] = values[block].astype(sum_ref.dtype)


def back2_kernel(ring2, bundle, grads, sum_ref):
    back(2, ring2, bundle, grads, sum_ref)


def back1_kernel(ring1, bundle, grads, sum_ref):
    back(1, ring1, bundle, grads, sum_ref)


def add_kernel(own, arrived, sum_ref):
    count = arrived.shape[0]
    sum_ref[:count] = (own[:count] + arrived[...].astype(F32)).astype(BF16)
    sum_ref[count:] = own[count:].astype(BF16)


def back0_kernel(ring0, bundle, grads, sum_ref):
    back(0, ring0, bundle, grads, sum_ref)


def fold_kernel(parts, folded_ref):
    total = jnp.sum(parts[...].astype(F32), axis=0).astype(BF16)
    lines = folded_ref.shape[2]
    for row in range(folded_ref.shape[1]):
        for copy in range(folded_ref.shape[0]):
            folded_ref[copy, row] = total[row * lines : (row + 1) * lines]


def pick_kernel(place_ref, parts, spread_ref):
    total = jnp.zeros(spread_ref.shape[1:], F32)
    for source in range(parts.shape[0]):
        total = total + parts[source, place_ref[0]].astype(F32)
    for peer in range(spread_ref.shape[0]):
        spread_ref[peer] = total


def last_kernel(parts, rows_ref):
    cores = parts.shape[1]
    half = rows_ref.shape[1] // cores
    for core in range(cores):
        rows_ref[:, core * half : (core + 1) * half] = jnp.sum(parts[:, core], axis=0)


def parcel_kernel(place_ref, gated_ref, back0, back1, *parcel_refs):
    size = gated_ref.shape[1]
    for step, parcel in enumerate(parcel_refs):
        target = lax.rem(place_ref[0] + step, HEADS)
        parcel[0:size] = gated_ref[target]
        parcel[size:] = (back0[target] + back1[target].astype(F32)).astype(BF16)


def join_kernel(place_ref, cand_ref, out_ref, *refs):
    *parcels, result_ref, grad_ref = refs
    inner, count = out_ref.shape[0], cand_ref.shape[0]
    size = inner // HEADS
    product = None
    for step, parcel in enumerate(parcels):
        head = lax.rem(place_ref[0] + HEADS - step, HEADS)
        rows = pl.ds(pl.multiple_of(head * size, size), size)
        part = lax.dot_general(parcel[0:size, :count], out_ref[rows], TN, preferred_element_type=F32)
        product = part if product is None else product + part
        grad_ref[:, rows] = parcel[size:, 0:size]
        grad_ref[:, pl.ds(pl.multiple_of(inner + head * size, size), size)] = parcel[size:, size:]
    result_ref[...] = (cand_ref[...].astype(F32) + product).astype(BF16)


def moved(block, distance):
    size = lax.axis_size(DEPTH)
    return lax.ppermute(block, DEPTH, [((i + distance) % size, i) for i in range(size)])


def exchanged(chunks, axis):
    return lax.all_to_all(chunks, axis, 0, 0, tiled=True)


def spread_over(block, axis):
    size = lax.axis_size(axis)
    return exchanged(jnp.broadcast_to(block[None], (size,) + block.shape), axis)


def summed(parts):
    return jnp.sum(parts.astype(F32), axis=0)


def on_device(
    candidates,
    cotangent,
    history,
    request_blocks,
    request_length,
    candidate_request,
    in_weight,
    out_weight,
):
    tall, wide = history.shape
    inner = wide // 2
    size = inner // HEADS
    count = candidates.shape[0]
    lanes = 2 * size
    total_cands = count * lax.axis_size(ALL)
    barrier = lax.optimization_barrier
    place = lax.axis_index("x").reshape(1).astype(jnp.int32)

    cots = lax.all_gather(cotangent, "x")
    ring_shape = shaped((HEADS, tall, 2 * size), BF16)
    by_head = pl.pallas_call(
        split_kernel,
        out_shape=ring_shape,
        in_specs=[pl.BlockSpec(memory_space=pl.ANY)],
        out_specs=pl.BlockSpec(memory_space=pltpu.VMEM),
        scratch_shapes=[pltpu.SemaphoreType.DMA((HEADS, 2))],
        compiler_params=pltpu.CompilerParams(vmem_limit_bytes=56 * 1024 * 1024),
    )(history)
    ring0 = exchanged(by_head, "x")

    ring2 = moved(ring0[: HEADS - 1], 2)
    ring1 = moved(ring0, 1)
    bundle = on_fetched(
        prepare_kernel,
        shaped((HEADS, 3 * size + 16, lanes), BF16),
        candidate_request.reshape(1, count),
        candidates,
        cotangent,
        in_weight,
        out_weight,
        scalars=(request_blocks, request_length),
    )
    bundle = exchanged(bundle, "x")

    attended_shape = shaped((HEADS, size, lanes), F32)
    before = on_core(early_kernel, attended_shape, ring0, ring1, bundle)
    attended, stats = on_core(
        late_kernel, (attended_shape, shaped((4 * HEADS, lanes), F32)), ring2, bundle, before
    )
    stats = spread_over(stats, "x")
    head_shape = shaped((HEADS, size, lanes), BF16)
    cores, zh, zl, xs = (lax.axis_size(name) for name in ("core", "zh", "zl", "x"))
    own, half = size // (zl * xs), out_weight.shape[1] // cores
    gated, grads = on_core(norm_kernel, (head_shape, head_shape), attended, bundle, stats)
    back2 = on_core(back2_kernel, shaped(ring2.shape, BF16), ring2, bundle, grads)
    gated, back2 = barrier((gated, back2))
    back2 = moved(back2, -1)
    out_grad = on_core(
        lambda *refs: out_grad_kernel(total_cands, *refs),
        shaped((cores, zl, size // zl, half), BF16),
        cots,
        gated,
    )
    out_grad, late_grads = barrier((out_grad, grads))
    back1 = on_core(back1_kernel, shaped(ring1.shape, F32), ring1, bundle, late_grads)
    out_grad, back2, back1, late_grads = barrier((out_grad, back2, back1, late_grads))
    part = exchanged(out_grad.reshape(cores * zl, size // zl, half), ("core", "zl"))
    back1 = on_core(add_kernel, shaped(ring1.shape, BF16), back1, back2)
    back0 = on_core(back0_kernel, shaped(ring0.shape, F32), ring0, bundle, late_grads)
    part, back0, back1 = barrier((part, back0, back1))
    part = on_core(fold_kernel, shaped((zh, xs, own, half), BF16), part)
    parcels = on_core(
        parcel_kernel, [shaped((2 * size, lanes), BF16)] * HEADS, gated, back0, moved(back1, -1), scalars=(place,)
    )
    part = exchanged(part.reshape(zh * xs, own, half), ("zh", "x")).reshape(zh, xs, own, half)
    depth = lax.axis_index("zh").reshape(1).astype(jnp.int32)
    peers = lax.axis_size("y") * cores
    part = on_core(pick_kernel, shaped((peers, own, half), F32), part, scalars=(depth,))

    arrived = [
        lax.ppermute(parcel, "x", [(i, (i + step) % HEADS) for i in range(HEADS)]) if step else parcel
        for step, parcel in enumerate(parcels)
    ]
    part = exchanged(part, ("y", "core")).reshape(-1, cores, own, half)
    grad_rows = on_core(last_kernel, shaped((own, cores * half), F32), part)

    layer_out, grad_history = on_core(
        join_kernel,
        (shaped(candidates.shape, BF16), shaped(history.shape, BF16)),
        candidates,
        out_weight,
        *arrived,
        scalars=(place,),
    )
    return (layer_out, grad_rows, grad_history)


def solution(mesh):
    inner = Mesh(mesh.devices.reshape(4, 2, 4, 4, 4), ALL)
    rows = P(ALL)
    return jax.shard_map(
        on_device,
        mesh=inner,
        in_specs=(rows, rows, rows, rows, rows, rows, P(), P()),
        out_specs=(rows, P(("zh", "zl", "x")), rows),
        check_vma=False,
    )
```

```python
import math

import jax
import jax.numpy as jnp
from jax import lax
from jax.experimental import pallas as pl
from jax.experimental.pallas import tpu as pltpu
from jax.sharding import Mesh, PartitionSpec as P

HEADS = 4
SPAN = 8
BF16 = jnp.bfloat16
F32 = jnp.float32
ALL = ("y", "core", "zh", "zl", "x")
DEPTH = ("zh", "zl")
NT = (((1,), (1,)), ((), ()))
TN = (((0,), (0,)), ((), ()))


def on_core(kernel, outs, *operands, scalars=()):
    spaces = [pltpu.SMEM] * len(scalars) + [pltpu.VMEM] * len(operands)
    return pl.pallas_call(
        kernel,
        out_shape=outs,
        in_specs=[pl.BlockSpec(memory_space=space) for space in spaces],
        out_specs=jax.tree.map(lambda _: pl.BlockSpec(memory_space=pltpu.VMEM), outs),
        compiler_params=pltpu.CompilerParams(vmem_limit_bytes=12 * 1024 * 1024),
    )(*scalars, *operands)


def on_fetched(kernel, outs, *operands, scalars=()):
    fetched = list(scalars) + list(operands)
    many = len(fetched)
    first = many + len(jax.tree.leaves(outs))
    pieces = [4 if one.size >= 1 << 19 else 1 for one in fetched]

    def body(*refs):
        places, arrivals = refs[first : first + many], refs[first + many]
        waits = []
        for i, (source, place) in enumerate(zip(refs[:many], places)):
            step = place.shape[0] // pieces[i]
            copies = []
            for part in range(pieces[i]):
                rows = (slice(None),) if pieces[i] == 1 else (pl.ds(part * step, step),)
                copy = pltpu.make_async_copy(source.at[rows], place.at[rows], arrivals.at[i, part])
                copy.start()
                copies.append(copy)
            waits.append(lambda copies=copies: [copy.wait() for copy in copies])
        kernel(*zip(places, waits), *refs[many:first])

    return pl.pallas_call(
        body,
        out_shape=outs,
        in_specs=[pl.BlockSpec(memory_space=pl.ANY)] * many,
        out_specs=jax.tree.map(lambda _: pl.BlockSpec(memory_space=pltpu.VMEM), outs),
        scratch_shapes=[pltpu.SMEM(one.shape, one.dtype) for one in scalars]
        + [pltpu.VMEM(one.shape, one.dtype) for one in operands]
        + [pltpu.SemaphoreType.DMA((many, 4))],
        compiler_params=pltpu.CompilerParams(vmem_limit_bytes=56 * 1024 * 1024),
    )(*fetched)


def shaped(shape, kind):
    return jax.ShapeDtypeStruct(shape, kind)


def sigmoid(values):
    return 0.5 + 0.5 * jnp.tanh(0.5 * values)


def served(ring, group):
    return {0: range(group, HEADS), 1: range(0, HEADS), 2: range(0, group)}[ring]


def split_kernel(history_ref, chunks_ref, arrivals):
    heads, _, both = chunks_ref.shape
    size = both // 2
    copies = []
    for head in range(heads):
        for kind in range(2):
            columns = pl.ds((kind * heads + head) * size, size)
            copies.append(
                pltpu.make_async_copy(
                    history_ref.at[:, columns],
                    chunks_ref.at[head, :, pl.ds(kind * size, size)],
                    arrivals.at[head, kind],
                )
            )
    for copy in copies:
        copy.start()
    for copy in copies:
        copy.wait()


def used_blocks(blocks_ref, length_ref, owner_ref):
    requests, width = blocks_ref.shape
    owners = owner_ref[...]
    positions = lax.broadcasted_iota(jnp.int32, (16, owners.shape[1]), 0)
    usage = jnp.zeros(positions.shape, F32)
    for request in range(requests):
        used = jnp.zeros(positions.shape, F32)
        for entry in range(width):
            block = jnp.where(entry < length_ref[request], blocks_ref[request, entry], -1)
            used = used + jnp.where(positions == block, 1.0, 0.0)
        usage = usage + jnp.where(owners == request, used, 0.0)
    return usage


def prepare_kernel(blocks, lengths, owners, cands, cots, in_weight, out_weight, bundle_ref):
    (cand_ref, cand_here), (cot_ref, cot_here) = cands, cots
    (in_ref, in_here), (out_ref, out_here) = in_weight, out_weight
    inner, count = out_ref.shape[0], cand_ref.shape[0]
    size = inner // HEADS
    bundle_ref[:, :, count:] = jnp.zeros(
        (HEADS, bundle_ref.shape[1], bundle_ref.shape[2] - count), BF16
    )
    for _, here in (blocks, lengths, owners):
        here()
    usage = used_blocks(blocks[0], lengths[0], owners[0]).astype(BF16)
    cand_here()
    rows = cand_ref[...].astype(F32)
    centered = rows - jnp.mean(rows, axis=-1, keepdims=True)
    inv_scale = lax.rsqrt(jnp.mean(centered * centered, axis=-1, keepdims=True) + 1e-05)
    normed = (centered * inv_scale).astype(BF16)
    cot_here()
    out_here()
    zed_grad = lax.dot_general(out_ref[...], cot_ref[...], NT, preferred_element_type=F32)
    in_here()
    projected = jnp.dot(normed, in_ref[...], preferred_element_type=F32).T
    for head in range(HEADS):
        part = slice(head * size, (head + 1) * size)
        gate_in = projected[inner + head * size : inner + (head + 1) * size]
        gating = gate_in * sigmoid(gate_in)
        bundle_ref[head, 0:size, :count] = projected[part].astype(BF16)
        bundle_ref[head, size : 2 * size, :count] = gating.astype(BF16)
        bundle_ref[head, 2 * size : 3 * size, :count] = (zed_grad[part] * gating).astype(BF16)
        bundle_ref[head, 3 * size :, :count] = usage


def scored(ring, blocks_ref, bundle_ref, group):
    span = served(ring, group)
    tall, size = blocks_ref.shape[1], blocks_ref.shape[2] // 2
    rows = blocks_ref[span[0] : span[-1] + 1].reshape(len(span) * tall, 2 * size)
    scores = jnp.dot(rows[:, :size], bundle_ref[group, 0:size], preferred_element_type=F32)
    scores = scores * (1.0 / math.sqrt(size))
    usage = bundle_ref[group, 3 * size :].astype(F32)
    parts = []
    for place, block in enumerate(span):
        position = HEADS * ring + block - group
        parts.append((scores[place * tall : (place + 1) * tall], usage[position : position + 1]))
    return rows[:, size:], parts


def attend(ring, blocks_ref, bundle_ref, group):
    values, parts = scored(ring, blocks_ref, bundle_ref, group)
    weights = [(scores * sigmoid(scores) * usage).astype(BF16) for scores, usage in parts]
    return lax.dot_general(
        values, jnp.concatenate(weights, axis=0), TN, preferred_element_type=F32
    )


def early_kernel(ring0, ring1, bundle, attended_ref):
    for group in range(HEADS):
        attended_ref[group] = attend(0, ring0, bundle, group) + attend(1, ring1, bundle, group)


def late_kernel(ring2, bundle, before, attended_ref, stats_ref):
    size = before.shape[1]
    for group in range(HEADS):
        attended = before[group]
        if len(served(2, group)) > 0:
            attended = attended + attend(2, ring2, bundle, group)
        attended_ref[group] = attended
        dy = bundle[group, 2 * size : 3 * size].astype(F32)
        mean = jnp.mean(attended, axis=0, keepdims=True)
        centered = attended - mean
        stats_ref[4 * group : 4 * group + 1] = mean
        stats_ref[4 * group + 1 : 4 * group + 2] = jnp.sum(centered * centered, axis=0, keepdims=True)
        stats_ref[4 * group + 2 : 4 * group + 3] = jnp.sum(dy, axis=0, keepdims=True)
        stats_ref[4 * group + 3 : 4 * group + 4] = jnp.sum(dy * centered, axis=0, keepdims=True)


def norm_kernel(attended, bundle, stats, gated_ref, grad_ref):
    size = attended.shape[1]
    width = HEADS * size
    for group in range(HEADS):
        head_stats = [stats[head, 4 * group : 4 * group + 4] for head in range(HEADS)]
        mean = sum(one[0:1] for one in head_stats) * (1.0 / HEADS)
        apart = [one[0:1] - mean for one in head_stats]
        spread = sum(one[1:2] + size * off * off for one, off in zip(head_stats, apart))
        inv_scale = lax.rsqrt(spread * (1.0 / width) + 1e-05)
        mean_dy = sum(one[2:3] for one in head_stats) * (1.0 / width)
        mixed = sum(one[3:4] + off * one[2:3] for one, off in zip(head_stats, apart))
        mean_mixed = mixed * inv_scale * (1.0 / width)
        normed = (attended[group] - mean) * inv_scale
        dy = bundle[group, 2 * size : 3 * size].astype(F32)
        gated_ref[group] = (normed * bundle[group, size : 2 * size].astype(F32)).astype(BF16)
        grad_ref[group] = (inv_scale * (dy - mean_dy - normed * mean_mixed)).astype(BF16)


def out_grad_kernel(total_cands, low, high, gated, out_grad_ref):
    count = low.shape[1]
    _, rows_of, lines, _ = out_grad_ref.shape
    for half, cots in enumerate((low, high)):
        total = None
        for group in range(HEADS):
            part = jnp.dot(gated[group, :, :count], cots[group], preferred_element_type=F32)
            total = part if total is None else total + part
        total = (total * (1.0 / math.sqrt(total_cands))).astype(BF16)
        for row in range(rows_of):
            out_grad_ref[half, row] = total[row * lines : (row + 1) * lines]


def back(ring, blocks_ref, bundle, grads, sum_ref):
    tall, size = blocks_ref.shape[1], blocks_ref.shape[2] // 2
    scale = 1.0 / math.sqrt(size)
    keys, values = {}, {}
    for group in range(HEADS):
        span = served(ring, group)
        if len(span) == 0:
            continue
        grad = grads[group]
        value_rows, parts = scored(ring, blocks_ref, bundle, group)
        weight_grad = jnp.dot(value_rows, grad, preferred_element_type=F32)
        for place, block in enumerate(span):
            scores, usage = parts[place]
            part = sigmoid(scores)
            weights = scores * part
            slopes = (part + weights * (1.0 - part)) * (usage * scale)
            lines = weight_grad[place * tall : (place + 1) * tall]
            key = lax.dot_general(
                (lines * slopes).astype(BF16), bundle[group, 0:size], NT, preferred_element_type=F32
            )
            value = lax.dot_general(
                (weights * usage).astype(BF16), grad, NT, preferred_element_type=F32
            )
            keys[block] = keys[block] + key if block in keys else key
            values[block] = values[block] + value if block in values else value
    for block in keys:
        sum_ref[block, :, 0:size] = keys[block].astype(sum_ref.dtype)
        sum_ref[block, :, size:] = values[block].astype(sum_ref.dtype)


def back2_kernel(ring2, bundle, grads, sum_ref):
    back(2, ring2, bundle, grads, sum_ref)


def back1_kernel(ring1, bundle, grads, sum_ref):
    back(1, ring1, bundle, grads, sum_ref)


def add_kernel(own, arrived, sum_ref):
    count = arrived.shape[0]
    sum_ref[:count] = (own[:count] + arrived[...].astype(F32)).astype(BF16)
    sum_ref[count:] = own[count:].astype(BF16)


def back0_kernel(ring0, bundle, grads, sum_ref):
    back(0, ring0, bundle, grads, sum_ref)


def fold_kernel(parts, folded_ref):
    total = jnp.sum(parts[...].astype(F32), axis=0).astype(BF16)
    lines = folded_ref.shape[2]
    for row in range(folded_ref.shape[1]):
        for copy in range(folded_ref.shape[0]):
            folded_ref[copy, row] = total[row * lines : (row + 1) * lines]


def pick_kernel(place_ref, parts, spread_ref):
    total = jnp.zeros(spread_ref.shape[1:], F32)
    for source in range(parts.shape[0]):
        total = total + parts[source, place_ref[0]].astype(F32)
    for peer in range(spread_ref.shape[0]):
        spread_ref[peer] = total


def last_kernel(parts, rows_ref):
    cores = parts.shape[1]
    half = rows_ref.shape[1] // cores
    for core in range(cores):
        rows_ref[:, core * half : (core + 1) * half] = jnp.sum(parts[:, core], axis=0)


def parcel_kernel(place_ref, gated_ref, back0, back1, *parcel_refs):
    size = gated_ref.shape[1]
    for step, parcel in enumerate(parcel_refs):
        target = lax.rem(place_ref[0] + step, HEADS)
        parcel[0:size] = gated_ref[target]
        parcel[size:] = (back0[target] + back1[target].astype(F32)).astype(BF16)


def join_kernel(place_ref, cand_ref, out_ref, *refs):
    *parcels, result_ref, grad_ref = refs
    inner, count = out_ref.shape[0], cand_ref.shape[0]
    size = inner // HEADS
    product = None
    for step, parcel in enumerate(parcels):
        head = lax.rem(place_ref[0] + HEADS - step, HEADS)
        rows = pl.ds(pl.multiple_of(head * size, size), size)
        part = lax.dot_general(parcel[0:size, :count], out_ref[rows], TN, preferred_element_type=F32)
        product = part if product is None else product + part
        grad_ref[:, rows] = parcel[size:, 0:size]
        grad_ref[:, pl.ds(pl.multiple_of(inner + head * size, size), size)] = parcel[size:, size:]
    result_ref[...] = (cand_ref[...].astype(F32) + product).astype(BF16)


def moved(block, distance):
    size = lax.axis_size(DEPTH)
    return lax.ppermute(block, DEPTH, [((i + distance) % size, i) for i in range(size)])


def exchanged(chunks, axis):
    return lax.all_to_all(chunks, axis, 0, 0, tiled=True)


def spread_over(block, axis):
    size = lax.axis_size(axis)
    return exchanged(jnp.broadcast_to(block[None], (size,) + block.shape), axis)


def summed(parts):
    return jnp.sum(parts.astype(F32), axis=0)


def on_device(
    candidates,
    cotangent,
    history,
    request_blocks,
    request_length,
    candidate_request,
    in_weight,
    out_weight,
):
    tall = history.shape[0]
    inner = history.shape[1] // 2
    size = inner // HEADS
    count = candidates.shape[0]
    lanes = 2 * size
    total_cands = count * lax.axis_size(ALL)
    barrier = lax.optimization_barrier
    place = lax.axis_index("x").reshape(1).astype(jnp.int32)

    ring_shape = shaped((HEADS, tall, 2 * size), BF16)
    by_head = pl.pallas_call(
        split_kernel,
        out_shape=ring_shape,
        in_specs=[pl.BlockSpec(memory_space=pl.ANY)],
        out_specs=pl.BlockSpec(memory_space=pltpu.VMEM),
        scratch_shapes=[pltpu.SemaphoreType.DMA((HEADS, 2))],
        compiler_params=pltpu.CompilerParams(vmem_limit_bytes=56 * 1024 * 1024),
    )(history)
    ring0 = exchanged(by_head, "x")

    ring2 = moved(ring0[: HEADS - 1], 2)
    ring1 = moved(ring0, 1)
    bundle = on_fetched(
        prepare_kernel,
        shaped((HEADS, 3 * size + 16, lanes), BF16),
        candidate_request.reshape(1, count),
        candidates,
        cotangent,
        in_weight,
        out_weight,
        scalars=(request_blocks, request_length),
    )
    bundle = exchanged(bundle, "x")
    cores = lax.axis_size("core")
    half = out_weight.shape[1] // cores
    wide = (lax.axis_size("x"), count, half)
    bundle, low, high = barrier(
        (bundle,) + tuple(jnp.broadcast_to(cotangent[None, :, i * half : (i + 1) * half], wide) for i in range(2))
    )
    low = exchanged(low, "x")

    attended_shape = shaped((HEADS, size, lanes), F32)
    before = on_core(early_kernel, attended_shape, ring0, ring1, bundle)
    attended, stats = on_core(
        late_kernel, (attended_shape, shaped((4 * HEADS, lanes), F32)), ring2, bundle, before
    )
    stats, high = barrier((spread_over(stats, "x"), high))
    high = exchanged(high, "x")
    head_shape = shaped((HEADS, size, lanes), BF16)
    zh, zl, xs = (lax.axis_size(name) for name in ("zh", "zl", "x"))
    own = size // (zl * xs)
    gated, grads = on_core(norm_kernel, (head_shape, head_shape), attended, bundle, stats)
    back2 = moved(on_core(back2_kernel, shaped(ring2.shape, BF16), ring2, bundle, grads), -1)
    back1 = on_core(back1_kernel, shaped(ring1.shape, F32), ring1, bundle, grads)
    back1 = on_core(add_kernel, shaped(ring1.shape, BF16), back1, back2)
    high, back1 = barrier((high, back1))
    out_grad = on_core(
        lambda *refs: out_grad_kernel(total_cands, *refs),
        shaped((cores, zl, size // zl, half), BF16),
        low,
        high,
        gated,
    )
    out_grad, late_grads = barrier((out_grad, grads))
    part = exchanged(out_grad.reshape(cores * zl, size // zl, half), ("core", "zl"))
    back0 = on_core(back0_kernel, shaped(ring0.shape, F32), ring0, bundle, late_grads)
    parcels = on_core(
        parcel_kernel, [shaped((2 * size, lanes), BF16)] * HEADS, gated, back0, moved(back1, -1), scalars=(place,)
    )
    part, *parcels = barrier((part, *parcels))
    part, *parcels = barrier((on_core(fold_kernel, shaped((zh, xs, own, half), BF16), part), *parcels))
    part = exchanged(part.reshape(zh * xs, own, half), ("zh", "x")).reshape(zh, xs, own, half)
    depth = lax.axis_index("zh").reshape(1).astype(jnp.int32)
    peers = lax.axis_size("y") * cores
    part = on_core(pick_kernel, shaped((peers, own, half), F32), part, scalars=(depth,))

    arrived = [
        lax.ppermute(parcel, "x", [(i, (i + step) % HEADS) for i in range(HEADS)]) if step else parcel
        for step, parcel in enumerate(parcels)
    ]
    part = exchanged(part, ("y", "core")).reshape(-1, cores, own, half)
    grad_rows = on_core(last_kernel, shaped((own, cores * half), F32), part)

    layer_out, grad_history = on_core(
        join_kernel,
        (shaped(candidates.shape, BF16), shaped(history.shape, BF16)),
        candidates,
        out_weight,
        *arrived,
        scalars=(place,),
    )
    return (layer_out, grad_rows, grad_history)


def solution(mesh):
    inner = Mesh(mesh.devices.reshape(4, 2, 4, 4, 4), ALL)
    rows = P(ALL)
    return jax.shard_map(
        on_device,
        mesh=inner,
        in_specs=(rows, rows, rows, rows, rows, rows, P(), P()),
        out_specs=(rows, P(("zh", "zl", "x")), rows),
        check_vma=False,
    )
```

```python
import math

import jax
import jax.numpy as jnp
from jax import lax
from jax.experimental import pallas as pl
from jax.experimental.pallas import tpu as pltpu
from jax.sharding import Mesh, PartitionSpec as P

HEADS = 4
SPAN = 8
BF16 = jnp.bfloat16
F32 = jnp.float32
ALL = ("y", "core", "zh", "zl", "x")
DEPTH = ("zh", "zl")
NT = (((1,), (1,)), ((), ()))
TN = (((0,), (0,)), ((), ()))


def on_core(kernel, outs, *operands, scalars=()):
    spaces = [pltpu.SMEM] * len(scalars) + [pltpu.VMEM] * len(operands)
    return pl.pallas_call(
        kernel,
        out_shape=outs,
        in_specs=[pl.BlockSpec(memory_space=space) for space in spaces],
        out_specs=jax.tree.map(lambda _: pl.BlockSpec(memory_space=pltpu.VMEM), outs),
        compiler_params=pltpu.CompilerParams(vmem_limit_bytes=12 * 1024 * 1024),
    )(*scalars, *operands)


def on_fetched(kernel, outs, *operands, scalars=()):
    fetched = list(scalars) + list(operands)
    many = len(fetched)
    first = many + len(jax.tree.leaves(outs))
    pieces = [4 if one.size >= 1 << 19 else 1 for one in fetched]

    def body(*refs):
        places, arrivals = refs[first : first + many], refs[first + many]
        waits = []
        for i, (source, place) in enumerate(zip(refs[:many], places)):
            step = place.shape[0] // pieces[i]
            copies = []
            for part in range(pieces[i]):
                rows = (slice(None),) if pieces[i] == 1 else (pl.ds(part * step, step),)
                copy = pltpu.make_async_copy(source.at[rows], place.at[rows], arrivals.at[i, part])
                copy.start()
                copies.append(copy)
            waits.append(lambda copies=copies: [copy.wait() for copy in copies])
        kernel(*zip(places, waits), *refs[many:first])

    return pl.pallas_call(
        body,
        out_shape=outs,
        in_specs=[pl.BlockSpec(memory_space=pl.ANY)] * many,
        out_specs=jax.tree.map(lambda _: pl.BlockSpec(memory_space=pltpu.VMEM), outs),
        scratch_shapes=[pltpu.SMEM(one.shape, one.dtype) for one in scalars]
        + [pltpu.VMEM(one.shape, one.dtype) for one in operands]
        + [pltpu.SemaphoreType.DMA((many, 4))],
        compiler_params=pltpu.CompilerParams(vmem_limit_bytes=56 * 1024 * 1024),
    )(*fetched)


def shaped(shape, kind):
    return jax.ShapeDtypeStruct(shape, kind)


def sigmoid(values):
    return 0.5 + 0.5 * jnp.tanh(0.5 * values)


def served(ring, group):
    return {0: range(group, HEADS), 1: range(0, HEADS), 2: range(0, group)}[ring]


def split_kernel(history_ref, chunks_ref, arrivals):
    heads, _, both = chunks_ref.shape
    size = both // 2
    copies = []
    for head in range(heads):
        for kind in range(2):
            columns = pl.ds((kind * heads + head) * size, size)
            copies.append(
                pltpu.make_async_copy(
                    history_ref.at[:, columns],
                    chunks_ref.at[head, :, pl.ds(kind * size, size)],
                    arrivals.at[head, kind],
                )
            )
    for copy in copies:
        copy.start()
    for copy in copies:
        copy.wait()


def used_blocks(blocks_ref, length_ref, owner_ref):
    requests, width = blocks_ref.shape
    owners = owner_ref[...]
    positions = lax.broadcasted_iota(jnp.int32, (16, owners.shape[1]), 0)
    usage = jnp.zeros(positions.shape, F32)
    for request in range(requests):
        used = jnp.zeros(positions.shape, F32)
        for entry in range(width):
            block = jnp.where(entry < length_ref[request], blocks_ref[request, entry], -1)
            used = used + jnp.where(positions == block, 1.0, 0.0)
        usage = usage + jnp.where(owners == request, used, 0.0)
    return usage


def prepare_kernel(blocks, lengths, owners, cands, cots, in_weight, out_weight, bundle_ref):
    (cand_ref, cand_here), (cot_ref, cot_here) = cands, cots
    (in_ref, in_here), (out_ref, out_here) = in_weight, out_weight
    inner, count = out_ref.shape[0], cand_ref.shape[0]
    size = inner // HEADS
    bundle_ref[:, :, count:] = jnp.zeros(
        (HEADS, bundle_ref.shape[1], bundle_ref.shape[2] - count), BF16
    )
    for _, here in (blocks, lengths, owners):
        here()
    usage = used_blocks(blocks[0], lengths[0], owners[0]).astype(BF16)
    cand_here()
    rows = cand_ref[...].astype(F32)
    centered = rows - jnp.mean(rows, axis=-1, keepdims=True)
    inv_scale = lax.rsqrt(jnp.mean(centered * centered, axis=-1, keepdims=True) + 1e-05)
    normed = (centered * inv_scale).astype(BF16)
    cot_here()
    out_here()
    zed_grad = lax.dot_general(out_ref[...], cot_ref[...], NT, preferred_element_type=F32)
    in_here()
    projected = jnp.dot(normed, in_ref[...], preferred_element_type=F32).T
    for head in range(HEADS):
        part = slice(head * size, (head + 1) * size)
        gate_in = projected[inner + head * size : inner + (head + 1) * size]
        gating = gate_in * sigmoid(gate_in)
        bundle_ref[head, 0:size, :count] = projected[part].astype(BF16)
        bundle_ref[head, size : 2 * size, :count] = gating.astype(BF16)
        bundle_ref[head, 2 * size : 3 * size, :count] = (zed_grad[part] * gating).astype(BF16)
        bundle_ref[head, 3 * size :, :count] = usage


def scored(ring, blocks_ref, bundle_ref, group):
    span = served(ring, group)
    tall, size = blocks_ref.shape[1], blocks_ref.shape[2] // 2
    rows = blocks_ref[span[0] : span[-1] + 1].reshape(len(span) * tall, 2 * size)
    scores = jnp.dot(rows[:, :size], bundle_ref[group, 0:size], preferred_element_type=F32)
    scores = scores * (1.0 / math.sqrt(size))
    usage = bundle_ref[group, 3 * size :].astype(F32)
    parts = []
    for place, block in enumerate(span):
        position = HEADS * ring + block - group
        parts.append((scores[place * tall : (place + 1) * tall], usage[position : position + 1]))
    return rows[:, size:], parts


def attend(ring, blocks_ref, bundle_ref, group):
    values, parts = scored(ring, blocks_ref, bundle_ref, group)
    weights = [(scores * sigmoid(scores) * usage).astype(BF16) for scores, usage in parts]
    return lax.dot_general(
        values, jnp.concatenate(weights, axis=0), TN, preferred_element_type=F32
    )


def early_kernel(ring0, ring1, bundle, attended_ref):
    for group in range(HEADS):
        attended_ref[group] = attend(0, ring0, bundle, group) + attend(1, ring1, bundle, group)


def late_kernel(ring2, bundle, before, attended_ref, stats_ref):
    size = before.shape[1]
    for group in range(HEADS):
        attended = before[group]
        if len(served(2, group)) > 0:
            attended = attended + attend(2, ring2, bundle, group)
        attended_ref[group] = attended
        dy = bundle[group, 2 * size : 3 * size].astype(F32)
        mean = jnp.mean(attended, axis=0, keepdims=True)
        centered = attended - mean
        stats_ref[4 * group : 4 * group + 1] = mean
        stats_ref[4 * group + 1 : 4 * group + 2] = jnp.sum(centered * centered, axis=0, keepdims=True)
        stats_ref[4 * group + 2 : 4 * group + 3] = jnp.sum(dy, axis=0, keepdims=True)
        stats_ref[4 * group + 3 : 4 * group + 4] = jnp.sum(dy * centered, axis=0, keepdims=True)


def norm_kernel(attended, bundle, stats, gated_ref, grad_ref):
    size = attended.shape[1]
    width = HEADS * size
    for group in range(HEADS):
        head_stats = [stats[head, 4 * group : 4 * group + 4] for head in range(HEADS)]
        mean = sum(one[0:1] for one in head_stats) * (1.0 / HEADS)
        apart = [one[0:1] - mean for one in head_stats]
        spread = sum(one[1:2] + size * off * off for one, off in zip(head_stats, apart))
        inv_scale = lax.rsqrt(spread * (1.0 / width) + 1e-05)
        mean_dy = sum(one[2:3] for one in head_stats) * (1.0 / width)
        mixed = sum(one[3:4] + off * one[2:3] for one, off in zip(head_stats, apart))
        mean_mixed = mixed * inv_scale * (1.0 / width)
        normed = (attended[group] - mean) * inv_scale
        dy = bundle[group, 2 * size : 3 * size].astype(F32)
        gated_ref[group] = (normed * bundle[group, size : 2 * size].astype(F32)).astype(BF16)
        grad_ref[group] = (inv_scale * (dy - mean_dy - normed * mean_mixed)).astype(BF16)


def out_grad_kernel(total_cands, place_ref, gated, *refs):
    *cots, out_grad_ref = refs
    count = cots[0].shape[0]
    total = None
    for step, rows in enumerate(cots):
        group = lax.rem(place_ref[0] + HEADS - step, HEADS)
        part = jnp.dot(gated[group, :, :count], rows[...], preferred_element_type=F32)
        total = part if total is None else total + part
    total = (total * (1.0 / math.sqrt(total_cands))).astype(BF16)
    halves, rows_of, lines, columns = out_grad_ref.shape
    for half in range(halves):
        for row in range(rows_of):
            out_grad_ref[half, row] = total[
                row * lines : (row + 1) * lines, half * columns : (half + 1) * columns
            ]


def back(ring, blocks_ref, bundle, grads, sum_ref):
    tall, size = blocks_ref.shape[1], blocks_ref.shape[2] // 2
    scale = 1.0 / math.sqrt(size)
    keys, values = {}, {}
    for group in range(HEADS):
        span = served(ring, group)
        if len(span) == 0:
            continue
        grad = grads[group]
        value_rows, parts = scored(ring, blocks_ref, bundle, group)
        weight_grad = jnp.dot(value_rows, grad, preferred_element_type=F32)
        for place, block in enumerate(span):
            scores, usage = parts[place]
            part = sigmoid(scores)
            weights = scores * part
            slopes = (part + weights * (1.0 - part)) * (usage * scale)
            lines = weight_grad[place * tall : (place + 1) * tall]
            key = lax.dot_general(
                (lines * slopes).astype(BF16), bundle[group, 0:size], NT, preferred_element_type=F32
            )
            value = lax.dot_general(
                (weights * usage).astype(BF16), grad, NT, preferred_element_type=F32
            )
            keys[block] = keys[block] + key if block in keys else key
            values[block] = values[block] + value if block in values else value
    for block in keys:
        sum_ref[block, :, 0:size] = keys[block].astype(sum_ref.dtype)
        sum_ref[block, :, size:] = values[block].astype(sum_ref.dtype)


def back2_kernel(ring2, bundle, grads, sum_ref):
    back(2, ring2, bundle, grads, sum_ref)


def back1_kernel(ring1, bundle, grads, sum_ref):
    back(1, ring1, bundle, grads, sum_ref)


def add_kernel(own, arrived, sum_ref):
    count = arrived.shape[0]
    sum_ref[:count] = (own[:count] + arrived[...].astype(F32)).astype(BF16)
    sum_ref[count:] = own[count:].astype(BF16)


def back0_kernel(ring0, bundle, grads, sum_ref):
    back(0, ring0, bundle, grads, sum_ref)


def fold_kernel(parts, folded_ref):
    total = jnp.sum(parts[...].astype(F32), axis=0).astype(BF16)
    lines = folded_ref.shape[2]
    for row in range(folded_ref.shape[1]):
        for copy in range(folded_ref.shape[0]):
            folded_ref[copy, row] = total[row * lines : (row + 1) * lines]


def pick_kernel(place_ref, parts, spread_ref):
    total = jnp.zeros(spread_ref.shape[1:], F32)
    for source in range(parts.shape[0]):
        total = total + parts[source, place_ref[0]].astype(F32)
    for peer in range(spread_ref.shape[0]):
        spread_ref[peer] = total


def last_kernel(parts, rows_ref):
    cores = parts.shape[1]
    half = rows_ref.shape[1] // cores
    for core in range(cores):
        rows_ref[:, core * half : (core + 1) * half] = jnp.sum(parts[:, core], axis=0)


def parcel_kernel(place_ref, gated_ref, back0, back1, *parcel_refs):
    size = gated_ref.shape[1]
    for step, parcel in enumerate(parcel_refs):
        target = lax.rem(place_ref[0] + step, HEADS)
        parcel[0:size] = gated_ref[target]
        parcel[size:] = (back0[target] + back1[target].astype(F32)).astype(BF16)


def join_kernel(place_ref, cand_ref, out_ref, *refs):
    *parcels, result_ref, grad_ref = refs
    inner, count = out_ref.shape[0], cand_ref.shape[0]
    size = inner // HEADS
    product = None
    for step, parcel in enumerate(parcels):
        head = lax.rem(place_ref[0] + HEADS - step, HEADS)
        rows = pl.ds(pl.multiple_of(head * size, size), size)
        part = lax.dot_general(parcel[0:size, :count], out_ref[rows], TN, preferred_element_type=F32)
        product = part if product is None else product + part
        grad_ref[:, rows] = parcel[size:, 0:size]
        grad_ref[:, pl.ds(pl.multiple_of(inner + head * size, size), size)] = parcel[size:, size:]
    result_ref[...] = (cand_ref[...].astype(F32) + product).astype(BF16)


def moved(block, distance):
    size = lax.axis_size(DEPTH)
    return lax.ppermute(block, DEPTH, [((i + distance) % size, i) for i in range(size)])


def exchanged(chunks, axis):
    return lax.all_to_all(chunks, axis, 0, 0, tiled=True)


def spread_over(block, axis):
    size = lax.axis_size(axis)
    return exchanged(jnp.broadcast_to(block[None], (size,) + block.shape), axis)


def summed(parts):
    return jnp.sum(parts.astype(F32), axis=0)


def on_device(
    candidates,
    cotangent,
    history,
    request_blocks,
    request_length,
    candidate_request,
    in_weight,
    out_weight,
):
    tall, wide = history.shape
    inner = wide // 2
    size = inner // HEADS
    count = candidates.shape[0]
    lanes = 2 * size
    total_cands = count * lax.axis_size(ALL)
    barrier = lax.optimization_barrier
    place = lax.axis_index("x").reshape(1).astype(jnp.int32)

    cots = [cotangent] + [
        lax.ppermute(cotangent, "x", [(i, (i + step) % HEADS) for i in range(HEADS)]) for step in range(1, HEADS)
    ]
    ring_shape = shaped((HEADS, tall, 2 * size), BF16)
    by_head = pl.pallas_call(
        split_kernel,
        out_shape=ring_shape,
        in_specs=[pl.BlockSpec(memory_space=pl.ANY)],
        out_specs=pl.BlockSpec(memory_space=pltpu.VMEM),
        scratch_shapes=[pltpu.SemaphoreType.DMA((HEADS, 2))],
        compiler_params=pltpu.CompilerParams(vmem_limit_bytes=56 * 1024 * 1024),
    )(history)
    ring0 = exchanged(by_head, "x")

    ring2 = moved(ring0[: HEADS - 1], 2)
    ring1 = moved(ring0, 1)
    bundle = on_fetched(
        prepare_kernel,
        shaped((HEADS, 3 * size + 16, lanes), BF16),
        candidate_request.reshape(1, count),
        candidates,
        cotangent,
        in_weight,
        out_weight,
        scalars=(request_blocks, request_length),
    )
    bundle = exchanged(bundle, "x")

    attended_shape = shaped((HEADS, size, lanes), F32)
    before = on_core(early_kernel, attended_shape, ring0, ring1, bundle)
    attended, stats = on_core(
        late_kernel, (attended_shape, shaped((4 * HEADS, lanes), F32)), ring2, bundle, before
    )
    stats = spread_over(stats, "x")
    head_shape = shaped((HEADS, size, lanes), BF16)
    cores, zh, zl, xs = (lax.axis_size(name) for name in ("core", "zh", "zl", "x"))
    own, half = size // (zl * xs), out_weight.shape[1] // cores
    gated, grads = on_core(norm_kernel, (head_shape, head_shape), attended, bundle, stats)
    back2 = on_core(back2_kernel, shaped(ring2.shape, BF16), ring2, bundle, grads)
    gated, back2 = barrier((gated, back2))
    back2 = moved(back2, -1)
    out_grad = on_core(
        lambda *refs: out_grad_kernel(total_cands, *refs),
        shaped((cores, zl, size // zl, half), BF16),
        gated,
        *cots,
        scalars=(place,),
    )
    out_grad, late_grads = barrier((out_grad, grads))
    back1 = on_core(back1_kernel, shaped(ring1.shape, F32), ring1, bundle, late_grads)
    out_grad, back2, back1, late_grads = barrier((out_grad, back2, back1, late_grads))
    part = exchanged(out_grad.reshape(cores * zl, size // zl, half), ("core", "zl"))
    back1 = on_core(add_kernel, shaped(ring1.shape, BF16), back1, back2)
    back0 = on_core(back0_kernel, shaped(ring0.shape, F32), ring0, bundle, late_grads)
    parcels = on_core(
        parcel_kernel, [shaped((2 * size, lanes), BF16)] * HEADS, gated, back0, moved(back1, -1), scalars=(place,)
    )
    part, *parcels = barrier((part, *parcels))
    part, *parcels = barrier((on_core(fold_kernel, shaped((zh, xs, own, half), BF16), part), *parcels))
    part = exchanged(part.reshape(zh * xs, own, half), ("zh", "x")).reshape(zh, xs, own, half)
    depth = lax.axis_index("zh").reshape(1).astype(jnp.int32)
    peers = lax.axis_size("y") * cores
    part = on_core(pick_kernel, shaped((peers, own, half), F32), part, scalars=(depth,))

    arrived = [
        lax.ppermute(parcel, "x", [(i, (i + step) % HEADS) for i in range(HEADS)]) if step else parcel
        for step, parcel in enumerate(parcels)
    ]
    part = exchanged(part, ("y", "core")).reshape(-1, cores, own, half)
    grad_rows = on_core(last_kernel, shaped((own, cores * half), F32), part)

    layer_out, grad_history = on_core(
        join_kernel,
        (shaped(candidates.shape, BF16), shaped(history.shape, BF16)),
        candidates,
        out_weight,
        *arrived,
        scalars=(place,),
    )
    return (layer_out, grad_rows, grad_history)


def solution(mesh):
    inner = Mesh(mesh.devices.reshape(4, 2, 4, 4, 4), ALL)
    rows = P(ALL)
    return jax.shard_map(
        on_device,
        mesh=inner,
        in_specs=(rows, rows, rows, rows, rows, rows, P(), P()),
        out_specs=(rows, P(("zh", "zl", "x")), rows),
        check_vma=False,
    )
```
